512 devices in a mesh: band: 64 (over x, y, core), tp: 8 (over z).
Axes of the slice: x: 4, y: 8, z: 8, core: 2. Of those that a mesh axis runs over, the one named last changes fastest.
Arguments:
- control: float32 [69, 2, 512, 384], P(None, None, ('band', 'tp')), may hold values from -6 to 6
- spec_sigma: float32 [69, 512, 384], P(None, ('band', 'tp')), may hold values from 0.02 to 0.12
- prior_mean_field: float32 [69, 512, 1440], P(None, ('band', 'tp')), may hold values from -6 to 6
- magnitude_factor: float32 [69], replicated, may hold values from 0.25 to 1.75
- w_in: bfloat16 [69, 768], P(None, 'tp'), may hold values from -0.75 to 0.75
- w_out: bfloat16 [768, 69], P('tp'), may hold values from -0.21875 to 0.21875
- obs_band: int32 [64, 8, 1024, 1], P('band', 'tp'), may hold values from 0 to 63; in each aligned block of 1024 rows (0 to 1023, 1024 to 2047, ..., all dimensions but the last counted through in order) at most 64 rows name the same one
- obs_cell: int32 [64, 8, 1024], P('band', 'tp'), may hold values from 0 to 99359
- obs_value: float32 [64, 8, 1024], P('band', 'tp'), may hold values from -8 to 8
- obs_weight: float32 [64, 8, 1024], P('band', 'tp'), may hold values from 0.25 to 4
- obs_offset: float32 [64, 8, 1024], P('band', 'tp'), may hold values from 0 to 1
Outputs:
- grad_control: float32 [69, 2, 512, 384], P(None, None, ('band', 'tp'))
The draws below stay inside these ranges and needn't reach their ends.
Inputs may be any that keep to these rules, and one draw needn't show every extreme that they name: `obs_band`: among the observations of one device, at most 64 lie in any one band, and in every draw some device has exactly 64 in some band. The observed channel is obs_cell // 1440 and the stencil longitude obs_cell % 1440.
All inputs are finite; a program needn't handle non-finite values.
Results may differ from the reference program's by a relative error of at most 0.0016.
Values may be sent and summed in bfloat16 or wider, within the bound.
No kernel may reach another device: no remote copies, remote signals or barrier semaphores. Data moves between devices by JAX's collectives and lax.ppermute only.
A program may use at most 64 MiB of HBM per device.

```python
import math
import jax
import jax.numpy as jnp
import numpy as np
from jax import lax

C = 69
NLON = 1440
NN = 384
FF = 768
K_OWN = 1024
M = 512
NLAT = 512
CAP = 64
N_BAND = 64
N_TP = 8


def with_ends(values, key, low, largest):
    index_at = [jax.random.randint(jax.random.fold_in(key, axis), (), 0, length) for axis, length in enumerate(values.shape)]
    main_axis = values.shape.index(max(values.shape))
    beside = index_at[:main_axis] + [(index_at[main_axis] + 1) % values.shape[main_axis]] + index_at[main_axis + 1:]
    return values.at[tuple(index_at)].set(low).at[tuple(beside)].set(largest)


def shard_levels(rng, dims, split, smallest, largest):
    loudness = 1.0
    for axis_at, shards_of in split:
        steps = jax.random.uniform(jax.random.fold_in(jax.random.fold_in(rng, 6), axis_at), (shards_of,), jnp.float32, smallest / len(split), largest / len(split))
        loudness = loudness * jnp.repeat(jnp.exp(steps), dims[axis_at] // shards_of).reshape((-1,) + (1,) * (len(dims) - 1 - axis_at))
    return loudness


def assign_block(rng, own, number, rows, count, top, limit, slope):
    order = jax.random.permutation(rng, count)
    heavy_load, ordinary = shares(count, rows * top, limit, slope, True), shares(count, rows * top, limit, slope, False)
    places = jnp.arange(count)

    def named(lengths, turn):
        used = int((lengths > 0).sum())
        fixed = max(1, used // 4)
        moved = fixed + (places - fixed + turn * (used - fixed)) % max(1, count - fixed)
        return jnp.zeros((count,), jnp.int32).at[order[jnp.where(places < fixed, places, moved)]].set(jnp.asarray(lengths, jnp.int32))

    lengths = jnp.where(number % 4 == 0, named(heavy_load, number // 4), named(ordinary, number - number // 4 - 1))
    mixed = jax.random.permutation(jax.random.fold_in(own, 3), count)
    source_of, taker = mixed[0:count // 2 * 2:2], mixed[1:count // 2 * 2:2]
    margin = jnp.minimum(lengths[source_of] - 1, limit - lengths[taker]) // 2
    margin = jnp.where((source_of == order[0]) | (taker == order[0]) | (lengths[taker] == 0), 0, jnp.maximum(margin, 0))
    moved = jax.random.randint(jax.random.fold_in(own, 4), (count // 2,), 0, 1 << 20) % (margin + 1)
    lengths = lengths.at[source_of].add(-moved).at[taker].add(moved)
    items = jnp.searchsorted(jnp.cumsum(lengths), jnp.arange(rows * top), side="right").astype(jnp.int32)
    grid = items.reshape(top, rows).T
    grid = grid[jax.random.permutation(jax.random.fold_in(own, 1), rows)]
    turn = jax.random.randint(jax.random.fold_in(own, 2), (rows, 1), 0, top)
    return jnp.take_along_axis(grid, (jnp.arange(top)[None, :] + turn) % top, axis=1)


def shares(count, total, most, slope, full):
    portions = [(1 << 20) // math.isqrt(grade ** slope) + 1 for grade in range(1, count + 1)]
    largest = most if full else min(most, max(-(-total // count), total * portions[0] // sum(portions)))
    least = 1 if total - largest >= count - 1 else 0
    counts, surplus = [largest] + [least] * (count - 1), total - largest - least * (count - 1)
    while surplus > 0:
        candidates = [i for i in range(1, count) if counts[i] < largest] or [i for i in range(1, count) if counts[i] < most]
        whole, budget = sum([portions[i] for i in candidates]), surplus
        for i in candidates:
            addition = min(most - counts[i], max(1, budget * portions[i] // whole), surplus)
            counts[i] = counts[i] + addition
            surplus = surplus - addition
    return np.array(counts)


def centred(own_key, extent, deviation, reach, split=(), kind=jnp.bfloat16):
    gain = shard_levels(own_key, extent, split, -0.22, 0.18) if split else 1.0
    array = jax.random.normal(own_key, extent, jnp.float32) * deviation * gain
    return jnp.minimum(jnp.maximum(array, -reach), reach).astype(kind)


def setup_inputs(seed: int = 0) -> dict:
    splits = jax.random.split(jax.random.key(seed), 12)
    control = centred(splits[0], (C, 2, M, NN), 1.0, 6.0, ((2, 512),), jnp.float32)
    spec_sigma = jnp.clip(jnp.exp(math.log(0.12) - 1.7917595 * jax.random.uniform(splits[1], (C, M, NN), jnp.float32) ** shard_levels(splits[1], (C, M, NN), ((1, 512),), -0.2, 0.2)), 0.02, 0.12)
    prior_mean_field = centred(splits[2], (C, NLAT, NLON), 1.0, 6.0, ((1, 512),), jnp.float32)
    magnitude_factor = jnp.clip(1.0 + 0.15 * jax.random.normal(splits[3], (C,), jnp.float32), 0.25, 1.75)
    w_in = centred(splits[4], (C, FF), C ** -0.5, 0.75, ((1, 8),))
    w_out = centred(splits[5], (FF, C), FF ** -0.5, 0.21875, ((0, 8),))
    obs_band_keys = jax.random.split(jax.random.fold_in(splits[6], 1), N_BAND * N_TP * K_OWN // K_OWN)
    obs_band_turns = jax.random.permutation(jax.random.fold_in(splits[6], 3), N_BAND * N_TP * K_OWN // K_OWN)
    obs_band = jax.vmap(lambda own, number: assign_block(jax.random.fold_in(splits[6], 2), own, number, K_OWN, N_BAND, 1, CAP, 2))(obs_band_keys, obs_band_turns).reshape((N_BAND, N_TP, K_OWN, 1))
    obs_cell = with_ends(jax.random.randint(splits[7], (N_BAND, N_TP, K_OWN), 0, C * NLON), jax.random.fold_in(splits[7], 1), 0, (C * NLON) - 1).astype(jnp.int32)
    obs_value = centred(splits[8], (N_BAND, N_TP, K_OWN), 1.5, 8.0, ((0, 64), (1, 8)), jnp.float32)
    obs_weight = jnp.clip(jnp.exp(math.log(4.0) - 2.7725887 * jax.random.uniform(splits[9], (N_BAND, N_TP, K_OWN), jnp.float32) ** shard_levels(splits[9], (N_BAND, N_TP, K_OWN), ((0, 64), (1, 8)), -0.2, 0.2)), 0.25, 4.0)
    obs_offset = jnp.clip(1.0 * jax.random.uniform(splits[10], (N_BAND, N_TP, K_OWN), jnp.float32) ** shard_levels(splits[10], (N_BAND, N_TP, K_OWN), ((0, 64), (1, 8)), -0.2, 0.2), 0.0, 1.0)
    return {"control": control, "spec_sigma": spec_sigma, "prior_mean_field": prior_mean_field, "magnitude_factor": magnitude_factor, "w_in": w_in, "w_out": w_out, "obs_band": obs_band, "obs_cell": obs_cell, "obs_value": obs_value, "obs_weight": obs_weight, "obs_offset": obs_offset}


PRECISE = lax.Precision.HIGHEST
EPSILON = 1e-06

def legendre_table(wavenumber, wave_count, cycle_ids, lat_count):
    parity = wavenumber % 2
    frequency = jnp.arange(wave_count, dtype=jnp.int32) + parity
    phases = frequency[:, None] * (2 * cycle_ids[None, :] + 1) % (4 * lat_count)
    angles = phases.astype(jnp.float32) * (math.pi / (2 * lat_count))
    lat_basis = jnp.where(parity == 1, jnp.sin(angles), jnp.cos(angles))
    return lat_basis * math.sqrt(2.0 / lat_count)

def zonal_table(orders, columns, lon_count):
    phases = orders[:, None] * columns[None, :] % lon_count
    angles = phases.astype(jnp.float32) * (2.0 * math.pi / lon_count)
    return jnp.concatenate([jnp.cos(angles), jnp.sin(angles)], axis=0)

def rescale_unit(fields, gains):
    mean_sq = lax.optimization_barrier(jnp.mean(fields * fields, axis=0, keepdims=True))
    return fields * gains[:, None] * lax.rsqrt(mean_sq + EPSILON)

def magnitude_cotangent(fields, gains, grad_out):
    unused, pull = jax.vjp(lambda values: rescale_unit(values, gains), fields)
    return pull(grad_out)[0]

def gelu_tanh(values):
    return jax.nn.gelu(values, approximate=True)

def contract_first(left_op, right_op):
    return lax.dot_general(left_op, right_op, (((0,), (0,)), ((), ())), preferred_element_type=jnp.float32)

def group_forward(unit_scaled, in_group, out_group):
    pre_act = contract_first(in_group, unit_scaled)
    hidden = gelu_tanh(pre_act).astype(jnp.bfloat16)
    return contract_first(out_group, hidden)

def group_adjoint(unit_scaled, cotangent, in_group, out_group):
    pre_act = contract_first(in_group, unit_scaled)
    grad_hidden = jnp.dot(out_group, cotangent, preferred_element_type=jnp.float32)
    unused, pull = jax.vjp(gelu_tanh, pre_act)
    grad_pre = pull(grad_hidden)[0].astype(jnp.bfloat16)
    return jnp.dot(in_group, grad_pre, preferred_element_type=jnp.float32)

def quantized_aggregate(running_accumulate):
    rounded = lax.optimization_barrier(running_accumulate.astype(jnp.bfloat16))
    return lax.optimization_barrier(jnp.sum(rounded.astype(jnp.float32), axis=0))

def lagrange_weights(offsets):
    w_left = -offsets * (offsets - 1.0) * (offsets - 2.0) / 6.0
    w_here = (offsets + 1.0) * (offsets - 1.0) * (offsets - 2.0) / 2.0
    w_right = -(offsets + 1.0) * offsets * (offsets - 2.0) / 2.0
    w_far = (offsets + 1.0) * offsets * (offsets - 1.0) / 6.0
    return jnp.stack([w_left, w_here, w_right, w_far])

def reference(control, spec_sigma, prior_mean_field, magnitude_factor, w_in, w_out, obs_band, obs_cell, obs_value, obs_weight, obs_offset):
    coefficients = spec_sigma[:, None] * control
    cycle_ids = jnp.arange(NLAT, dtype=jnp.int32)
    mode_ids = jnp.arange(M, dtype=jnp.int32)
    by_mode = jnp.transpose(coefficients, (2, 0, 1, 3))

    def synthesize(pieces):
        wavenumber, column = pieces
        lat_basis = legendre_table(wavenumber, NN, cycle_ids, NLAT)
        return jnp.dot(column.reshape(2 * C, NN), lat_basis, precision=PRECISE)
    zonal_modes = lax.map(synthesize, (mode_ids, by_mode))
    cycle_modes = jnp.transpose(zonal_modes.reshape(M, C, 2, NLAT), (1, 3, 2, 0)).reshape(C * NLAT, 2 * M)
    zonal_basis = zonal_table(mode_ids, jnp.arange(NLON, dtype=jnp.int32), NLON)
    control_delta = jnp.dot(cycle_modes, zonal_basis, precision=PRECISE).reshape(C, NLAT, NLON)
    predicted_field = jnp.transpose(prior_mean_field + control_delta, (1, 0, 2))
    ff_group = FF // N_TP
    in_groups = jnp.transpose(w_in.reshape(C, N_TP, ff_group), (1, 0, 2))
    out_groups = w_out.reshape(N_TP, ff_group, C)

    def tangent_pass(cycle_state):
        unit_scaled = rescale_unit(cycle_state, magnitude_factor).astype(jnp.bfloat16)
        running_accumulate = lax.map(lambda pair: group_forward(unit_scaled, pair[0], pair[1]), (in_groups, out_groups))
        return cycle_state + quantized_aggregate(running_accumulate)
    integrate_ahead = lax.map(tangent_pass, predicted_field)
    tp_ids = jnp.arange(N_TP, dtype=jnp.int32)[None, :, None]
    cycle_of = obs_band[..., 0] * N_TP + tp_ids
    channel = obs_cell // NLON
    longitude = obs_cell % NLON
    shift_ids = jnp.arange(4, dtype=jnp.int32) - 1
    position_numbers = ((cycle_of * C + channel) * NLON)[None] + (longitude[None] + shift_ids[:, None, None, None]) % NLON
    coefficient_matrix = lagrange_weights(obs_offset)
    predicted_reading = lax.optimization_barrier(jnp.sum(coefficient_matrix * integrate_ahead.reshape(-1)[position_numbers], axis=0))
    innovation = obs_weight * (predicted_reading - obs_value)
    source_term = jnp.zeros((NLAT * C * NLON,), jnp.float32).at[position_numbers.reshape(-1)].add((coefficient_matrix * innovation[None]).reshape(-1))
    source_term = source_term.reshape(NLAT, C, NLON)

    def backward_loop_pass(pieces):
        cycle_state, cycle_forcing = pieces
        unit_scaled = rescale_unit(cycle_state, magnitude_factor).astype(jnp.bfloat16)
        cotangent = cycle_forcing.astype(jnp.bfloat16)
        running_accumulate = lax.map(lambda pair: group_adjoint(unit_scaled, cotangent, pair[0], pair[1]), (in_groups, out_groups))
        return cycle_forcing + magnitude_cotangent(cycle_state, magnitude_factor, quantized_aggregate(running_accumulate))
    costate_vector = lax.map(backward_loop_pass, (predicted_field, source_term))
    grad_modes = lax.dot_general(costate_vector.reshape(NLAT * C, NLON), zonal_basis, (((1,), (1,)), ((), ())), precision=PRECISE)
    grad_by_mode = jnp.transpose(grad_modes.reshape(NLAT, C, 2, M), (3, 1, 2, 0))

    def analyze(pieces):
        wavenumber, column = pieces
        lat_basis = legendre_table(wavenumber, NN, cycle_ids, NLAT)
        return lax.dot_general(column.reshape(2 * C, NLAT), lat_basis, (((1,), (1,)), ((), ())), precision=PRECISE)
    projected = lax.map(analyze, (mode_ids, grad_by_mode))
    projected = jnp.transpose(projected.reshape(M, C, 2, NN), (1, 2, 0, 3))
    return control + spec_sigma[:, None] * projected
```

```python
import math

import jax
import jax.numpy as jnp
import ml_dtypes
import numpy as np
from jax import lax
from jax.experimental import pallas as pl
from jax.experimental.pallas import tpu as pltpu
from jax.sharding import PartitionSpec as P

EPSILON = 1e-06
BF16 = jnp.bfloat16
F32 = jnp.float32

BLOCKS = 6
STRIDE = 240
WIDTH = 256
ROWS = 72
LANES = 128
BANDS = 64
TPS = 8
SLOTS = 64
FIELDS = 8
ROW_SHIFT = 256
OBS_CHUNK = 512


def split_np(table):
    high = table.astype(np.float32).astype(ml_dtypes.bfloat16)
    low = (table - high.astype(np.float64)).astype(np.float32).astype(ml_dtypes.bfloat16)
    return high, low


def legendre_np(wave_count, lat_count):
    cycles = np.arange(lat_count)
    tables = []
    for parity in range(2):
        frequency = np.arange(wave_count) + parity
        phases = (2 * cycles[:, None] + 1) * frequency[None, :] % (4 * lat_count)
        angles = phases * (math.pi / (2 * lat_count))
        basis = np.sin(angles) if parity else np.cos(angles)
        tables.append(basis * math.sqrt(2.0 / lat_count))
    return split_np(np.stack(tables))


def zonal_np(orders, lon_count):
    phases = np.arange(orders)[:, None] * np.arange(WIDTH)[None, :] % lon_count
    angles = phases * (2.0 * math.pi / lon_count)
    return split_np(np.concatenate([np.cos(angles), np.sin(angles)], axis=0))


def turn_np(orders, lon_count):
    phases = np.arange(BLOCKS)[:, None] * STRIDE * np.arange(orders)[None, :] % lon_count
    angles = phases * (2.0 * math.pi / lon_count)
    pad = np.zeros((8 - BLOCKS, orders))
    return np.concatenate([np.cos(angles), pad, np.sin(angles), pad]).astype(np.float32)


def split(values):
    high = values.astype(BF16)
    low = (values - high.astype(F32)).astype(BF16)
    return high, low


NN = (((1,), (0,)), ((), ()))
NT = (((1,), (1,)), ((), ()))


def dot(left, right, dims=NN):
    return lax.dot_general(left, right, dims, preferred_element_type=F32)


def dot3(left, right, dims=NN):
    return (
        dot(left[0], right[0], dims) + dot(left[0], right[1], dims) + dot(left[1], right[0], dims)
    )


def lane_ids(shape):
    return lax.broadcasted_iota(jnp.int32, shape, len(shape) - 1)


SEND_ROWS = 224
REST_LANE = 96


def synthesis_kernel(parity, control, sigma, w_in, w_out, table_high, table_low, out, coef, modes):
    channels = w_in.shape[0]
    coef[...] = jnp.zeros_like(coef)
    for block in range(3):
        lanes = pl.ds(block * LANES, LANES)
        deviation = sigma[pl.ds(block, channels, stride=3), :]
        first = deviation * control[pl.ds(block, channels, stride=6), :]
        second = deviation * control[pl.ds(3 + block, channels, stride=6), :]
        coef[0:channels, lanes] = first
        coef[ROWS:LANES, lanes] = second[: LANES - ROWS]
        tail = channels - (LANES - ROWS)
        coef[LANES + REST_LANE : LANES + REST_LANE + tail, lanes] = second[LANES - ROWS :]
    parts = split(coef[...])
    whole = dot3((table_high[0], table_low[0]), parts, NT)
    modes[0] = whole[:, 0:LANES]
    modes[1] = whole[:, LANES:]
    in_rows = jnp.pad(w_in[...].astype(F32), ((0, 80 - channels), (0, LANES - w_in.shape[1])))
    out_rows = jnp.pad(w_out[...].astype(F32), ((0, 80 - channels), (0, LANES - w_in.shape[1])))
    out_rows = out_rows.astype(BF16)
    for dest in range(TPS):
        whole = modes[0, pl.ds(dest, BANDS, stride=TPS), :]
        rest = modes[1, pl.ds(dest, BANDS, stride=TPS), :]
        out[dest, 0:BANDS, :] = whole.astype(BF16)
        out[dest, BANDS : 2 * BANDS, :] = (rest + in_rows[0:BANDS]).astype(BF16)
        out[dest, 2 * BANDS : 144, :] = in_rows[BANDS:].astype(BF16)
        out[dest, 144:SEND_ROWS, :] = out_rows


def synthesis(parity, control, sigma, w_in, w_out_t, table):
    wave_count = table[0].shape[2]
    lat_count = table[0].shape[1]
    whole = lambda shape: pl.BlockSpec(shape, lambda i, p: (0,) * len(shape))
    chosen = pl.BlockSpec((1, lat_count, wave_count), lambda i, p: (p[0], 0, 0))
    return pl.pallas_call(
        synthesis_kernel,
        out_shape=jax.ShapeDtypeStruct((TPS, SEND_ROWS, LANES), BF16),
        grid_spec=pltpu.PrefetchScalarGridSpec(
            num_scalar_prefetch=1,
            grid=(1,),
            in_specs=[
                whole(control.shape),
                whole(sigma.shape),
                whole(w_in.shape),
                whole(w_out_t.shape),
                chosen,
                chosen,
            ],
            out_specs=whole((TPS, SEND_ROWS, LANES)),
            scratch_shapes=[
                pltpu.VMEM((2 * LANES, wave_count), F32),
                pltpu.VMEM((2, lat_count, LANES), F32),
            ],
        ),
        cost_estimate=pl.CostEstimate(flops=400_000_000, bytes_accessed=2_000_000, transcendentals=0),
        name="synthesis",
    )(parity, control, sigma, w_in, w_out_t, *table)


def pack_kernel(band, cell, value, weight, offset, out):
    blocks = band.shape[0]
    cells = cell[...].astype(F32)
    channel = jnp.floor((cells + 0.5) * (1.0 / 1440.0))
    start = cells - 1440.0 * channel - 1.0
    start = jnp.where(start < 0.0, start + 1440.0, start)
    part = jnp.floor((start + 0.5) * (1.0 / STRIDE))
    fields = []
    for source in (value, weight, offset):
        high = source[...].astype(BF16).astype(F32)
        fields += [high, source[...] - high]
    fields += [part * ROWS + channel - ROW_SHIFT, start - part * STRIDE]
    band_ids = lax.broadcasted_iota(jnp.int32, (BANDS, LANES), 0)
    hits = [band_ids == band[i : i + 1, :] for i in range(blocks)]
    ones = [jnp.where(hit, 1.0, 0.0) for hit in hits]
    square = (LANES, 2 * LANES)
    row, column = lax.broadcasted_iota(jnp.int32, square, 0), lane_ids(square)
    before = jnp.where((row < column) | (column >= LANES), 1.0, 0.0).astype(BF16)
    counts = dot(jnp.concatenate(ones, axis=0).astype(BF16), before)
    slot_ids = lax.broadcasted_iota(jnp.int32, (LANES, LANES), 0).astype(F32)
    taken = jnp.zeros((BANDS, LANES), F32)
    total = jnp.zeros((BANDS, FIELDS * LANES), F32)
    for i in range(blocks):
        within = counts[i * BANDS : (i + 1) * BANDS, :]
        rank = jnp.sum(ones[i] * (within[:, :LANES] + taken), axis=0, keepdims=True)
        taken = taken + within[:, LANES:]
        here = slot_ids == rank + (LANES - SLOTS)
        spread = [jnp.where(here, field[i : i + 1, :], 0.0).astype(BF16) for field in fields]
        total = total + dot(ones[i].astype(BF16), jnp.concatenate(spread, axis=0), NT)
    out[...] = total


def pack_obs(band, cell, value, weight, offset):
    return pl.pallas_call(
        pack_kernel,
        out_shape=jax.ShapeDtypeStruct((BANDS, FIELDS * LANES), F32),
        cost_estimate=pl.CostEstimate(flops=200_000_000, bytes_accessed=300_000, transcendentals=0),
        name="pack_obs",
    )(band, cell, value, weight, offset)


def regroup_kernel(arrived, obs, out, rows):
    lanes = lane_ids((BANDS, LANES))
    for t in range(TPS):
        rows[pl.ds(t, BANDS, stride=16), :] = arrived[t, 0:BANDS, :].astype(F32)
        rest = pltpu.roll(arrived[t, BANDS : 2 * BANDS, :].astype(F32), LANES - REST_LANE, 1)
        rest = jnp.where(lanes < 16, rest, obs[:, t * LANES : (t + 1) * LANES])
        rows[pl.ds(8 + t, BANDS, stride=16), :] = rest
    out[...] = rows[...].astype(BF16)


def regroup(arrived, obs):
    return pl.pallas_call(
        regroup_kernel,
        out_shape=jax.ShapeDtypeStruct((BANDS * 16, LANES), BF16),
        scratch_shapes=[pltpu.VMEM((BANDS * 16, LANES), F32)],
        cost_estimate=pl.CostEstimate(flops=300_000, bytes_accessed=800_000, transcendentals=0),
        name="regroup",
    )(arrived, obs)


def weights_kernel(arrived, in_rows, in_columns, out_rows, out_columns):
    for columns, rows, start in ((in_columns, in_rows, BANDS), (out_columns, out_rows, 144)):
        pieces = []
        for t in range(TPS):
            piece = arrived[t, start : start + 80, :].astype(F32)
            piece = jnp.concatenate([piece, jnp.zeros((LANES - 80, LANES), F32)], axis=0)
            pieces.append(piece.T[0:96])
        upright = jnp.concatenate(pieces, axis=0)
        columns[...] = upright.astype(BF16)
        rows[...] = upright.T[0:80].astype(BF16)


def gather_weights(arrived):
    hidden = TPS * 96
    return pl.pallas_call(
        weights_kernel,
        out_shape=(
            jax.ShapeDtypeStruct((80, hidden), BF16),
            jax.ShapeDtypeStruct((hidden, LANES), BF16),
            jax.ShapeDtypeStruct((80, hidden), BF16),
            jax.ShapeDtypeStruct((hidden, LANES), BF16),
        ),
        cost_estimate=pl.CostEstimate(flops=1_000_000, bytes_accessed=1_500_000, transcendentals=0),
        name="weights",
    )(arrived)


GELU_SCALE = math.sqrt(2.0 / math.pi)
GELU_CUBE = 0.044715


def lagrange_rows(offset):
    return (
        -offset * (offset - 1.0) * (offset - 2.0) / 6.0,
        (offset + 1.0) * (offset - 1.0) * (offset - 2.0) / 2.0,
        -(offset + 1.0) * offset * (offset - 2.0) / 2.0,
        (offset + 1.0) * offset * (offset - 1.0) / 6.0,
    )


def cycle_kernel(
    channels,
    arrived,
    prior,
    gains,
    in_rows,
    in_columns,
    out_rows,
    out_columns,
    table_high,
    table_low,
    turns,
    out,
    state,
    forecast_t,
    slopes,
    obs,
    forcing,
    paired,
):
    orders = turns.shape[1]
    table = (table_high[...], table_low[...])
    slices = arrived[...].astype(F32)
    rest = slices[:, 8:16, :]
    cos_sin = slices[:, 0:8, :].reshape(orders, LANES).T
    tail = rest.reshape(orders, LANES).T
    cos_part = cos_sin[0:ROWS]
    sin_part = jnp.concatenate([cos_sin[ROWS:LANES], tail[0:16]], axis=0)
    pairs = rest.reshape(BANDS // 2, 2, FIELDS, LANES)
    near = pltpu.roll(pairs[:, 0].reshape(BANDS // 2 * FIELDS, LANES), LANES - SLOTS, 1)
    near = near.reshape(BANDS // 2, FIELDS, LANES)
    lanes = lane_ids(near.shape)
    obs[...] = jnp.where(lanes < SLOTS, near, pairs[:, 1])

    for a in range(BLOCKS):
        turn_cos, turn_sin = turns[a : a + 1, :], turns[8 + a : 9 + a, :]
        turned = jnp.concatenate(
            [cos_part * turn_cos + sin_part * turn_sin, sin_part * turn_cos - cos_part * turn_sin],
            axis=1,
        )
        field = prior[a] + dot3(split(turned), table)
        state[a] = field
        mean_sq = jnp.sum(field * field, axis=0, keepdims=True) * (1.0 / channels)
        unit = (field * gains[...] * lax.rsqrt(mean_sq + EPSILON)).astype(BF16)
        pre = dot(in_columns[:, 0:ROWS], unit)
        square = pre * pre
        inner = pre * (GELU_SCALE + (GELU_SCALE * GELU_CUBE) * square)
        half = 0.5 + 0.5 * jnp.tanh(inner)
        hidden = pre * half
        slopes[a] = half + hidden * (1.0 - half) * (
            2.0 * GELU_SCALE + (6.0 * GELU_SCALE * GELU_CUBE) * square
        )
        ahead = field + dot(out_rows[...], hidden.astype(BF16))[0:ROWS]
        ahead_t = ahead.T
        high = ahead_t.astype(BF16)
        forecast_t[0:WIDTH, a * ROWS : (a + 1) * ROWS] = high
        forecast_t[WIDTH : 2 * WIDTH, a * ROWS : (a + 1) * ROWS] = (
            ahead_t - high.astype(F32)
        ).astype(BF16)

    forcing[...] = jnp.zeros_like(forcing)
    row_ids = lax.broadcasted_iota(jnp.int32, (BLOCKS * ROWS, OBS_CHUNK), 0).astype(F32)
    place_ids = lax.broadcasted_iota(jnp.int32, (WIDTH, OBS_CHUNK), 0).astype(F32)
    per_chunk = OBS_CHUNK // LANES

    def observe(chunk, carry):
        fields = [obs[chunk * per_chunk + i] for i in range(per_chunk)]
        fields = jnp.concatenate(fields, axis=1)
        value = fields[0:1] + fields[1:2]
        weight = fields[2:3] + fields[3:4]
        offset = fields[4:5] + fields[5:6]
        row = fields[6:7] + float(ROW_SHIFT)
        place = place_ids - fields[7:8]
        chosen = jnp.where(row_ids == row, 1.0, 0.0).astype(BF16)
        picked = dot(forecast_t[...], chosen)
        w_left, w_here, w_right, w_far = lagrange_rows(offset)
        stencil = jnp.where(
            place == 0.0,
            w_left,
            jnp.where(
                place == 1.0,
                w_here,
                jnp.where(place == 2.0, w_right, jnp.where(place == 3.0, w_far, 0.0)),
            ),
        )
        reading = jnp.sum(stencil * (picked[0:WIDTH] + picked[WIDTH:]), axis=0, keepdims=True)
        spread = stencil * (weight * (reading - value))
        high, low = split(spread)
        forcing[...] += dot(chosen, jnp.concatenate([high, low], axis=0), NT)
        return carry

    lax.fori_loop(0, obs.shape[0] // per_chunk, observe, 0)

    lanes = lane_ids((ROWS, WIDTH))
    halos = []
    source = []
    for a in range(BLOCKS):
        rows = slice(a * ROWS, (a + 1) * ROWS)
        both = forcing[rows, 0:WIDTH] + forcing[rows, WIDTH : 2 * WIDTH]
        halos.append(pltpu.roll(both, WIDTH - STRIDE, 1))
        source.append(both)
    grad_cos = jnp.zeros((ROWS, orders), F32)
    grad_sin = jnp.zeros((ROWS, orders), F32)
    for a in range(BLOCKS):
        force = jnp.where(lanes < STRIDE, source[a], 0.0)
        force = force + jnp.where(lanes < 3, halos[a - 1], 0.0)
        grad_hidden = dot(out_columns[:, 0:ROWS], force.astype(BF16))
        grad_pre = (grad_hidden * slopes[a]).astype(BF16)
        grad_unit = dot(in_rows[...], grad_pre)[0:ROWS]
        field = state[a]
        mean_sq = jnp.sum(field * field, axis=0, keepdims=True) * (1.0 / channels)
        inverse = lax.rsqrt(mean_sq + EPSILON)
        scaled = grad_unit * gains[...]
        along = jnp.sum(scaled * field, axis=0, keepdims=True) * (1.0 / channels)
        costate = force + scaled * inverse - field * (along * inverse * inverse * inverse)
        block = dot3(split(costate), table, NT)
        turn_cos, turn_sin = turns[a : a + 1, :], turns[8 + a : 9 + a, :]
        block_cos, block_sin = block[:, 0:orders], block[:, orders:]
        grad_cos = grad_cos + turn_cos * block_cos - turn_sin * block_sin
        grad_sin = grad_sin + turn_sin * block_cos + turn_cos * block_sin

    lanes = lane_ids((orders, LANES))
    pad = jnp.zeros((LANES - ROWS, orders), F32)
    for r, grad in ((0, grad_cos), (1, grad_sin)):
        upright = jnp.concatenate([grad, pad], axis=0).T
        high = upright.astype(BF16).astype(F32)
        low = pltpu.roll(upright - high, channels, 1)
        paired[pl.ds(r, orders, stride=2), :] = jnp.where(lanes < channels, high, low)
    out[...] = paired[...].astype(BF16)


def run_cycle(channels, arrived, prior, gains, weights, table, turns):
    orders = turns.shape[1]
    hidden = weights[1].shape[0]
    return pl.pallas_call(
        lambda *refs: cycle_kernel(channels, *refs),
        out_shape=jax.ShapeDtypeStruct((2 * orders, LANES), BF16),
        scratch_shapes=[
            pltpu.VMEM((BLOCKS, ROWS, WIDTH), F32),
            pltpu.VMEM((2 * WIDTH, BLOCKS * ROWS), BF16),
            pltpu.VMEM((BLOCKS, hidden, WIDTH), F32),
            pltpu.VMEM((BANDS // 2, FIELDS, LANES), F32),
            pltpu.VMEM((BLOCKS * ROWS, 2 * WIDTH), F32),
            pltpu.VMEM((2 * orders, LANES), F32),
        ],
        compiler_params=pltpu.CompilerParams(vmem_limit_bytes=40 * 1024 * 1024),
        cost_estimate=pl.CostEstimate(
            flops=8_000_000_000, bytes_accessed=4_000_000, transcendentals=1_200_000
        ),
        name="cycle",
    )(arrived, prior, gains, *weights, *table, turns)


def analysis_kernel(parity, arrived, control, sigma, table_high, table_low, out, rows):
    channels = sigma.shape[0] // 3
    orders = arrived.shape[0] // 2
    rows[...] = arrived[...].astype(F32)
    lanes = lane_ids((orders, LANES))
    for r in range(2):
        both = rows[pl.ds(r, orders, stride=2), :]
        low = pltpu.roll(both, LANES - channels, 1)
        grad = jnp.where(lanes < channels, both, 0.0)
        grad = grad + jnp.where(lanes < LANES - channels, low, 0.0)
        grad_t = split(grad.T[0:ROWS])
        projected = dot3(grad_t, (table_high[0], table_low[0]))
        for block in range(3):
            deviation = sigma[pl.ds(block, channels, stride=3), :]
            place = pl.ds(3 * r + block, channels, stride=6)
            step = projected[0:channels, block * LANES : (block + 1) * LANES]
            out[place, :] = control[place, :] + deviation * step


def analysis(parity, arrived, control, sigma, table):
    wave_count = table[0].shape[2]
    lat_count = table[0].shape[1]
    whole = lambda shape: pl.BlockSpec(shape, lambda i, p: (0,) * len(shape))
    chosen = pl.BlockSpec((1, lat_count, wave_count), lambda i, p: (p[0], 0, 0))
    return pl.pallas_call(
        analysis_kernel,
        out_shape=jax.ShapeDtypeStruct(control.shape, F32),
        grid_spec=pltpu.PrefetchScalarGridSpec(
            num_scalar_prefetch=1,
            grid=(1,),
            in_specs=[
                whole(arrived.shape),
                whole(control.shape),
                whole(sigma.shape),
                chosen,
                chosen,
            ],
            out_specs=whole(control.shape),
            scratch_shapes=[pltpu.VMEM(arrived.shape, F32)],
        ),
        cost_estimate=pl.CostEstimate(flops=400_000_000, bytes_accessed=2_000_000, transcendentals=0),
        name="analysis",
    )(parity, arrived, control, sigma, *table)


def shards(
    control,
    spec_sigma,
    prior_mean_field,
    magnitude_factor,
    w_in,
    w_out,
    obs_band,
    obs_cell,
    obs_value,
    obs_weight,
    obs_offset,
):
    channels, _, _, wave_count = control.shape
    lat_count = BANDS * TPS
    lon_count = prior_mean_field.shape[2]
    legendre = legendre_np(wave_count, lat_count)
    zonal = zonal_np(lat_count, lon_count)
    turns = turn_np(lat_count, lon_count)
    parity = (lax.axis_index("tp") % 2).astype(jnp.int32).reshape(1)
    control_rows = control.reshape(-1, LANES)
    sigma_rows = spec_sigma.reshape(-1, LANES)

    send = synthesis(parity, control_rows, sigma_rows, w_in, w_out.T, legendre)
    got = lax.all_to_all(send, "tp", split_axis=0, concat_axis=0, tiled=True)
    obs = pack_obs(
        *(
            field.reshape(-1, LANES)
            for field in (obs_band, obs_cell, obs_value, obs_weight, obs_offset)
        )
    )
    send = regroup(got, obs).reshape(BANDS, 16, LANES)
    arrived = lax.all_to_all(send, "band", split_axis=0, concat_axis=0, tiled=True)
    weights = gather_weights(got)
    prior = jnp.pad(prior_mean_field[:, 0, :], ((0, ROWS - channels), (0, 0)))
    prior = jnp.concatenate([prior, prior[:, : WIDTH - STRIDE]], axis=1)
    prior = jnp.stack([prior[:, a * STRIDE : a * STRIDE + WIDTH] for a in range(BLOCKS)])
    gains = jnp.broadcast_to(
        jnp.pad(magnitude_factor, (0, ROWS - channels))[:, None], (ROWS, WIDTH)
    )
    modes = run_cycle(channels, arrived, prior, gains, weights, zonal, turns)
    modes = lax.all_to_all(
        modes.reshape(lat_count, 2, LANES),
        ("band", "tp"),
        split_axis=0,
        concat_axis=0,
        tiled=True,
    )
    result = analysis(
        parity, modes.reshape(2 * lat_count, LANES), control_rows, sigma_rows, legendre
    )
    return result.reshape(control.shape)


def solution(mesh):
    placed = (
        P(None, None, ("band", "tp"), None),
        P(None, ("band", "tp"), None),
        P(None, ("band", "tp"), None),
        P(),
        P(None, "tp"),
        P("tp", None),
        P("band", "tp", None, None),
        P("band", "tp", None),
        P("band", "tp", None),
        P("band", "tp", None),
        P("band", "tp", None),
    )
    return jax.shard_map(
        shards,
        mesh=mesh,
        in_specs=placed,
        out_specs=P(None, None, ("band", "tp"), None),
        check_vma=False,
    )
```

```python
import math

import jax
import jax.numpy as jnp
import ml_dtypes
import numpy as np
from jax import lax
from jax.experimental import pallas as pl
from jax.experimental.pallas import tpu as pltpu
from jax.sharding import PartitionSpec as P

EPSILON = 1e-06
BF16 = jnp.bfloat16
F32 = jnp.float32

BLOCKS = 6
STRIDE = 240
WIDTH = 256
ROWS = 72
LANES = 128
BANDS = 64
TPS = 8
SLOTS = 64
FIELDS = 8
ROW_SHIFT = 256
OBS_CHUNK = 512
MIB = 1024 * 1024


def split_np(table):
    high = table.astype(np.float32).astype(ml_dtypes.bfloat16)
    low = (table - high.astype(np.float64)).astype(np.float32).astype(ml_dtypes.bfloat16)
    return high, low


def legendre_np(wave_count, lat_count):
    cycles = np.arange(lat_count)
    tables = []
    for parity in range(2):
        frequency = np.arange(wave_count) + parity
        phases = (2 * cycles[:, None] + 1) * frequency[None, :] % (4 * lat_count)
        angles = phases * (math.pi / (2 * lat_count))
        basis = np.sin(angles) if parity else np.cos(angles)
        tables.append(basis * math.sqrt(2.0 / lat_count))
    return split_np(np.stack(tables))


def zonal_np(orders, lon_count):
    phases = np.arange(orders)[:, None] * np.arange(WIDTH)[None, :] % lon_count
    angles = phases * (2.0 * math.pi / lon_count)
    high, low = split_np(np.concatenate([np.cos(angles), np.sin(angles)], axis=0))
    return high, low, np.ascontiguousarray(high.T), np.ascontiguousarray(low.T)


def turn_np(orders, lon_count):
    phases = np.arange(BLOCKS)[:, None] * STRIDE * np.arange(orders)[None, :] % lon_count
    angles = phases * (2.0 * math.pi / lon_count)
    pad = np.zeros((8 - BLOCKS, orders))
    return np.concatenate([np.cos(angles), pad, np.sin(angles), pad]).astype(np.float32)


def split(values):
    high = values.astype(BF16)
    low = (values - high.astype(F32)).astype(BF16)
    return high, low


NN = (((1,), (0,)), ((), ()))
NT = (((1,), (1,)), ((), ()))


def dot(left, right, dims=NN):
    return lax.dot_general(left, right, dims, preferred_element_type=F32)


def dot3(left, right, dims=NN):
    return (
        dot(left[0], right[0], dims) + dot(left[0], right[1], dims) + dot(left[1], right[0], dims)
    )


def lane_ids(shape):
    return lax.broadcasted_iota(jnp.int32, shape, len(shape) - 1)


SEND_ROWS = 224
REST_LANE = 96


def synthesis_kernel(parity, control, sigma, w_in, w_out, table_high, table_low, out, coef, modes):
    channels = w_in.shape[0]
    coef[...] = jnp.zeros_like(coef)
    deviation = sigma[:, 0, :]
    first = deviation * control[:, 0, 0, :]
    second = deviation * control[:, 1, 0, :]
    coef[0:channels, :] = first
    coef[ROWS:LANES, :] = second[: LANES - ROWS]
    tail = channels - (LANES - ROWS)
    coef[LANES + REST_LANE : LANES + REST_LANE + tail, :] = second[LANES - ROWS :]
    parts = split(coef[...])
    whole = dot3((table_high[0], table_low[0]), parts, NT)
    modes[0] = whole[:, 0:LANES]
    modes[1] = whole[:, LANES:]
    in_rows = jnp.pad(w_in[...].astype(F32), ((0, 80 - channels), (0, LANES - w_in.shape[1])))
    out_rows = jnp.pad(w_out[...].astype(F32), ((0, 80 - channels), (0, LANES - w_in.shape[1])))
    out_rows = out_rows.astype(BF16)
    for dest in range(TPS):
        whole = modes[0, pl.ds(dest, BANDS, stride=TPS), :]
        rest = modes[1, pl.ds(dest, BANDS, stride=TPS), :]
        out[dest, 0:BANDS, :] = whole.astype(BF16)
        out[dest, BANDS : 2 * BANDS, :] = (rest + in_rows[0:BANDS]).astype(BF16)
        out[dest, 2 * BANDS : 144, :] = in_rows[BANDS:].astype(BF16)
        out[dest, 144:SEND_ROWS, :] = out_rows


def synthesis(parity, control, sigma, w_in, w_out_t, table):
    wave_count = table[0].shape[2]
    lat_count = table[0].shape[1]
    whole = lambda shape: pl.BlockSpec(shape, lambda i, p: (0,) * len(shape))
    chosen = pl.BlockSpec((1, lat_count, wave_count), lambda i, p: (p[0], 0, 0))
    return pl.pallas_call(
        synthesis_kernel,
        out_shape=jax.ShapeDtypeStruct((TPS, SEND_ROWS, LANES), BF16),
        grid_spec=pltpu.PrefetchScalarGridSpec(
            num_scalar_prefetch=1,
            grid=(1,),
            in_specs=[
                whole(control.shape),
                whole(sigma.shape),
                whole(w_in.shape),
                whole(w_out_t.shape),
                chosen,
                chosen,
            ],
            out_specs=whole((TPS, SEND_ROWS, LANES)),
            scratch_shapes=[
                pltpu.VMEM((2 * LANES, wave_count), F32),
                pltpu.VMEM((2, lat_count, LANES), F32),
            ],
        ),
        cost_estimate=pl.CostEstimate(flops=400_000_000, bytes_accessed=2_000_000, transcendentals=0),
        compiler_params=pltpu.CompilerParams(vmem_limit_bytes=12 * MIB),
        name="synthesis",
    )(parity, control, sigma, w_in, w_out_t, *table)


def pack_kernel(band, cell, value, weight, offset, out):
    blocks = band.shape[0]
    cells = cell[...].astype(F32)
    channel = jnp.floor((cells + 0.5) * (1.0 / 1440.0))
    start = cells - 1440.0 * channel - 1.0
    start = jnp.where(start < 0.0, start + 1440.0, start)
    part = jnp.floor((start + 0.5) * (1.0 / STRIDE))
    fields = []
    for source in (value, weight, offset):
        high = source[...].astype(BF16).astype(F32)
        fields += [high, source[...] - high]
    fields += [part * ROWS + channel - ROW_SHIFT, start - part * STRIDE]
    band_ids = lax.broadcasted_iota(jnp.int32, (BANDS, LANES), 0)
    hits = [band_ids == band[i : i + 1, :] for i in range(blocks)]
    ones = [jnp.where(hit, 1.0, 0.0) for hit in hits]
    square = (LANES, 2 * LANES)
    row, column = lax.broadcasted_iota(jnp.int32, square, 0), lane_ids(square)
    before = jnp.where((row < column) | (column >= LANES), 1.0, 0.0).astype(BF16)
    counts = dot(jnp.concatenate(ones, axis=0).astype(BF16), before)
    slot_ids = lax.broadcasted_iota(jnp.int32, (LANES, LANES), 0).astype(F32)
    taken = jnp.zeros((BANDS, LANES), F32)
    total = jnp.zeros((BANDS, FIELDS * LANES), F32)
    for i in range(blocks):
        within = counts[i * BANDS : (i + 1) * BANDS, :]
        rank = jnp.sum(ones[i] * (within[:, :LANES] + taken), axis=0, keepdims=True)
        taken = taken + within[:, LANES:]
        here = slot_ids == rank + (LANES - SLOTS)
        spread = [jnp.where(here, field[i : i + 1, :], 0.0).astype(BF16) for field in fields]
        total = total + dot(ones[i].astype(BF16), jnp.concatenate(spread, axis=0), NT)
    out[...] = total


def pack_obs(band, cell, value, weight, offset):
    return pl.pallas_call(
        pack_kernel,
        out_shape=jax.ShapeDtypeStruct((BANDS, FIELDS * LANES), F32),
        cost_estimate=pl.CostEstimate(flops=200_000_000, bytes_accessed=300_000, transcendentals=0),
        compiler_params=pltpu.CompilerParams(vmem_limit_bytes=8 * MIB),
        name="pack_obs",
    )(band, cell, value, weight, offset)


def regroup_kernel(arrived, obs, out, rows):
    lanes = lane_ids((BANDS, LANES))
    for t in range(TPS):
        rows[pl.ds(t, BANDS, stride=16), :] = arrived[t, 0:BANDS, :].astype(F32)
        rest = pltpu.roll(arrived[t, BANDS : 2 * BANDS, :].astype(F32), LANES - REST_LANE, 1)
        rest = jnp.where(lanes < 16, rest, obs[:, t * LANES : (t + 1) * LANES])
        rows[pl.ds(8 + t, BANDS, stride=16), :] = rest
    out[...] = rows[...].astype(BF16)


def regroup(arrived, obs):
    return pl.pallas_call(
        regroup_kernel,
        out_shape=jax.ShapeDtypeStruct((BANDS * 16, LANES), BF16),
        scratch_shapes=[pltpu.VMEM((BANDS * 16, LANES), F32)],
        cost_estimate=pl.CostEstimate(flops=300_000, bytes_accessed=800_000, transcendentals=0),
        compiler_params=pltpu.CompilerParams(vmem_limit_bytes=8 * MIB),
        name="regroup",
    )(arrived, obs)


def weights_kernel(arrived, in_rows, in_columns, out_rows, out_columns):
    for columns, rows, start in ((in_columns, in_rows, BANDS), (out_columns, out_rows, 144)):
        pieces = []
        for t in range(TPS):
            piece = arrived[t, start : start + 80, :].astype(F32)
            piece = jnp.concatenate([piece, jnp.zeros((LANES - 80, LANES), F32)], axis=0)
            pieces.append(piece.T[0:96])
        upright = jnp.concatenate(pieces, axis=0)
        columns[...] = upright.astype(BF16)
        rows[...] = upright.T[0:80].astype(BF16)


def gather_weights(arrived):
    hidden = TPS * 96
    return pl.pallas_call(
        weights_kernel,
        out_shape=(
            jax.ShapeDtypeStruct((80, hidden), BF16),
            jax.ShapeDtypeStruct((hidden, LANES), BF16),
            jax.ShapeDtypeStruct((80, hidden), BF16),
            jax.ShapeDtypeStruct((hidden, LANES), BF16),
        ),
        cost_estimate=pl.CostEstimate(flops=1_000_000, bytes_accessed=1_500_000, transcendentals=0),
        compiler_params=pltpu.CompilerParams(vmem_limit_bytes=8 * MIB),
        name="weights",
    )(arrived)


GELU_SCALE = math.sqrt(2.0 / math.pi)
GELU_CUBE = 0.044715


def lagrange_rows(offset):
    return (
        -offset * (offset - 1.0) * (offset - 2.0) / 6.0,
        (offset + 1.0) * (offset - 1.0) * (offset - 2.0) / 2.0,
        -(offset + 1.0) * offset * (offset - 2.0) / 2.0,
        (offset + 1.0) * offset * (offset - 1.0) / 6.0,
    )


def cycle_kernel(
    channels,
    arrived,
    prior,
    gains,
    in_rows,
    in_columns,
    out_rows,
    out_columns,
    table_high,
    table_low,
    wide_high,
    wide_low,
    turns,
    out,
    state,
    slopes,
    obs,
    chosen_all,
    spread_all,
    paired,
):
    orders = turns.shape[1]
    slices = arrived[...].astype(F32)
    rest = slices[:, 8:16, :]
    cos_sin = slices[:, 0:8, :].reshape(orders, LANES).T
    tail = rest.reshape(orders, LANES).T
    cos_part = cos_sin[0:ROWS]
    sin_part = jnp.concatenate([cos_sin[ROWS:LANES], tail[0:16]], axis=0)
    pairs = rest.reshape(BANDS // 2, 2, FIELDS, LANES)
    near = pltpu.roll(pairs[:, 0].reshape(BANDS // 2 * FIELDS, LANES), LANES - SLOTS, 1)
    near = near.reshape(BANDS // 2, FIELDS, LANES)
    obs[...] = jnp.where(lane_ids(near.shape) < SLOTS, near, pairs[:, 1])

    turned = []
    for a in range(BLOCKS):
        turn_cos, turn_sin = turns[a : a + 1, :], turns[8 + a : 9 + a, :]
        turned_cos = cos_part * turn_cos + sin_part * turn_sin
        turned_sin = sin_part * turn_cos - cos_part * turn_sin
        turned.append(jnp.concatenate([turned_cos, turned_sin], axis=1))
    turned = split(jnp.concatenate(turned, axis=0))
    state[...] = prior[...].reshape(BLOCKS * ROWS, WIDTH) + dot3(
        turned, (table_high[...], table_low[...])
    )

    forecast = []
    for a in range(BLOCKS):
        field = state[a * ROWS : (a + 1) * ROWS, :]
        mean_sq = jnp.sum(field * field, axis=0, keepdims=True) * (1.0 / channels)
        unit = (field * gains[...] * lax.rsqrt(mean_sq + EPSILON)).astype(BF16)
        pre = dot(in_columns[:, 0:ROWS], unit)
        square = pre * pre
        inner = pre * (GELU_SCALE + (GELU_SCALE * GELU_CUBE) * square)
        half = 0.5 + 0.5 * jnp.tanh(inner)
        hidden = pre * half
        slopes[a] = half + hidden * (1.0 - half) * (
            2.0 * GELU_SCALE + (6.0 * GELU_SCALE * GELU_CUBE) * square
        )
        forecast.append(field + dot(out_rows[...], hidden.astype(BF16))[0:ROWS])
    forecast = split(jnp.concatenate(forecast, axis=0).T)
    forecast = jnp.concatenate(forecast, axis=0)

    per_chunk = OBS_CHUNK // LANES
    low_ids = lax.broadcasted_iota(jnp.int32, (16, OBS_CHUNK), 0).astype(F32)
    near_ids = lax.broadcasted_iota(jnp.int32, (32, OBS_CHUNK), 0).astype(F32)
    none = jnp.zeros((16, OBS_CHUNK), BF16)
    for chunk in range(obs.shape[0] // per_chunk):
        fields = [obs[chunk * per_chunk + i] for i in range(per_chunk)]
        fields = jnp.concatenate(fields, axis=1)
        value = fields[0:1] + fields[1:2]
        weight = fields[2:3] + fields[3:4]
        offset = fields[4:5] + fields[5:6]
        row = fields[6:7] + float(ROW_SHIFT)
        row_group = jnp.floor(row * (1.0 / 16.0))
        first = jnp.where(low_ids == row - 16.0 * row_group, 1.0, 0.0).astype(BF16)
        row_group = jnp.broadcast_to(row_group, (16, OBS_CHUNK)).astype(BF16)
        chosen = jnp.concatenate(
            [
                jnp.where(row_group == jnp.array(float(g), BF16), first, none)
                for g in range(BLOCKS * ROWS // 16)
            ],
            axis=0,
        )
        columns = slice(chunk * OBS_CHUNK, (chunk + 1) * OBS_CHUNK)
        chosen_all[:, columns] = chosen
        picked = dot(forecast, chosen)
        group = jnp.floor(fields[7:8] * (1.0 / 16.0))
        place = near_ids - (fields[7:8] - 16.0 * group)
        group8 = jnp.broadcast_to(group, (8, OBS_CHUNK))
        window = [jnp.zeros((8, OBS_CHUNK), F32)] * 4
        for g in range(WIDTH // 16 - 1):
            mask = group8 == float(g)
            for i in range(4):
                rows = slice(16 * g + 8 * i, 16 * g + 8 * i + 8)
                window[i] = jnp.where(mask, picked[rows] + picked[WIDTH:][rows], window[i])
        window = jnp.concatenate(window, axis=0)
        w_left, w_here, w_right, w_far = lagrange_rows(offset)
        stencil = jnp.where(
            place == 0.0,
            w_left,
            jnp.where(
                place == 1.0,
                w_here,
                jnp.where(place == 2.0, w_right, jnp.where(place == 3.0, w_far, 0.0)),
            ),
        )
        reading = jnp.sum(stencil * window, axis=0, keepdims=True)
        parts = split(stencil * (weight * (reading - value)))
        group = jnp.broadcast_to(group, (16, OBS_CHUNK)).astype(BF16)
        masks = [group == jnp.array(float(g), BF16) for g in range(WIDTH // 16 - 1)]
        for i, part in enumerate(parts):
            pieces = []
            for g in range(WIDTH // 16):
                piece = none
                if g > 0:
                    piece = jnp.where(masks[g - 1], part[16:32], piece)
                if g < WIDTH // 16 - 1:
                    piece = jnp.where(masks[g], part[0:16], piece)
                pieces.append(piece)
            spread_all[i * WIDTH : (i + 1) * WIDTH, columns] = jnp.concatenate(pieces, axis=0)
    forcing = dot(chosen_all[...], spread_all[...], NT)
    forcing = forcing[:, 0:WIDTH] + forcing[:, WIDTH:]

    lanes = lane_ids((BLOCKS * ROWS, WIDTH))
    halo = pltpu.roll(forcing, WIDTH - STRIDE, 1)
    halo = jnp.concatenate([halo[(BLOCKS - 1) * ROWS :], halo[: (BLOCKS - 1) * ROWS]], axis=0)
    forcing = jnp.where(lanes < STRIDE, forcing, 0.0) + jnp.where(lanes < 3, halo, 0.0)
    costate = []
    for a in range(BLOCKS):
        force = forcing[a * ROWS : (a + 1) * ROWS]
        grad_hidden = dot(out_columns[:, 0:ROWS], force.astype(BF16))
        grad_pre = (grad_hidden * slopes[a]).astype(BF16)
        grad_unit = dot(in_rows[...], grad_pre)[0:ROWS]
        field = state[a * ROWS : (a + 1) * ROWS, :]
        mean_sq = jnp.sum(field * field, axis=0, keepdims=True) * (1.0 / channels)
        inverse = lax.rsqrt(mean_sq + EPSILON)
        scaled = grad_unit * gains[...]
        along = jnp.sum(scaled * field, axis=0, keepdims=True) * (1.0 / channels)
        costate.append(force + scaled * inverse - field * (along * inverse * inverse * inverse))
    costate = split(jnp.concatenate(costate, axis=0))
    blocks = dot3(costate, (wide_high[...], wide_low[...]))
    grad_cos = jnp.zeros((ROWS, orders), F32)
    grad_sin = jnp.zeros((ROWS, orders), F32)
    for a in range(BLOCKS):
        turn_cos, turn_sin = turns[a : a + 1, :], turns[8 + a : 9 + a, :]
        block = blocks[a * ROWS : (a + 1) * ROWS]
        block_cos, block_sin = block[:, 0:orders], block[:, orders:]
        grad_cos = grad_cos + turn_cos * block_cos - turn_sin * block_sin
        grad_sin = grad_sin + turn_sin * block_cos + turn_cos * block_sin

    lanes = lane_ids((orders, LANES))
    pad = jnp.zeros((LANES - ROWS, orders), F32)
    for r, grad in ((0, grad_cos), (1, grad_sin)):
        upright = jnp.concatenate([grad, pad], axis=0).T
        high = upright.astype(BF16).astype(F32)
        low = pltpu.roll(upright - high, channels, 1)
        paired[pl.ds(r, orders, stride=2), :] = jnp.where(lanes < channels, high, low)
    out[...] = paired[...].astype(BF16)


def run_cycle(channels, arrived, prior, gains, weights, table, turns):
    orders = turns.shape[1]
    hidden = weights[1].shape[0]
    return pl.pallas_call(
        lambda *refs: cycle_kernel(channels, *refs),
        out_shape=jax.ShapeDtypeStruct((2 * orders, LANES), BF16),
        scratch_shapes=[
            pltpu.VMEM((BLOCKS * ROWS, WIDTH), F32),
            pltpu.VMEM((BLOCKS, hidden, WIDTH), F32),
            pltpu.VMEM((BANDS // 2, FIELDS, LANES), F32),
            pltpu.VMEM((BLOCKS * ROWS, BANDS * SLOTS), BF16),
            pltpu.VMEM((2 * WIDTH, BANDS * SLOTS), BF16),
            pltpu.VMEM((2 * orders, LANES), F32),
        ],
        compiler_params=pltpu.CompilerParams(vmem_limit_bytes=36 * MIB),
        cost_estimate=pl.CostEstimate(
            flops=8_000_000_000, bytes_accessed=4_000_000, transcendentals=1_200_000
        ),
        name="cycle",
    )(arrived, prior, gains, *weights, *table, turns)


def analysis_kernel(parity, arrived, control, sigma, table_high, table_low, out, rows):
    channels = sigma.shape[0]
    orders = arrived.shape[0] // 2
    rows[...] = arrived[...].astype(F32)
    lanes = lane_ids((orders, LANES))
    for r in range(2):
        both = rows[pl.ds(r, orders, stride=2), :]
        low = pltpu.roll(both, LANES - channels, 1)
        grad = jnp.where(lanes < channels, both, 0.0)
        grad = grad + jnp.where(lanes < LANES - channels, low, 0.0)
        grad_t = split(grad.T[0:ROWS])
        projected = dot3(grad_t, (table_high[0], table_low[0]))
        out[:, r, 0, :] = control[:, r, 0, :] + sigma[:, 0, :] * projected[0:channels]


def analysis(parity, arrived, control, sigma, table):
    wave_count = table[0].shape[2]
    lat_count = table[0].shape[1]
    whole = lambda shape: pl.BlockSpec(shape, lambda i, p: (0,) * len(shape))
    chosen = pl.BlockSpec((1, lat_count, wave_count), lambda i, p: (p[0], 0, 0))
    return pl.pallas_call(
        analysis_kernel,
        out_shape=jax.ShapeDtypeStruct(control.shape, F32),
        grid_spec=pltpu.PrefetchScalarGridSpec(
            num_scalar_prefetch=1,
            grid=(1,),
            in_specs=[
                whole(arrived.shape),
                whole(control.shape),
                whole(sigma.shape),
                chosen,
                chosen,
            ],
            out_specs=whole(control.shape),
            scratch_shapes=[pltpu.VMEM(arrived.shape, F32)],
        ),
        cost_estimate=pl.CostEstimate(flops=400_000_000, bytes_accessed=2_000_000, transcendentals=0),
        compiler_params=pltpu.CompilerParams(vmem_limit_bytes=12 * MIB),
        name="analysis",
    )(parity, arrived, control, sigma, *table)


def shards(
    control,
    spec_sigma,
    prior_mean_field,
    magnitude_factor,
    w_in,
    w_out,
    obs_band,
    obs_cell,
    obs_value,
    obs_weight,
    obs_offset,
):
    channels, _, _, wave_count = control.shape
    lat_count = BANDS * TPS
    lon_count = prior_mean_field.shape[2]
    legendre = legendre_np(wave_count, lat_count)
    zonal = zonal_np(lat_count, lon_count)
    turns = turn_np(lat_count, lon_count)
    parity = (lax.axis_index("tp") % 2).astype(jnp.int32).reshape(1)

    send = synthesis(parity, control, spec_sigma, w_in, w_out.T, legendre)
    got = lax.all_to_all(send, "tp", split_axis=0, concat_axis=0, tiled=True)
    obs = pack_obs(
        *(
            field.reshape(-1, LANES)
            for field in (obs_band, obs_cell, obs_value, obs_weight, obs_offset)
        )
    )
    send = regroup(got, obs).reshape(BANDS, 16, LANES)
    arrived = lax.all_to_all(send, "band", split_axis=0, concat_axis=0, tiled=True)
    weights = gather_weights(got)
    prior = jnp.pad(prior_mean_field[:, 0, :], ((0, ROWS - channels), (0, 0)))
    prior = jnp.concatenate([prior, prior[:, : WIDTH - STRIDE]], axis=1)
    prior = jnp.stack([prior[:, a * STRIDE : a * STRIDE + WIDTH] for a in range(BLOCKS)])
    gains = jnp.broadcast_to(
        jnp.pad(magnitude_factor, (0, ROWS - channels))[:, None], (ROWS, WIDTH)
    )
    modes = run_cycle(channels, arrived, prior, gains, weights, zonal, turns)
    modes = lax.all_to_all(
        modes.reshape(lat_count, 2, LANES),
        ("band", "tp"),
        split_axis=0,
        concat_axis=0,
        tiled=True,
    )
    modes = modes.reshape(2 * lat_count, LANES)
    return analysis(parity, modes, control, spec_sigma, legendre)


def solution(mesh):
    placed = (
        P(None, None, ("band", "tp"), None),
        P(None, ("band", "tp"), None),
        P(None, ("band", "tp"), None),
        P(),
        P(None, "tp"),
        P("tp", None),
        P("band", "tp", None, None),
        P("band", "tp", None),
        P("band", "tp", None),
        P("band", "tp", None),
        P("band", "tp", None),
    )
    return jax.shard_map(
        shards,
        mesh=mesh,
        in_specs=placed,
        out_specs=P(None, None, ("band", "tp"), None),
        check_vma=False,
    )
```

```python
import math

import jax
import jax.numpy as jnp
import ml_dtypes
import numpy as np
from jax import lax
from jax.experimental import pallas as pl
from jax.experimental.pallas import tpu as pltpu
from jax.sharding import PartitionSpec as P

EPSILON = 1e-06
BF16 = jnp.bfloat16
F32 = jnp.float32

BLOCKS = 6
STRIDE = 240
WIDTH = 256
ROWS = 72
LANES = 128
BANDS = 64
TPS = 8
SLOTS = 64
FIELDS = 8
ROW_SHIFT = 256
OBS_CHUNK = 512
MIB = 1024 * 1024


def split_np(table):
    high = table.astype(np.float32).astype(ml_dtypes.bfloat16)
    low = (table - high.astype(np.float64)).astype(np.float32).astype(ml_dtypes.bfloat16)
    return high, low


def legendre_np(wave_count, lat_count):
    cycles = np.arange(lat_count)
    tables = []
    for parity in range(2):
        frequency = np.arange(wave_count) + parity
        phases = (2 * cycles[:, None] + 1) * frequency[None, :] % (4 * lat_count)
        angles = phases * (math.pi / (2 * lat_count))
        basis = np.sin(angles) if parity else np.cos(angles)
        tables.append(basis * math.sqrt(2.0 / lat_count))
    return split_np(np.stack(tables))


def zonal_np(orders, lon_count):
    phases = np.arange(orders)[:, None] * np.arange(WIDTH)[None, :] % lon_count
    angles = phases * (2.0 * math.pi / lon_count)
    high, low = split_np(np.concatenate([np.cos(angles), np.sin(angles)], axis=0))
    return high, low, np.ascontiguousarray(high.T), np.ascontiguousarray(low.T)


def turn_np(orders, lon_count):
    phases = np.arange(BLOCKS)[:, None] * STRIDE * np.arange(orders)[None, :] % lon_count
    angles = phases * (2.0 * math.pi / lon_count)
    pad = np.zeros((8 - BLOCKS, orders))
    return np.concatenate([np.cos(angles), pad, np.sin(angles), pad]).astype(np.float32)


def split(values):
    high = values.astype(BF16)
    low = (values - high.astype(F32)).astype(BF16)
    return high, low


NN = (((1,), (0,)), ((), ()))
NT = (((1,), (1,)), ((), ()))


def dot(left, right, dims=NN):
    return lax.dot_general(left, right, dims, preferred_element_type=F32)


def dot3(left, right, dims=NN):
    return (
        dot(left[0], right[0], dims) + dot(left[0], right[1], dims) + dot(left[1], right[0], dims)
    )


def lane_ids(shape):
    return lax.broadcasted_iota(jnp.int32, shape, len(shape) - 1)


SEND_ROWS = 144
REST_LANE = 96


def synthesis_kernel(
    control_hbm,
    sigma_hbm,
    high_hbm,
    low_hbm,
    shard,
    out,
    control,
    sigma,
    table_high,
    table_low,
    coef,
    modes,
    arrivals,
):
    parity = lax.rem(lax.axis_index("tp"), 2)
    copies = [
        pltpu.make_async_copy(source, target, arrivals.at[i])
        for i, (source, target) in enumerate(
            (
                (control_hbm, control),
                (sigma_hbm, sigma),
                (high_hbm.at[parity], table_high),
                (low_hbm.at[parity], table_low),
            )
        )
    ]
    for copy in copies:
        copy.start()
    channels = sigma.shape[0]
    coef[...] = jnp.zeros_like(coef)
    copies[0].wait()
    copies[1].wait()
    deviation = sigma[:, 0, :]
    first = deviation * control[:, 0, 0, :]
    second = deviation * control[:, 1, 0, :]
    coef[0:channels, :] = first
    coef[ROWS:LANES, :] = second[: LANES - ROWS]
    tail = channels - (LANES - ROWS)
    coef[LANES + REST_LANE : LANES + REST_LANE + tail, :] = second[LANES - ROWS :]
    parts = split(coef[...])
    copies[2].wait()
    copies[3].wait()
    whole = dot3((table_high[...], table_low[...]), parts, NT)
    modes[0] = whole[:, 0:LANES]
    modes[1] = whole[:, LANES:]
    rows = shard[...].astype(F32)
    for dest in range(TPS):
        out[dest, 0:BANDS, :] = modes[0, pl.ds(dest, BANDS, stride=TPS), :].astype(BF16)
        rest = modes[1, pl.ds(dest, BANDS, stride=TPS), :]
        out[dest, BANDS : 2 * BANDS, :] = (rest + rows[0:BANDS]).astype(BF16)
        out[dest, 2 * BANDS : SEND_ROWS, :] = rows[BANDS:].astype(BF16)


IN_VMEM = pl.BlockSpec(memory_space=pltpu.VMEM)
IN_HBM = pl.BlockSpec(memory_space=pltpu.HBM)


def synthesis(control, sigma, shard, table):
    lat_count, wave_count = table[0].shape[1:]
    return pl.pallas_call(
        synthesis_kernel,
        out_shape=jax.ShapeDtypeStruct((TPS, SEND_ROWS, LANES), BF16),
        in_specs=[IN_HBM] * 4 + [IN_VMEM],
        out_specs=IN_VMEM,
        scratch_shapes=[
            pltpu.VMEM(control.shape, F32),
            pltpu.VMEM(sigma.shape, F32),
            pltpu.VMEM((lat_count, wave_count), BF16),
            pltpu.VMEM((lat_count, wave_count), BF16),
            pltpu.VMEM((2 * LANES, wave_count), F32),
            pltpu.VMEM((2, lat_count, LANES), F32),
            pltpu.SemaphoreType.DMA((4,)),
        ],
        cost_estimate=pl.CostEstimate(flops=400_000_000, bytes_accessed=2_000_000, transcendentals=0),
        compiler_params=pltpu.CompilerParams(vmem_limit_bytes=12 * MIB),
        name="synthesis",
    )(control, sigma, *table, shard)


def pack_kernel(band, cell, value, weight, offset, out):
    blocks = band.shape[0]
    cells = cell[...].astype(F32)
    channel = jnp.floor((cells + 0.5) * (1.0 / 1440.0))
    start = cells - 1440.0 * channel - 1.0
    start = jnp.where(start < 0.0, start + 1440.0, start)
    part = jnp.floor((start + 0.5) * (1.0 / STRIDE))
    fields = []
    for source in (value, weight, offset):
        high = source[...].astype(BF16).astype(F32)
        fields += [high, source[...] - high]
    fields += [part * ROWS + channel - ROW_SHIFT, start - part * STRIDE]
    band_ids = lax.broadcasted_iota(jnp.int32, (BANDS, LANES), 0)
    hits = [band_ids == band[i : i + 1, :] for i in range(blocks)]
    ones = [jnp.where(hit, 1.0, 0.0) for hit in hits]
    square = (LANES, 2 * LANES)
    row, column = lax.broadcasted_iota(jnp.int32, square, 0), lane_ids(square)
    before = jnp.where((row < column) | (column >= LANES), 1.0, 0.0).astype(BF16)
    counts = dot(jnp.concatenate(ones, axis=0).astype(BF16), before)
    slot_ids = lax.broadcasted_iota(jnp.int32, (LANES, LANES), 0).astype(F32)
    taken = jnp.zeros((BANDS, LANES), F32)
    total = jnp.zeros((BANDS, FIELDS * LANES), F32)
    for i in range(blocks):
        within = counts[i * BANDS : (i + 1) * BANDS, :]
        rank = jnp.sum(ones[i] * (within[:, :LANES] + taken), axis=0, keepdims=True)
        taken = taken + within[:, LANES:]
        here = slot_ids == rank + (LANES - SLOTS)
        spread = [jnp.where(here, field[i : i + 1, :], 0.0).astype(BF16) for field in fields]
        total = total + dot(ones[i].astype(BF16), jnp.concatenate(spread, axis=0), NT)
    out[...] = total


def pack_obs(band, cell, value, weight, offset):
    return pl.pallas_call(
        pack_kernel,
        out_shape=jax.ShapeDtypeStruct((BANDS, FIELDS * LANES), F32),
        cost_estimate=pl.CostEstimate(flops=200_000_000, bytes_accessed=300_000, transcendentals=0),
        compiler_params=pltpu.CompilerParams(vmem_limit_bytes=8 * MIB),
        name="pack_obs",
    )(band, cell, value, weight, offset)


def regroup_kernel(arrived, obs, out, rows):
    lanes = lane_ids((BANDS, LANES))
    for t in range(TPS):
        rows[pl.ds(t, BANDS, stride=16), :] = arrived[t, 0:BANDS, :].astype(F32)
        rest = pltpu.roll(arrived[t, BANDS : 2 * BANDS, :].astype(F32), LANES - REST_LANE, 1)
        rest = jnp.where(lanes < 16, rest, obs[:, t * LANES : (t + 1) * LANES])
        rows[pl.ds(8 + t, BANDS, stride=16), :] = rest
    out[...] = rows[...].astype(BF16)


def regroup(arrived, obs):
    return pl.pallas_call(
        regroup_kernel,
        out_shape=jax.ShapeDtypeStruct((BANDS * 16, LANES), BF16),
        scratch_shapes=[pltpu.VMEM((BANDS * 16, LANES), F32)],
        cost_estimate=pl.CostEstimate(flops=300_000, bytes_accessed=800_000, transcendentals=0),
        compiler_params=pltpu.CompilerParams(vmem_limit_bytes=8 * MIB),
        name="regroup",
    )(arrived, obs)


def weights_kernel(own, other, in_rows, in_columns, out_rows, out_columns):
    even = lax.rem(lax.axis_index("band"), 2) == 0
    for columns, rows, first in ((in_columns, in_rows, True), (out_columns, out_rows, False)):
        pieces = []
        for t in range(TPS):
            mine = own[t, BANDS:SEND_ROWS, :].astype(F32)
            theirs = other[t, BANDS:SEND_ROWS, :].astype(F32)
            piece = jnp.where(even == first, mine, theirs)
            piece = jnp.concatenate([piece, jnp.zeros((LANES - 80, LANES), F32)], axis=0)
            pieces.append(piece.T[0:96])
        upright = jnp.concatenate(pieces, axis=0)
        columns[...] = upright.astype(BF16)
        rows[...] = upright.T[0:80].astype(BF16)


def gather_weights(own, other):
    hidden = TPS * 96
    return pl.pallas_call(
        weights_kernel,
        out_shape=(
            jax.ShapeDtypeStruct((80, hidden), BF16),
            jax.ShapeDtypeStruct((hidden, LANES), BF16),
            jax.ShapeDtypeStruct((80, hidden), BF16),
            jax.ShapeDtypeStruct((hidden, LANES), BF16),
        ),
        cost_estimate=pl.CostEstimate(flops=1_000_000, bytes_accessed=1_500_000, transcendentals=0),
        compiler_params=pltpu.CompilerParams(vmem_limit_bytes=8 * MIB),
        name="weights",
    )(own, other)


GELU_SCALE = math.sqrt(2.0 / math.pi)
GELU_CUBE = 0.044715


def lagrange_rows(offset):
    return (
        -offset * (offset - 1.0) * (offset - 2.0) / 6.0,
        (offset + 1.0) * (offset - 1.0) * (offset - 2.0) / 2.0,
        -(offset + 1.0) * offset * (offset - 2.0) / 2.0,
        (offset + 1.0) * offset * (offset - 1.0) / 6.0,
    )


def cycle_kernel(
    channels,
    arrived,
    prior,
    gains,
    in_rows,
    in_columns,
    out_rows,
    out_columns,
    turns,
    table_high_hbm,
    table_low_hbm,
    wide_high_hbm,
    wide_low_hbm,
    out,
    table_high,
    table_low,
    wide_high,
    wide_low,
    arrivals,
    state,
    slopes,
    obs,
    chosen_all,
    spread_all,
    paired,
):
    orders = turns.shape[1]
    copies = [
        pltpu.make_async_copy(source, target, arrivals.at[i])
        for i, (source, target) in enumerate(
            (
                (table_high_hbm, table_high),
                (table_low_hbm, table_low),
                (wide_high_hbm, wide_high),
                (wide_low_hbm, wide_low),
            )
        )
    ]
    for copy in copies:
        copy.start()
    slices = arrived[...].astype(F32)
    rest = slices[:, 8:16, :]
    cos_sin = slices[:, 0:8, :].reshape(orders, LANES).T
    tail = rest.reshape(orders, LANES).T
    cos_part = cos_sin[0:ROWS]
    sin_part = jnp.concatenate([cos_sin[ROWS:LANES], tail[0:16]], axis=0)
    pairs = rest.reshape(BANDS // 2, 2, FIELDS, LANES)
    near = pltpu.roll(pairs[:, 0].reshape(BANDS // 2 * FIELDS, LANES), LANES - SLOTS, 1)
    near = near.reshape(BANDS // 2, FIELDS, LANES)
    obs[...] = jnp.where(lane_ids(near.shape) < SLOTS, near, pairs[:, 1])

    turned = []
    for a in range(BLOCKS):
        turn_cos, turn_sin = turns[a : a + 1, :], turns[8 + a : 9 + a, :]
        turned_cos = cos_part * turn_cos + sin_part * turn_sin
        turned_sin = sin_part * turn_cos - cos_part * turn_sin
        turned.append(jnp.concatenate([turned_cos, turned_sin], axis=1))
    turned = split(jnp.concatenate(turned, axis=0))
    copies[0].wait()
    copies[1].wait()
    state[...] = prior[...].reshape(BLOCKS * ROWS, WIDTH) + dot3(
        turned, (table_high[...], table_low[...])
    )

    forecast = []
    for a in range(BLOCKS):
        field = state[a * ROWS : (a + 1) * ROWS, :]
        mean_sq = jnp.sum(field * field, axis=0, keepdims=True) * (1.0 / channels)
        unit = (field * gains[...] * lax.rsqrt(mean_sq + EPSILON)).astype(BF16)
        pre = dot(in_columns[:, 0:ROWS], unit)
        square = pre * pre
        inner = pre * (GELU_SCALE + (GELU_SCALE * GELU_CUBE) * square)
        half = 0.5 + 0.5 * jnp.tanh(inner)
        hidden = pre * half
        slopes[a] = half + hidden * (1.0 - half) * (
            2.0 * GELU_SCALE + (6.0 * GELU_SCALE * GELU_CUBE) * square
        )
        forecast.append(field + dot(out_rows[...], hidden.astype(BF16))[0:ROWS])
    forecast = split(jnp.concatenate(forecast, axis=0).T)
    forecast = jnp.concatenate(forecast, axis=0)

    per_chunk = OBS_CHUNK // LANES
    low_ids = lax.broadcasted_iota(jnp.int32, (16, OBS_CHUNK), 0).astype(F32)
    near_ids = lax.broadcasted_iota(jnp.int32, (32, OBS_CHUNK), 0).astype(F32)
    none = jnp.zeros((16, OBS_CHUNK), BF16)
    for chunk in range(obs.shape[0] // per_chunk):
        fields = [obs[chunk * per_chunk + i] for i in range(per_chunk)]
        fields = jnp.concatenate(fields, axis=1)
        value = fields[0:1] + fields[1:2]
        weight = fields[2:3] + fields[3:4]
        offset = fields[4:5] + fields[5:6]
        row = fields[6:7] + float(ROW_SHIFT)
        row_group = jnp.floor(row * (1.0 / 16.0))
        first = jnp.where(low_ids == row - 16.0 * row_group, 1.0, 0.0).astype(BF16)
        row_group = jnp.broadcast_to(row_group, (16, OBS_CHUNK)).astype(BF16)
        chosen = jnp.concatenate(
            [
                jnp.where(row_group == jnp.array(float(g), BF16), first, none)
                for g in range(BLOCKS * ROWS // 16)
            ],
            axis=0,
        )
        columns = slice(chunk * OBS_CHUNK, (chunk + 1) * OBS_CHUNK)
        chosen_all[:, columns] = chosen
        picked = dot(forecast, chosen)
        group = jnp.floor(fields[7:8] * (1.0 / 16.0))
        place = near_ids - (fields[7:8] - 16.0 * group)
        group8 = jnp.broadcast_to(group, (8, OBS_CHUNK))
        window = [jnp.zeros((8, OBS_CHUNK), F32)] * 4
        for g in range(WIDTH // 16 - 1):
            mask = group8 == float(g)
            for i in range(4):
                rows = slice(16 * g + 8 * i, 16 * g + 8 * i + 8)
                window[i] = jnp.where(mask, picked[rows] + picked[WIDTH:][rows], window[i])
        window = jnp.concatenate(window, axis=0)
        w_left, w_here, w_right, w_far = lagrange_rows(offset)
        stencil = jnp.where(
            place == 0.0,
            w_left,
            jnp.where(
                place == 1.0,
                w_here,
                jnp.where(place == 2.0, w_right, jnp.where(place == 3.0, w_far, 0.0)),
            ),
        )
        reading = jnp.sum(stencil * window, axis=0, keepdims=True)
        parts = split(stencil * (weight * (reading - value)))
        group = jnp.broadcast_to(group, (16, OBS_CHUNK)).astype(BF16)
        masks = [group == jnp.array(float(g), BF16) for g in range(WIDTH // 16 - 1)]
        for i, part in enumerate(parts):
            pieces = []
            for g in range(WIDTH // 16):
                piece = none
                if g > 0:
                    piece = jnp.where(masks[g - 1], part[16:32], piece)
                if g < WIDTH // 16 - 1:
                    piece = jnp.where(masks[g], part[0:16], piece)
                pieces.append(piece)
            spread_all[i * WIDTH : (i + 1) * WIDTH, columns] = jnp.concatenate(pieces, axis=0)
    forcing = dot(spread_all[...], chosen_all[...], NT)
    forcing = (forcing[0:WIDTH] + forcing[WIDTH:]).T

    lanes = lane_ids((BLOCKS * ROWS, WIDTH))
    halo = pltpu.roll(forcing, WIDTH - STRIDE, 1)
    halo = jnp.concatenate([halo[(BLOCKS - 1) * ROWS :], halo[: (BLOCKS - 1) * ROWS]], axis=0)
    forcing = jnp.where(lanes < STRIDE, forcing, 0.0) + jnp.where(lanes < 3, halo, 0.0)
    costate = []
    for a in range(BLOCKS):
        force = forcing[a * ROWS : (a + 1) * ROWS]
        grad_hidden = dot(out_columns[:, 0:ROWS], force.astype(BF16))
        grad_pre = (grad_hidden * slopes[a]).astype(BF16)
        grad_unit = dot(in_rows[...], grad_pre)[0:ROWS]
        field = state[a * ROWS : (a + 1) * ROWS, :]
        mean_sq = jnp.sum(field * field, axis=0, keepdims=True) * (1.0 / channels)
        inverse = lax.rsqrt(mean_sq + EPSILON)
        scaled = grad_unit * gains[...]
        along = jnp.sum(scaled * field, axis=0, keepdims=True) * (1.0 / channels)
        costate.append(force + scaled * inverse - field * (along * inverse * inverse * inverse))
    costate = split(jnp.concatenate(costate, axis=0))
    copies[2].wait()
    copies[3].wait()
    blocks = dot3(costate, (wide_high[...], wide_low[...]))
    grad_cos = jnp.zeros((ROWS, orders), F32)
    grad_sin = jnp.zeros((ROWS, orders), F32)
    for a in range(BLOCKS):
        turn_cos, turn_sin = turns[a : a + 1, :], turns[8 + a : 9 + a, :]
        block = blocks[a * ROWS : (a + 1) * ROWS]
        block_cos, block_sin = block[:, 0:orders], block[:, orders:]
        grad_cos = grad_cos + turn_cos * block_cos - turn_sin * block_sin
        grad_sin = grad_sin + turn_sin * block_cos + turn_cos * block_sin

    lanes = lane_ids((orders, LANES))
    pad = jnp.zeros((LANES - ROWS, orders), F32)
    for r, grad in ((0, grad_cos), (1, grad_sin)):
        upright = jnp.concatenate([grad, pad], axis=0).T
        high = upright.astype(BF16).astype(F32)
        low = pltpu.roll(upright - high, channels, 1)
        paired[pl.ds(r, orders, stride=2), :] = jnp.where(lanes < channels, high, low)
    out[...] = paired[...].astype(BF16)


def run_cycle(channels, arrived, prior, gains, weights, table, turns):
    orders = turns.shape[1]
    hidden = weights[1].shape[0]
    return pl.pallas_call(
        lambda *refs: cycle_kernel(channels, *refs),
        out_shape=jax.ShapeDtypeStruct((2 * orders, LANES), BF16),
        in_specs=[IN_VMEM] * 8 + [IN_HBM] * 4,
        out_specs=IN_VMEM,
        scratch_shapes=[
            *(pltpu.VMEM(part.shape, BF16) for part in table),
            pltpu.SemaphoreType.DMA((4,)),
            pltpu.VMEM((BLOCKS * ROWS, WIDTH), F32),
            pltpu.VMEM((BLOCKS, hidden, WIDTH), F32),
            pltpu.VMEM((BANDS // 2, FIELDS, LANES), F32),
            pltpu.VMEM((BLOCKS * ROWS, BANDS * SLOTS), BF16),
            pltpu.VMEM((2 * WIDTH, BANDS * SLOTS), BF16),
            pltpu.VMEM((2 * orders, LANES), F32),
        ],
        compiler_params=pltpu.CompilerParams(vmem_limit_bytes=36 * MIB),
        cost_estimate=pl.CostEstimate(
            flops=8_000_000_000, bytes_accessed=4_000_000, transcendentals=1_200_000
        ),
        name="cycle",
    )(arrived, prior, gains, *weights, turns, *table)


def analysis_kernel(parity, arrived, control, sigma, table_high, table_low, out, rows):
    channels = sigma.shape[0]
    orders = arrived.shape[0] // 2
    rows[...] = arrived[...].astype(F32)
    lanes = lane_ids((orders, LANES))
    for r in range(2):
        both = rows[pl.ds(r, orders, stride=2), :]
        low = pltpu.roll(both, LANES - channels, 1)
        grad = jnp.where(lanes < channels, both, 0.0)
        grad = grad + jnp.where(lanes < LANES - channels, low, 0.0)
        grad_t = split(grad.T[0:ROWS])
        projected = dot3(grad_t, (table_high[0], table_low[0]))
        out[:, r, 0, :] = control[:, r, 0, :] + sigma[:, 0, :] * projected[0:channels]


def analysis(parity, arrived, control, sigma, table):
    wave_count = table[0].shape[2]
    lat_count = table[0].shape[1]
    whole = lambda shape: pl.BlockSpec(shape, lambda i, p: (0,) * len(shape))
    chosen = pl.BlockSpec((1, lat_count, wave_count), lambda i, p: (p[0], 0, 0))
    return pl.pallas_call(
        analysis_kernel,
        out_shape=jax.ShapeDtypeStruct(control.shape, F32),
        grid_spec=pltpu.PrefetchScalarGridSpec(
            num_scalar_prefetch=1,
            grid=(1,),
            in_specs=[
                whole(arrived.shape),
                whole(control.shape),
                whole(sigma.shape),
                chosen,
                chosen,
            ],
            out_specs=whole(control.shape),
            scratch_shapes=[pltpu.VMEM(arrived.shape, F32)],
        ),
        cost_estimate=pl.CostEstimate(flops=400_000_000, bytes_accessed=2_000_000, transcendentals=0),
        compiler_params=pltpu.CompilerParams(vmem_limit_bytes=12 * MIB),
        name="analysis",
    )(parity, arrived, control, sigma, *table)


def shards(
    control,
    spec_sigma,
    prior_mean_field,
    magnitude_factor,
    w_in,
    w_out,
    obs_band,
    obs_cell,
    obs_value,
    obs_weight,
    obs_offset,
):
    channels, _, _, wave_count = control.shape
    lat_count = BANDS * TPS
    lon_count = prior_mean_field.shape[2]
    legendre = legendre_np(wave_count, lat_count)
    zonal = zonal_np(lat_count, lon_count)
    turns = turn_np(lat_count, lon_count)
    parity = (lax.axis_index("tp") % 2).astype(jnp.int32).reshape(1)
    even = lax.axis_index("band") % 2 == 0
    pads = ((0, 80 - channels), (0, LANES - w_in.shape[1]))
    shard = jnp.pad(jnp.where(even, w_in, w_out.T), pads)
    send = synthesis(control, spec_sigma, shard, legendre)
    got = lax.all_to_all(send, "tp", split_axis=0, concat_axis=0, tiled=True)
    obs = pack_obs(
        *(
            field.reshape(-1, LANES)
            for field in (obs_band, obs_cell, obs_value, obs_weight, obs_offset)
        )
    )
    send = regroup(got, obs).reshape(BANDS, 16, LANES)
    arrived = lax.all_to_all(send, "band", split_axis=0, concat_axis=0, tiled=True)
    other = lax.ppermute(got, "band", [(i, i ^ 1) for i in range(BANDS)])
    weights = gather_weights(got, other)
    prior = jnp.pad(prior_mean_field[:, 0, :], ((0, ROWS - channels), (0, 0)))
    prior = jnp.concatenate([prior, prior[:, : WIDTH - STRIDE]], axis=1)
    prior = jnp.stack([prior[:, a * STRIDE : a * STRIDE + WIDTH] for a in range(BLOCKS)])
    gains = jnp.broadcast_to(
        jnp.pad(magnitude_factor, (0, ROWS - channels))[:, None], (ROWS, WIDTH)
    )
    modes = run_cycle(channels, arrived, prior, gains, weights, zonal, turns)
    modes = lax.all_to_all(
        modes.reshape(lat_count, 2, LANES),
        ("band", "tp"),
        split_axis=0,
        concat_axis=0,
        tiled=True,
    )
    modes = modes.reshape(2 * lat_count, LANES)
    return analysis(parity, modes, control, spec_sigma, legendre)


def solution(mesh):
    placed = (
        P(None, None, ("band", "tp"), None),
        P(None, ("band", "tp"), None),
        P(None, ("band", "tp"), None),
        P(),
        P(None, "tp"),
        P("tp", None),
        P("band", "tp", None, None),
        P("band", "tp", None),
        P("band", "tp", None),
        P("band", "tp", None),
        P("band", "tp", None),
    )
    return jax.shard_map(
        shards,
        mesh=mesh,
        in_specs=placed,
        out_specs=P(None, None, ("band", "tp"), None),
        check_vma=False,
    )
```

```python
import math

import jax
import jax.numpy as jnp
import ml_dtypes
import numpy as np
from jax import lax
from jax.experimental import pallas as pl
from jax.experimental.pallas import tpu as pltpu
from jax.sharding import PartitionSpec as P

EPSILON = 1e-06
BF16 = jnp.bfloat16
F32 = jnp.float32

BLOCKS = 6
STRIDE = 240
WIDTH = 256
ROWS = 72
LANES = 128
BANDS = 64
TPS = 8
SLOTS = 64
FIELDS = 8
ROW_SHIFT = 256
OBS_CHUNK = 512
MIB = 1024 * 1024


def split_np(table):
    high = table.astype(np.float32).astype(ml_dtypes.bfloat16)
    low = (table - high.astype(np.float64)).astype(np.float32).astype(ml_dtypes.bfloat16)
    return high, low


def legendre_np(wave_count, lat_count):
    cycles = np.arange(lat_count)
    tables = []
    for parity in range(2):
        frequency = np.arange(wave_count) + parity
        phases = (2 * cycles[:, None] + 1) * frequency[None, :] % (4 * lat_count)
        angles = phases * (math.pi / (2 * lat_count))
        basis = np.sin(angles) if parity else np.cos(angles)
        tables.append(basis * math.sqrt(2.0 / lat_count))
    return split_np(np.stack(tables))


def zonal_np(orders, lon_count):
    phases = np.arange(orders)[:, None] * np.arange(WIDTH)[None, :] % lon_count
    angles = phases * (2.0 * math.pi / lon_count)
    high, low = split_np(np.concatenate([np.cos(angles), np.sin(angles)], axis=0))
    return high, low, np.ascontiguousarray(high.T), np.ascontiguousarray(low.T)


def turn_np(orders, lon_count):
    phases = np.arange(BLOCKS)[:, None] * STRIDE * np.arange(orders)[None, :] % lon_count
    angles = phases * (2.0 * math.pi / lon_count)
    pad = np.zeros((8 - BLOCKS, orders))
    return np.concatenate([np.cos(angles), pad, np.sin(angles), pad]).astype(np.float32)


def split(values):
    high = values.astype(BF16)
    low = (values - high.astype(F32)).astype(BF16)
    return high, low


NN = (((1,), (0,)), ((), ()))
NT = (((1,), (1,)), ((), ()))


def dot(left, right, dims=NN):
    return lax.dot_general(left, right, dims, preferred_element_type=F32)


def dot3(left, right, dims=NN):
    return (
        dot(left[0], right[0], dims) + dot(left[0], right[1], dims) + dot(left[1], right[0], dims)
    )


def lane_ids(shape):
    return lax.broadcasted_iota(jnp.int32, shape, len(shape) - 1)


SEND_ROWS = 144
REST_LANE = 96


def synthesis_kernel(
    control_hbm,
    sigma_hbm,
    high_hbm,
    low_hbm,
    w_in_hbm,
    w_out_hbm,
    out,
    control,
    sigma,
    table_high,
    table_low,
    w_in,
    w_out,
    coef,
    modes,
    arrivals,
):
    parity = lax.rem(lax.axis_index("tp"), 2)
    copies = [
        pltpu.make_async_copy(source, target, arrivals.at[i])
        for i, (source, target) in enumerate(
            (
                (control_hbm, control),
                (sigma_hbm, sigma),
                (high_hbm.at[parity], table_high),
                (low_hbm.at[parity], table_low),
                (w_in_hbm, w_in),
                (w_out_hbm, w_out),
            )
        )
    ]
    for copy in copies:
        copy.start()
    channels = sigma.shape[0]
    coef[...] = jnp.zeros_like(coef)
    copies[0].wait()
    copies[1].wait()
    deviation = sigma[:, 0, :]
    first = deviation * control[:, 0, 0, :]
    second = deviation * control[:, 1, 0, :]
    coef[0:channels, :] = first
    coef[ROWS:LANES, :] = second[: LANES - ROWS]
    tail = channels - (LANES - ROWS)
    coef[LANES + REST_LANE : LANES + REST_LANE + tail, :] = second[LANES - ROWS :]
    parts = split(coef[...])
    for copy in copies[2:]:
        copy.wait()
    whole = dot3((table_high[...], table_low[...]), parts, NT)
    modes[0] = whole[:, 0:LANES]
    modes[1] = whole[:, LANES:]
    even = lax.rem(lax.axis_index("band"), 2) == 0
    rows = jnp.where(even, w_in[...].astype(F32), w_out[...].astype(F32))
    rows = jnp.pad(rows, ((0, 80 - channels), (0, LANES - rows.shape[1])))
    for dest in range(TPS):
        out[dest, 0:BANDS, :] = modes[0, pl.ds(dest, BANDS, stride=TPS), :].astype(BF16)
        rest = modes[1, pl.ds(dest, BANDS, stride=TPS), :]
        out[dest, BANDS : 2 * BANDS, :] = (rest + rows[0:BANDS]).astype(BF16)
        out[dest, 2 * BANDS : SEND_ROWS, :] = rows[BANDS:].astype(BF16)


def in_hbm(*arrays):
    return tuple(pltpu.with_memory_space_constraint(jnp.asarray(a), pltpu.HBM) for a in arrays)


IN_VMEM = pl.BlockSpec(memory_space=pltpu.VMEM)
IN_HBM = pl.BlockSpec(memory_space=pltpu.HBM)


def synthesis(control, sigma, w_in, w_out_t, table):
    lat_count, wave_count = table[0].shape[1:]
    return pl.pallas_call(
        synthesis_kernel,
        out_shape=jax.ShapeDtypeStruct((TPS, SEND_ROWS, LANES), BF16),
        in_specs=[IN_HBM] * 6,
        out_specs=IN_VMEM,
        scratch_shapes=[
            pltpu.VMEM(control.shape, F32),
            pltpu.VMEM(sigma.shape, F32),
            pltpu.VMEM((lat_count, wave_count), BF16),
            pltpu.VMEM((lat_count, wave_count), BF16),
            pltpu.VMEM(w_in.shape, BF16),
            pltpu.VMEM(w_in.shape, BF16),
            pltpu.VMEM((2 * LANES, wave_count), F32),
            pltpu.VMEM((2, lat_count, LANES), F32),
            pltpu.SemaphoreType.DMA((6,)),
        ],
        cost_estimate=pl.CostEstimate(flops=400_000_000, bytes_accessed=2_000_000, transcendentals=0),
        compiler_params=pltpu.CompilerParams(vmem_limit_bytes=12 * MIB),
        name="synthesis",
    )(*in_hbm(control, sigma, *table, w_in, w_out_t))


def pack_kernel(band, cell, value, weight, offset, out):
    blocks = band.shape[0]
    cells = cell[...].astype(F32)
    channel = jnp.floor((cells + 0.5) * (1.0 / 1440.0))
    start = cells - 1440.0 * channel - 1.0
    start = jnp.where(start < 0.0, start + 1440.0, start)
    part = jnp.floor((start + 0.5) * (1.0 / STRIDE))
    fields = []
    for source in (value, weight, offset):
        high = source[...].astype(BF16).astype(F32)
        fields += [high, source[...] - high]
    fields += [part * ROWS + channel - ROW_SHIFT, start - part * STRIDE]
    band_ids = lax.broadcasted_iota(jnp.int32, (BANDS, LANES), 0)
    hits = [band_ids == band[i : i + 1, :] for i in range(blocks)]
    ones = [jnp.where(hit, 1.0, 0.0) for hit in hits]
    square = (LANES, 2 * LANES)
    row, column = lax.broadcasted_iota(jnp.int32, square, 0), lane_ids(square)
    before = jnp.where((row < column) | (column >= LANES), 1.0, 0.0).astype(BF16)
    counts = dot(jnp.concatenate(ones, axis=0).astype(BF16), before)
    slot_ids = lax.broadcasted_iota(jnp.int32, (LANES, LANES), 0).astype(F32)
    taken = jnp.zeros((BANDS, LANES), F32)
    total = jnp.zeros((BANDS, FIELDS * LANES), F32)
    for i in range(blocks):
        within = counts[i * BANDS : (i + 1) * BANDS, :]
        rank = jnp.sum(ones[i] * (within[:, :LANES] + taken), axis=0, keepdims=True)
        taken = taken + within[:, LANES:]
        here = slot_ids == rank + (LANES - SLOTS)
        spread = [jnp.where(here, field[i : i + 1, :], 0.0).astype(BF16) for field in fields]
        total = total + dot(ones[i].astype(BF16), jnp.concatenate(spread, axis=0), NT)
    out[...] = total


def pack_obs(band, cell, value, weight, offset):
    return pl.pallas_call(
        pack_kernel,
        out_shape=jax.ShapeDtypeStruct((BANDS, FIELDS * LANES), F32),
        cost_estimate=pl.CostEstimate(flops=200_000_000, bytes_accessed=300_000, transcendentals=0),
        compiler_params=pltpu.CompilerParams(vmem_limit_bytes=8 * MIB),
        name="pack_obs",
    )(band, cell, value, weight, offset)


def regroup_kernel(arrived, obs, out, rows):
    lanes = lane_ids((BANDS, LANES))
    for t in range(TPS):
        rows[pl.ds(t, BANDS, stride=16), :] = arrived[t, 0:BANDS, :].astype(F32)
        rest = pltpu.roll(arrived[t, BANDS : 2 * BANDS, :].astype(F32), LANES - REST_LANE, 1)
        rest = jnp.where(lanes < 16, rest, obs[:, t * LANES : (t + 1) * LANES])
        rows[pl.ds(8 + t, BANDS, stride=16), :] = rest
    out[...] = rows[...].astype(BF16)


def regroup(arrived, obs):
    return pl.pallas_call(
        regroup_kernel,
        out_shape=jax.ShapeDtypeStruct((BANDS * 16, LANES), BF16),
        scratch_shapes=[pltpu.VMEM((BANDS * 16, LANES), F32)],
        cost_estimate=pl.CostEstimate(flops=300_000, bytes_accessed=800_000, transcendentals=0),
        compiler_params=pltpu.CompilerParams(vmem_limit_bytes=8 * MIB),
        name="regroup",
    )(arrived, obs)


def prepare_kernel(own, other, *refs):
    sources, (in_rows, in_columns, out_rows, out_columns, *targets), (arrivals,) = (
        refs[:1],
        refs[1:6],
        refs[6:],
    )
    copies = [
        pltpu.make_async_copy(source, target, arrivals.at[i])
        for i, (source, target) in enumerate(zip(sources, targets))
    ]
    for copy in copies:
        copy.start()
    even = lax.rem(lax.axis_index("band"), 2) == 0
    for columns, rows, first in ((in_columns, in_rows, True), (out_columns, out_rows, False)):
        pieces = []
        for t in range(TPS):
            mine = own[t, BANDS:SEND_ROWS, :].astype(F32)
            theirs = other[t, BANDS:SEND_ROWS, :].astype(F32)
            piece = jnp.where(even == first, mine, theirs)
            piece = jnp.concatenate([piece, jnp.zeros((LANES - 80, LANES), F32)], axis=0)
            pieces.append(piece.T[0:96])
        upright = jnp.concatenate(pieces, axis=0)
        columns[...] = upright.astype(BF16)
        rows[...] = upright.T[0:80].astype(BF16)
    for copy in copies:
        copy.wait()


def prepare(own, other, tables):
    hidden = TPS * 96
    return pl.pallas_call(
        prepare_kernel,
        out_shape=(
            jax.ShapeDtypeStruct((80, hidden), BF16),
            jax.ShapeDtypeStruct((hidden, LANES), BF16),
            jax.ShapeDtypeStruct((80, hidden), BF16),
            jax.ShapeDtypeStruct((hidden, LANES), BF16),
            *(jax.ShapeDtypeStruct(table.shape, table.dtype) for table in tables),
        ),
        in_specs=[IN_VMEM] * 2 + [IN_HBM],
        out_specs=[IN_VMEM] * 5,
        scratch_shapes=[pltpu.SemaphoreType.DMA((1,))],
        cost_estimate=pl.CostEstimate(flops=1_000_000, bytes_accessed=5_000_000, transcendentals=0),
        compiler_params=pltpu.CompilerParams(vmem_limit_bytes=8 * MIB),
        name="prepare",
    )(own, other, *in_hbm(*tables))


GELU_SCALE = math.sqrt(2.0 / math.pi)
GELU_CUBE = 0.044715


def lagrange_rows(offset):
    return (
        -offset * (offset - 1.0) * (offset - 2.0) / 6.0,
        (offset + 1.0) * (offset - 1.0) * (offset - 2.0) / 2.0,
        -(offset + 1.0) * offset * (offset - 2.0) / 2.0,
        (offset + 1.0) * offset * (offset - 1.0) / 6.0,
    )


def cycle_kernel(
    channels,
    arrived,
    prior,
    gains,
    in_rows,
    in_columns,
    out_rows,
    out_columns,
    turns,
    table_high_hbm,
    table_low_hbm,
    wide_high_hbm,
    wide_low_hbm,
    out,
    table_high,
    table_low,
    wide_high,
    wide_low,
    arrivals,
    state,
    slopes,
    obs,
    chosen_all,
    spread_all,
    paired,
):
    orders = turns.shape[1]
    copies = [
        pltpu.make_async_copy(table_high_hbm, table_high, arrivals.at[0]),
        pltpu.make_async_copy(table_low_hbm, table_low, arrivals.at[1]),
        pltpu.make_async_copy(wide_high_hbm, wide_high, arrivals.at[2]),
        pltpu.make_async_copy(wide_low_hbm, wide_low, arrivals.at[3]),
    ]
    for copy in copies:
        copy.start()
    slices = arrived[...].astype(F32)
    rest = slices[:, 8:16, :]
    cos_sin = slices[:, 0:8, :].reshape(orders, LANES).T
    tail = rest.reshape(orders, LANES).T
    cos_part = cos_sin[0:ROWS]
    sin_part = jnp.concatenate([cos_sin[ROWS:LANES], tail[0:16]], axis=0)
    pairs = rest.reshape(BANDS // 2, 2, FIELDS, LANES)
    near = pltpu.roll(pairs[:, 0].reshape(BANDS // 2 * FIELDS, LANES), LANES - SLOTS, 1)
    near = near.reshape(BANDS // 2, FIELDS, LANES)
    obs[...] = jnp.where(lane_ids(near.shape) < SLOTS, near, pairs[:, 1])

    turned = []
    for a in range(BLOCKS):
        turn_cos, turn_sin = turns[a : a + 1, :], turns[8 + a : 9 + a, :]
        turned_cos = cos_part * turn_cos + sin_part * turn_sin
        turned_sin = sin_part * turn_cos - cos_part * turn_sin
        turned.append(jnp.concatenate([turned_cos, turned_sin], axis=1))
    turned = split(jnp.concatenate(turned, axis=0))
    for copy in copies[:2]:
        copy.wait()
    state[...] = prior[...].reshape(BLOCKS * ROWS, WIDTH) + dot3(
        turned, (table_high[...], table_low[...])
    )

    forecast = []
    for a in range(BLOCKS):
        field = state[a * ROWS : (a + 1) * ROWS, :]
        mean_sq = jnp.sum(field * field, axis=0, keepdims=True) * (1.0 / channels)
        unit = (field * gains[...] * lax.rsqrt(mean_sq + EPSILON)).astype(BF16)
        pre = dot(in_columns[:, 0:ROWS], unit)
        square = pre * pre
        inner = pre * (GELU_SCALE + (GELU_SCALE * GELU_CUBE) * square)
        half = 0.5 + 0.5 * jnp.tanh(inner)
        hidden = pre * half
        slopes[a] = half + hidden * (1.0 - half) * (
            2.0 * GELU_SCALE + (6.0 * GELU_SCALE * GELU_CUBE) * square
        )
        forecast.append(field + dot(out_rows[...], hidden.astype(BF16))[0:ROWS])
    forecast = split(jnp.concatenate(forecast, axis=0).T)
    forecast = jnp.concatenate(forecast, axis=0)

    per_chunk = OBS_CHUNK // LANES
    low_ids = lax.broadcasted_iota(jnp.int32, (16, OBS_CHUNK), 0).astype(F32)
    near_ids = lax.broadcasted_iota(jnp.int32, (32, OBS_CHUNK), 0).astype(F32)
    none = jnp.zeros((16, OBS_CHUNK), BF16)
    for chunk in range(obs.shape[0] // per_chunk):
        fields = [obs[chunk * per_chunk + i] for i in range(per_chunk)]
        fields = jnp.concatenate(fields, axis=1)
        value = fields[0:1] + fields[1:2]
        weight = fields[2:3] + fields[3:4]
        offset = fields[4:5] + fields[5:6]
        row = fields[6:7] + float(ROW_SHIFT)
        row_group = jnp.floor(row * (1.0 / 16.0))
        first = jnp.where(low_ids == row - 16.0 * row_group, 1.0, 0.0).astype(BF16)
        row_group = jnp.broadcast_to(row_group, (16, OBS_CHUNK)).astype(BF16)
        chosen = jnp.concatenate(
            [
                jnp.where(row_group == jnp.array(float(g), BF16), first, none)
                for g in range(BLOCKS * ROWS // 16)
            ],
            axis=0,
        )
        columns = slice(chunk * OBS_CHUNK, (chunk + 1) * OBS_CHUNK)
        chosen_all[:, columns] = chosen
        picked = dot(forecast, chosen)
        group = jnp.floor(fields[7:8] * (1.0 / 16.0))
        place = near_ids - (fields[7:8] - 16.0 * group)
        group8 = jnp.broadcast_to(group, (8, OBS_CHUNK))
        window = [jnp.zeros((8, OBS_CHUNK), F32)] * 4
        for g in range(WIDTH // 16 - 1):
            mask = group8 == float(g)
            for i in range(4):
                rows = slice(16 * g + 8 * i, 16 * g + 8 * i + 8)
                window[i] = jnp.where(mask, picked[rows] + picked[WIDTH:][rows], window[i])
        window = jnp.concatenate(window, axis=0)
        w_left, w_here, w_right, w_far = lagrange_rows(offset)
        stencil = jnp.where(
            place == 0.0,
            w_left,
            jnp.where(
                place == 1.0,
                w_here,
                jnp.where(place == 2.0, w_right, jnp.where(place == 3.0, w_far, 0.0)),
            ),
        )
        reading = jnp.sum(stencil * window, axis=0, keepdims=True)
        parts = split(stencil * (weight * (reading - value)))
        group = jnp.broadcast_to(group, (16, OBS_CHUNK)).astype(BF16)
        masks = [group == jnp.array(float(g), BF16) for g in range(WIDTH // 16 - 1)]
        for i, part in enumerate(parts):
            pieces = []
            for g in range(WIDTH // 16):
                piece = none
                if g > 0:
                    piece = jnp.where(masks[g - 1], part[16:32], piece)
                if g < WIDTH // 16 - 1:
                    piece = jnp.where(masks[g], part[0:16], piece)
                pieces.append(piece)
            spread_all[i * WIDTH : (i + 1) * WIDTH, columns] = jnp.concatenate(pieces, axis=0)
    forcing = dot(spread_all[...], chosen_all[...], NT)
    forcing = (forcing[0:WIDTH] + forcing[WIDTH:]).T

    lanes = lane_ids((BLOCKS * ROWS, WIDTH))
    halo = pltpu.roll(forcing, WIDTH - STRIDE, 1)
    halo = jnp.concatenate([halo[(BLOCKS - 1) * ROWS :], halo[: (BLOCKS - 1) * ROWS]], axis=0)
    forcing = jnp.where(lanes < STRIDE, forcing, 0.0) + jnp.where(lanes < 3, halo, 0.0)
    costate = []
    for a in range(BLOCKS):
        force = forcing[a * ROWS : (a + 1) * ROWS]
        grad_hidden = dot(out_columns[:, 0:ROWS], force.astype(BF16))
        grad_pre = (grad_hidden * slopes[a]).astype(BF16)
        grad_unit = dot(in_rows[...], grad_pre)[0:ROWS]
        field = state[a * ROWS : (a + 1) * ROWS, :]
        mean_sq = jnp.sum(field * field, axis=0, keepdims=True) * (1.0 / channels)
        inverse = lax.rsqrt(mean_sq + EPSILON)
        scaled = grad_unit * gains[...]
        along = jnp.sum(scaled * field, axis=0, keepdims=True) * (1.0 / channels)
        costate.append(force + scaled * inverse - field * (along * inverse * inverse * inverse))
    costate = split(jnp.concatenate(costate, axis=0))
    for copy in copies[2:]:
        copy.wait()
    blocks = dot3(costate, (wide_high[...], wide_low[...]))
    grad_cos = jnp.zeros((ROWS, orders), F32)
    grad_sin = jnp.zeros((ROWS, orders), F32)
    for a in range(BLOCKS):
        turn_cos, turn_sin = turns[a : a + 1, :], turns[8 + a : 9 + a, :]
        block = blocks[a * ROWS : (a + 1) * ROWS]
        block_cos, block_sin = block[:, 0:orders], block[:, orders:]
        grad_cos = grad_cos + turn_cos * block_cos - turn_sin * block_sin
        grad_sin = grad_sin + turn_sin * block_cos + turn_cos * block_sin

    lanes = lane_ids((orders, LANES))
    pad = jnp.zeros((LANES - ROWS, orders), F32)
    for r, grad in ((0, grad_cos), (1, grad_sin)):
        upright = jnp.concatenate([grad, pad], axis=0).T
        high = upright.astype(BF16).astype(F32)
        low = pltpu.roll(upright - high, channels, 1)
        paired[pl.ds(r, orders, stride=2), :] = jnp.where(lanes < channels, high, low)
    out[...] = paired[...].astype(BF16)


def run_cycle(channels, arrived, prior, gains, prepared, table):
    orders = prepared[4].shape[1]
    hidden = prepared[1].shape[0]
    return pl.pallas_call(
        lambda *refs: cycle_kernel(channels, *refs),
        out_shape=jax.ShapeDtypeStruct((2 * orders, LANES), BF16),
        in_specs=[IN_VMEM] * 8 + [IN_HBM] * 4,
        out_specs=IN_VMEM,
        scratch_shapes=[
            *(pltpu.VMEM(part.shape, BF16) for part in table),
            pltpu.SemaphoreType.DMA((4,)),
            pltpu.VMEM((BLOCKS * ROWS, WIDTH), F32),
            pltpu.VMEM((BLOCKS, hidden, WIDTH), F32),
            pltpu.VMEM((BANDS // 2, FIELDS, LANES), F32),
            pltpu.VMEM((BLOCKS * ROWS, BANDS * SLOTS), BF16),
            pltpu.VMEM((2 * WIDTH, BANDS * SLOTS), BF16),
            pltpu.VMEM((2 * orders, LANES), F32),
        ],
        compiler_params=pltpu.CompilerParams(vmem_limit_bytes=36 * MIB),
        cost_estimate=pl.CostEstimate(
            flops=8_000_000_000, bytes_accessed=4_000_000, transcendentals=1_200_000
        ),
        name="cycle",
    )(arrived, prior, gains, *prepared, *in_hbm(*table))


def analysis_kernel(parity, arrived, control, sigma, table_high, table_low, out, rows):
    channels = sigma.shape[0]
    orders = arrived.shape[0] // 2
    rows[...] = arrived[...].astype(F32)
    lanes = lane_ids((orders, LANES))
    for r in range(2):
        both = rows[pl.ds(r, orders, stride=2), :]
        low = pltpu.roll(both, LANES - channels, 1)
        grad = jnp.where(lanes < channels, both, 0.0)
        grad = grad + jnp.where(lanes < LANES - channels, low, 0.0)
        grad_t = split(grad.T[0:ROWS])
        projected = dot3(grad_t, (table_high[0], table_low[0]))
        out[:, r, 0, :] = control[:, r, 0, :] + sigma[:, 0, :] * projected[0:channels]


def analysis(parity, arrived, control, sigma, table):
    wave_count = table[0].shape[2]
    lat_count = table[0].shape[1]
    whole = lambda shape: pl.BlockSpec(shape, lambda i, p: (0,) * len(shape))
    chosen = pl.BlockSpec((1, lat_count, wave_count), lambda i, p: (p[0], 0, 0))
    return pl.pallas_call(
        analysis_kernel,
        out_shape=jax.ShapeDtypeStruct(control.shape, F32),
        grid_spec=pltpu.PrefetchScalarGridSpec(
            num_scalar_prefetch=1,
            grid=(1,),
            in_specs=[
                whole(arrived.shape),
                whole(control.shape),
                whole(sigma.shape),
                chosen,
                chosen,
            ],
            out_specs=whole(control.shape),
            scratch_shapes=[pltpu.VMEM(arrived.shape, F32)],
        ),
        cost_estimate=pl.CostEstimate(flops=400_000_000, bytes_accessed=2_000_000, transcendentals=0),
        compiler_params=pltpu.CompilerParams(vmem_limit_bytes=12 * MIB),
        name="analysis",
    )(parity, arrived, control, sigma, *table)


def shards(
    control,
    spec_sigma,
    prior_mean_field,
    magnitude_factor,
    w_in,
    w_out,
    obs_band,
    obs_cell,
    obs_value,
    obs_weight,
    obs_offset,
):
    channels, _, _, wave_count = control.shape
    lat_count = BANDS * TPS
    lon_count = prior_mean_field.shape[2]
    legendre = legendre_np(wave_count, lat_count)
    zonal = zonal_np(lat_count, lon_count)
    turns = turn_np(lat_count, lon_count)
    parity = (lax.axis_index("tp") % 2).astype(jnp.int32).reshape(1)
    send = synthesis(control, spec_sigma, w_in, w_out.T, legendre)
    got = lax.all_to_all(send, "tp", split_axis=0, concat_axis=0, tiled=True)
    obs = pack_obs(
        *(
            field.reshape(-1, LANES)
            for field in (obs_band, obs_cell, obs_value, obs_weight, obs_offset)
        )
    )
    send = regroup(got, obs).reshape(BANDS, 16, LANES)
    arrived = lax.all_to_all(send, "band", split_axis=0, concat_axis=0, tiled=True)
    other = lax.ppermute(got, "band", [(i, i ^ 1) for i in range(BANDS)])
    prepared = prepare(got, other, (turns,))
    prior = jnp.pad(prior_mean_field[:, 0, :], ((0, ROWS - channels), (0, 0)))
    prior = jnp.concatenate([prior, prior[:, : WIDTH - STRIDE]], axis=1)
    prior = jnp.stack([prior[:, a * STRIDE : a * STRIDE + WIDTH] for a in range(BLOCKS)])
    gains = jnp.broadcast_to(
        jnp.pad(magnitude_factor, (0, ROWS - channels))[:, None], (ROWS, WIDTH)
    )
    modes = run_cycle(channels, arrived, prior, gains, prepared, zonal)
    modes = lax.all_to_all(
        modes.reshape(lat_count, 2, LANES),
        ("band", "tp"),
        split_axis=0,
        concat_axis=0,
        tiled=True,
    )
    modes = modes.reshape(2 * lat_count, LANES)
    return analysis(parity, modes, control, spec_sigma, legendre)


def solution(mesh):
    placed = (
        P(None, None, ("band", "tp"), None),
        P(None, ("band", "tp"), None),
        P(None, ("band", "tp"), None),
        P(),
        P(None, "tp"),
        P("tp", None),
        P("band", "tp", None, None),
        P("band", "tp", None),
        P("band", "tp", None),
        P("band", "tp", None),
        P("band", "tp", None),
    )
    return jax.shard_map(
        shards,
        mesh=mesh,
        in_specs=placed,
        out_specs=P(None, None, ("band", "tp"), None),
        check_vma=False,
    )
```

```python
import math

import jax
import jax.numpy as jnp
import ml_dtypes
import numpy as np
from jax import lax
from jax.experimental import pallas as pl
from jax.experimental.pallas import tpu as pltpu
from jax.sharding import PartitionSpec as P

EPSILON = 1e-06
BF16 = jnp.bfloat16
F32 = jnp.float32

BLOCKS = 6
PAIRS = BLOCKS // 2
STRIDE = 240
WIDTH = 256
ROWS = 72
LANES = 128
BANDS = 64
TPS = 8
SLOTS = 64
FIELDS = 8
ROW_SHIFT = 256
OBS_CHUNK = 512
MIB = 1024 * 1024


def split_np(table):
    high = table.astype(np.float32).astype(ml_dtypes.bfloat16)
    low = (table - high.astype(np.float64)).astype(np.float32).astype(ml_dtypes.bfloat16)
    return high, low


def legendre_np(wave_count, lat_count):
    cycles = np.arange(lat_count)
    tables = []
    for parity in range(2):
        frequency = np.arange(wave_count) + parity
        phases = (2 * cycles[:, None] + 1) * frequency[None, :] % (4 * lat_count)
        angles = phases * (math.pi / (2 * lat_count))
        basis = np.sin(angles) if parity else np.cos(angles)
        tables.append(basis * math.sqrt(2.0 / lat_count))
    return split_np(np.stack(tables))


def even_odd_np(orders):
    return np.concatenate([np.arange(0, orders, 2), np.arange(1, orders, 2)])


def zonal_np(orders, lon_count):
    phases = even_odd_np(orders)[:, None] * np.arange(WIDTH)[None, :] % lon_count
    angles = phases * (2.0 * math.pi / lon_count)
    halves = angles.reshape(2, 1, orders // 2, WIDTH)
    parts = np.concatenate([np.cos(halves), np.sin(halves)], axis=1)
    high, low = split_np(parts.reshape(2 * orders, WIDTH))
    return high, low, np.ascontiguousarray(high.T), np.ascontiguousarray(low.T)


def turn_np(orders, lon_count):
    phases = np.arange(PAIRS)[:, None] * STRIDE * even_odd_np(orders)[None, :] % lon_count
    angles = phases * (2.0 * math.pi / lon_count)
    pad = np.zeros((4 - PAIRS, orders))
    return np.concatenate([np.cos(angles), pad, np.sin(angles), pad]).astype(np.float32)


def split(values):
    high = values.astype(BF16)
    low = (values - high.astype(F32)).astype(BF16)
    return high, low


NN = (((1,), (0,)), ((), ()))
NT = (((1,), (1,)), ((), ()))


def dot(left, right, dims=NN):
    return lax.dot_general(left, right, dims, preferred_element_type=F32)


def dot3(left, right, dims=NN):
    return (
        dot(left[0], right[0], dims) + dot(left[0], right[1], dims) + dot(left[1], right[0], dims)
    )


def lane_ids(shape):
    return lax.broadcasted_iota(jnp.int32, shape, len(shape) - 1)


SEND_ROWS = 128
REST_LANE = 96
PIECE_LANE = 112


def synthesis_kernel(
    control_hbm,
    sigma_hbm,
    high_hbm,
    low_hbm,
    w_in_hbm,
    w_out_hbm,
    out,
    control,
    sigma,
    table_high,
    table_low,
    w_in,
    w_out,
    coef,
    modes,
    arrivals,
):
    parity = lax.rem(lax.axis_index("tp"), 2)
    copies = [
        pltpu.make_async_copy(source, target, arrivals.at[i])
        for i, (source, target) in enumerate(
            (
                (control_hbm, control),
                (sigma_hbm, sigma),
                (high_hbm.at[parity], table_high),
                (low_hbm.at[parity], table_low),
                (w_in_hbm, w_in),
                (w_out_hbm, w_out),
            )
        )
    ]
    for copy in copies:
        copy.start()
    channels = sigma.shape[0]
    coef[...] = jnp.zeros_like(coef)
    copies[0].wait()
    copies[1].wait()
    deviation = sigma[:, 0, :]
    first = deviation * control[:, 0, 0, :]
    second = deviation * control[:, 1, 0, :]
    coef[0:channels, :] = first
    coef[ROWS:LANES, :] = second[: LANES - ROWS]
    tail = channels - (LANES - ROWS)
    coef[LANES + REST_LANE : LANES + REST_LANE + tail, :] = second[LANES - ROWS :]
    parts = split(coef[...])
    for copy in copies[2:]:
        copy.wait()
    whole = dot3((table_high[...], table_low[...]), parts, NT)
    modes[0] = whole[:, 0:LANES]
    modes[1] = whole[:, LANES:]
    even = lax.rem(lax.axis_index("band"), 2) == 0
    rows = jnp.where(even, w_in[...].astype(F32), w_out[...].astype(F32))
    rows = jnp.pad(rows, ((0, ROWS - channels), (0, LANES - rows.shape[1])))
    lanes = lane_ids((8, LANES))
    pieces = [
        jnp.where(
            lanes >= PIECE_LANE,
            pltpu.roll(rows[BANDS:ROWS], PIECE_LANE - start, 1),
            rows[start // 2 : start // 2 + 8],
        )
        for start in range(0, REST_LANE, 16)
    ]
    rows = jnp.concatenate([*pieces, rows[REST_LANE // 2 : BANDS]], axis=0)
    for dest in range(TPS):
        out[dest, 0:BANDS, :] = modes[0, pl.ds(dest, BANDS, stride=TPS), :].astype(BF16)
        rest = modes[1, pl.ds(dest, BANDS, stride=TPS), :]
        out[dest, BANDS:SEND_ROWS, :] = (rest + rows).astype(BF16)


def in_hbm(*arrays):
    return tuple(pltpu.with_memory_space_constraint(jnp.asarray(a), pltpu.HBM) for a in arrays)


IN_VMEM = pl.BlockSpec(memory_space=pltpu.VMEM)
IN_HBM = pl.BlockSpec(memory_space=pltpu.HBM)


def synthesis(control, sigma, w_in, w_out_t, table):
    lat_count, wave_count = table[0].shape[1:]
    return pl.pallas_call(
        synthesis_kernel,
        out_shape=jax.ShapeDtypeStruct((TPS, SEND_ROWS, LANES), BF16),
        in_specs=[IN_HBM] * 6,
        out_specs=IN_VMEM,
        scratch_shapes=[
            pltpu.VMEM(control.shape, F32),
            pltpu.VMEM(sigma.shape, F32),
            pltpu.VMEM((lat_count, wave_count), BF16),
            pltpu.VMEM((lat_count, wave_count), BF16),
            pltpu.VMEM(w_in.shape, BF16),
            pltpu.VMEM(w_in.shape, BF16),
            pltpu.VMEM((2 * LANES, wave_count), F32),
            pltpu.VMEM((2, lat_count, LANES), F32),
            pltpu.SemaphoreType.DMA((6,)),
        ],
        cost_estimate=pl.CostEstimate(flops=400_000_000, bytes_accessed=2_000_000, transcendentals=0),
        compiler_params=pltpu.CompilerParams(vmem_limit_bytes=12 * MIB),
        name="synthesis",
    )(*in_hbm(control, sigma, *table, w_in, w_out_t))


def pack_kernel(band, cell, value, weight, offset, out):
    blocks = band.shape[0]
    cells = cell[...].astype(F32)
    channel = jnp.floor((cells + 0.5) * (1.0 / 1440.0))
    start = cells - 1440.0 * channel - 1.0
    start = jnp.where(start < 0.0, start + 1440.0, start)
    part = jnp.floor((start + 0.5) * (1.0 / STRIDE))
    fields = []
    for source in (value, weight, offset):
        high = source[...].astype(BF16).astype(F32)
        fields += [high, source[...] - high]
    fields += [part * ROWS + channel - ROW_SHIFT, start - part * STRIDE]
    band_ids = lax.broadcasted_iota(jnp.int32, (BANDS, LANES), 0)
    hits = [band_ids == band[i : i + 1, :] for i in range(blocks)]
    ones = [jnp.where(hit, 1.0, 0.0) for hit in hits]
    square = (LANES, 2 * LANES)
    row, column = lax.broadcasted_iota(jnp.int32, square, 0), lane_ids(square)
    before = jnp.where((row < column) | (column >= LANES), 1.0, 0.0).astype(BF16)
    counts = dot(jnp.concatenate(ones, axis=0).astype(BF16), before)
    slot_ids = lax.broadcasted_iota(jnp.int32, (LANES, LANES), 0).astype(F32)
    taken = jnp.zeros((BANDS, LANES), F32)
    total = jnp.zeros((BANDS, FIELDS * LANES), F32)
    for i in range(blocks):
        within = counts[i * BANDS : (i + 1) * BANDS, :]
        rank = jnp.sum(ones[i] * (within[:, :LANES] + taken), axis=0, keepdims=True)
        taken = taken + within[:, LANES:]
        here = slot_ids == rank + (LANES - SLOTS)
        spread = [jnp.where(here, field[i : i + 1, :], 0.0).astype(BF16) for field in fields]
        total = total + dot(ones[i].astype(BF16), jnp.concatenate(spread, axis=0), NT)
    out[...] = total


def pack_obs(band, cell, value, weight, offset):
    return pl.pallas_call(
        pack_kernel,
        out_shape=jax.ShapeDtypeStruct((BANDS, FIELDS * LANES), F32),
        cost_estimate=pl.CostEstimate(flops=200_000_000, bytes_accessed=300_000, transcendentals=0),
        compiler_params=pltpu.CompilerParams(vmem_limit_bytes=8 * MIB),
        name="pack_obs",
    )(band, cell, value, weight, offset)


def regroup_kernel(arrived, obs, out, rows):
    lanes = lane_ids((BANDS, LANES))
    for t in range(TPS):
        rows[pl.ds(t, BANDS, stride=16), :] = arrived[t, 0:BANDS, :].astype(F32)
        rest = pltpu.roll(arrived[t, BANDS : 2 * BANDS, :].astype(F32), LANES - REST_LANE, 1)
        rest = jnp.where(lanes < 16, rest, obs[:, t * LANES : (t + 1) * LANES])
        rows[pl.ds(8 + t, BANDS, stride=16), :] = rest
    out[...] = rows[...].astype(BF16)


def regroup(arrived, obs):
    return pl.pallas_call(
        regroup_kernel,
        out_shape=jax.ShapeDtypeStruct((BANDS * 16, LANES), BF16),
        scratch_shapes=[pltpu.VMEM((BANDS * 16, LANES), F32)],
        cost_estimate=pl.CostEstimate(flops=300_000, bytes_accessed=800_000, transcendentals=0),
        compiler_params=pltpu.CompilerParams(vmem_limit_bytes=8 * MIB),
        name="regroup",
    )(arrived, obs)


def prepare_kernel(own, other, *refs):
    sources, (in_rows, in_columns, out_rows, out_columns, *targets), (arrivals,) = (
        refs[:1],
        refs[1:6],
        refs[6:],
    )
    copies = [
        pltpu.make_async_copy(source, target, arrivals.at[i])
        for i, (source, target) in enumerate(zip(sources, targets))
    ]
    for copy in copies:
        copy.start()
    even = lax.rem(lax.axis_index("band"), 2) == 0
    lanes = lane_ids((8, LANES))
    filler = jnp.zeros((LANES - ROWS, LANES), F32)
    for columns, rows, first in ((in_columns, in_rows, True), (out_columns, out_rows, False)):
        pieces = []
        for t in range(TPS):
            mine = own[t, BANDS:SEND_ROWS, :].astype(F32)
            theirs = other[t, BANDS:SEND_ROWS, :].astype(F32)
            piece = jnp.where(even == first, mine, theirs)
            last = jnp.zeros((8, LANES), F32)
            for start in range(0, REST_LANE, 16):
                part = piece[start // 2 : start // 2 + 8]
                part = pltpu.roll(part, LANES - PIECE_LANE + start, 1)
                last = jnp.where((lanes >= start) & (lanes < start + 16), part, last)
            piece = jnp.concatenate([piece, last, filler], axis=0)
            pieces.append(piece.T[0:REST_LANE])
        upright = jnp.concatenate(pieces, axis=0)
        columns[...] = upright.astype(BF16)
        rows[...] = upright.T[0:80].astype(BF16)
    for copy in copies:
        copy.wait()


def prepare(own, other, tables):
    hidden = TPS * 96
    return pl.pallas_call(
        prepare_kernel,
        out_shape=(
            jax.ShapeDtypeStruct((80, hidden), BF16),
            jax.ShapeDtypeStruct((hidden, LANES), BF16),
            jax.ShapeDtypeStruct((80, hidden), BF16),
            jax.ShapeDtypeStruct((hidden, LANES), BF16),
            *(jax.ShapeDtypeStruct(table.shape, table.dtype) for table in tables),
        ),
        in_specs=[IN_VMEM] * 2 + [IN_HBM],
        out_specs=[IN_VMEM] * 5,
        scratch_shapes=[pltpu.SemaphoreType.DMA((1,))],
        cost_estimate=pl.CostEstimate(flops=1_000_000, bytes_accessed=5_000_000, transcendentals=0),
        compiler_params=pltpu.CompilerParams(vmem_limit_bytes=8 * MIB),
        name="prepare",
    )(own, other, *in_hbm(*tables))


GELU_SCALE = math.sqrt(2.0 / math.pi)
GELU_CUBE = 0.044715


def lagrange_rows(offset):
    return (
        -offset * (offset - 1.0) * (offset - 2.0) / 6.0,
        (offset + 1.0) * (offset - 1.0) * (offset - 2.0) / 2.0,
        -(offset + 1.0) * offset * (offset - 2.0) / 2.0,
        (offset + 1.0) * offset * (offset - 1.0) / 6.0,
    )


def cycle_kernel(
    channels,
    arrived,
    prior,
    gains,
    in_rows,
    in_columns,
    out_rows,
    out_columns,
    turns,
    table_high_hbm,
    table_low_hbm,
    wide_high_hbm,
    wide_low_hbm,
    out,
    table_high,
    table_low,
    wide_high,
    wide_low,
    arrivals,
    state,
    slopes,
    obs,
    chosen_all,
    spread_all,
    paired,
):
    orders = turns.shape[1]
    copies = [
        pltpu.make_async_copy(table_high_hbm, table_high, arrivals.at[0]),
        pltpu.make_async_copy(table_low_hbm, table_low, arrivals.at[1]),
        pltpu.make_async_copy(wide_high_hbm, wide_high, arrivals.at[2]),
        pltpu.make_async_copy(wide_low_hbm, wide_low, arrivals.at[3]),
    ]
    for copy in copies:
        copy.start()
    slices = arrived[...].astype(F32)
    rest = slices[:, 8:16, :]
    half = orders // 2
    paired[0:orders, :] = slices[:, 0:8, :].reshape(orders, LANES)
    paired[orders:, :] = rest.reshape(orders, LANES)
    cos_sin = [paired[pl.ds(p, half, stride=2), :] for p in range(2)]
    cos_sin = jnp.concatenate(cos_sin, axis=0).T
    tail = [paired[pl.ds(orders + p, half, stride=2), :] for p in range(2)]
    tail = jnp.concatenate(tail, axis=0).T
    cos_part = cos_sin[0:ROWS]
    sin_part = jnp.concatenate([cos_sin[ROWS:LANES], tail[0:16]], axis=0)
    pairs = rest.reshape(BANDS // 2, 2, FIELDS, LANES)
    near = pltpu.roll(pairs[:, 0].reshape(BANDS // 2 * FIELDS, LANES), LANES - SLOTS, 1)
    near = near.reshape(BANDS // 2, FIELDS, LANES)
    obs[...] = jnp.where(lane_ids(near.shape) < SLOTS, near, pairs[:, 1])

    turned = []
    for a in range(PAIRS):
        turn_cos, turn_sin = turns[a : a + 1, :], turns[4 + a : 5 + a, :]
        turned_cos = cos_part * turn_cos + sin_part * turn_sin
        turned_sin = sin_part * turn_cos - cos_part * turn_sin
        turned.append(
            jnp.concatenate(
                [turned_cos[:, :half], turned_sin[:, :half], turned_cos[:, half:], turned_sin[:, half:]],
                axis=1,
            )
        )
    turned = split(jnp.concatenate(turned, axis=0))
    for copy in copies[:2]:
        copy.wait()
    sums = []
    for p in range(2):
        span = slice(p * orders, (p + 1) * orders)
        part = (turned[0][:, span], turned[1][:, span])
        sums.append(dot3(part, (table_high[span, :], table_low[span, :])))
    field = jnp.concatenate([sums[0] + sums[1], sums[0] - sums[1]], axis=0)
    state[...] = prior[...].reshape(BLOCKS * ROWS, WIDTH) + field

    forecast = []
    for a in range(BLOCKS):
        field = state[a * ROWS : (a + 1) * ROWS, :]
        mean_sq = jnp.sum(field * field, axis=0, keepdims=True) * (1.0 / channels)
        unit = (field * gains[...] * lax.rsqrt(mean_sq + EPSILON)).astype(BF16)
        pre = dot(in_columns[:, 0:ROWS], unit)
        square = pre * pre
        inner = pre * (GELU_SCALE + (GELU_SCALE * GELU_CUBE) * square)
        gate = 0.5 + 0.5 * jnp.tanh(inner)
        hidden = pre * gate
        slopes[a] = gate + hidden * (1.0 - gate) * (
            2.0 * GELU_SCALE + (6.0 * GELU_SCALE * GELU_CUBE) * square
        )
        forecast.append(field + dot(out_rows[...], hidden.astype(BF16))[0:ROWS])
    forecast = split(jnp.concatenate(forecast, axis=0).T)
    forecast = jnp.concatenate(forecast, axis=0)

    per_chunk = OBS_CHUNK // LANES
    chunks = obs.shape[0] // per_chunk
    low_ids = lax.broadcasted_iota(jnp.int32, (16, OBS_CHUNK), 0).astype(F32)
    near_ids = lax.broadcasted_iota(jnp.int32, (32, OBS_CHUNK), 0).astype(F32)
    none = jnp.zeros((16, OBS_CHUNK), BF16)

    def fields_of(chunk):
        fields = [obs[chunk * per_chunk + i] for i in range(per_chunk)]
        return jnp.concatenate(fields, axis=1)

    def choose(chunk):
        row = fields_of(chunk)[6:7] + float(ROW_SHIFT)
        row_group = jnp.floor(row * (1.0 / 16.0))
        first = jnp.where(low_ids == row - 16.0 * row_group, 1.0, 0.0).astype(BF16)
        row_group = jnp.broadcast_to(row_group, (16, OBS_CHUNK)).astype(BF16)
        chosen = jnp.concatenate(
            [
                jnp.where(row_group == jnp.array(float(g), BF16), first, none)
                for g in range(BLOCKS * ROWS // 16)
            ],
            axis=0,
        )
        chosen_all[:, chunk * OBS_CHUNK : (chunk + 1) * OBS_CHUNK] = chosen
        return chosen

    def observe(chunk, picked):
        fields = fields_of(chunk)
        columns = slice(chunk * OBS_CHUNK, (chunk + 1) * OBS_CHUNK)
        value = fields[0:1] + fields[1:2]
        weight = fields[2:3] + fields[3:4]
        offset = fields[4:5] + fields[5:6]
        group = jnp.floor(fields[7:8] * (1.0 / 16.0))
        place = near_ids - (fields[7:8] - 16.0 * group)
        group8 = jnp.broadcast_to(group, (8, OBS_CHUNK))
        window = [jnp.zeros((8, OBS_CHUNK), F32)] * 4
        for g in range(WIDTH // 16 - 1):
            mask = group8 == float(g)
            for i in range(4):
                rows = slice(16 * g + 8 * i, 16 * g + 8 * i + 8)
                window[i] = jnp.where(mask, picked[rows] + picked[WIDTH:][rows], window[i])
        window = jnp.concatenate(window, axis=0)
        w_left, w_here, w_right, w_far = lagrange_rows(offset)
        stencil = jnp.where(
            place == 0.0,
            w_left,
            jnp.where(
                place == 1.0,
                w_here,
                jnp.where(place == 2.0, w_right, jnp.where(place == 3.0, w_far, 0.0)),
            ),
        )
        reading = jnp.sum(stencil * window, axis=0, keepdims=True)
        parts = split(stencil * (weight * (reading - value)))
        group = jnp.broadcast_to(group, (16, OBS_CHUNK)).astype(BF16)
        masks = [group == jnp.array(float(g), BF16) for g in range(WIDTH // 16 - 1)]
        for i, part in enumerate(parts):
            pieces = []
            for g in range(WIDTH // 16):
                piece = none
                if g > 0:
                    piece = jnp.where(masks[g - 1], part[16:32], piece)
                if g < WIDTH // 16 - 1:
                    piece = jnp.where(masks[g], part[0:16], piece)
                pieces.append(piece)
            spread_all[i * WIDTH : (i + 1) * WIDTH, columns] = jnp.concatenate(pieces, axis=0)

    chosen = choose(0)
    picked = None
    for chunk in range(chunks):
        latest = dot(forecast, chosen)
        if chunk + 1 < chunks:
            chosen = choose(chunk + 1)
        if chunk > 0:
            observe(chunk - 1, picked)
        picked = latest
    observe(chunks - 1, picked)
    forcing = dot(spread_all[...], chosen_all[...], NT)
    forcing = (forcing[0:WIDTH] + forcing[WIDTH:]).T

    lanes = lane_ids((BLOCKS * ROWS, WIDTH))
    halo = pltpu.roll(forcing, WIDTH - STRIDE, 1)
    halo = jnp.concatenate([halo[(BLOCKS - 1) * ROWS :], halo[: (BLOCKS - 1) * ROWS]], axis=0)
    forcing = jnp.where(lanes < STRIDE, forcing, 0.0) + jnp.where(lanes < 3, halo, 0.0)
    costate = []
    for a in range(BLOCKS):
        force = forcing[a * ROWS : (a + 1) * ROWS]
        grad_hidden = dot(out_columns[:, 0:ROWS], force.astype(BF16))
        grad_pre = (grad_hidden * slopes[a]).astype(BF16)
        grad_unit = dot(in_rows[...], grad_pre)[0:ROWS]
        field = state[a * ROWS : (a + 1) * ROWS, :]
        mean_sq = jnp.sum(field * field, axis=0, keepdims=True) * (1.0 / channels)
        inverse = lax.rsqrt(mean_sq + EPSILON)
        scaled = grad_unit * gains[...]
        along = jnp.sum(scaled * field, axis=0, keepdims=True) * (1.0 / channels)
        costate.append(force + scaled * inverse - field * (along * inverse * inverse * inverse))
    near = jnp.concatenate(costate[:PAIRS], axis=0)
    far = jnp.concatenate(costate[PAIRS:], axis=0)
    for copy in copies[2:]:
        copy.wait()
    pad = jnp.zeros((LANES - ROWS, half), F32)
    lanes = lane_ids((half, LANES))
    for p, both in enumerate((near + far, near - far)):
        span = slice(p * orders, (p + 1) * orders)
        blocks = dot3(split(both), (wide_high[:, span], wide_low[:, span]))
        grads = [jnp.zeros((ROWS, half), F32)] * 2
        for a in range(PAIRS):
            turn_cos = turns[a : a + 1, p * half : (p + 1) * half]
            turn_sin = turns[4 + a : 5 + a, p * half : (p + 1) * half]
            block = blocks[a * ROWS : (a + 1) * ROWS]
            block_cos, block_sin = block[:, :half], block[:, half:]
            grads[0] = grads[0] + turn_cos * block_cos - turn_sin * block_sin
            grads[1] = grads[1] + turn_sin * block_cos + turn_cos * block_sin
        for r in range(2):
            upright = jnp.concatenate([grads[r], pad], axis=0).T
            high = upright.astype(BF16).astype(F32)
            low = pltpu.roll(upright - high, channels, 1)
            place = pl.ds(2 * p + r, half, stride=4)
            paired[place, :] = jnp.where(lanes < channels, high, low)
    out[...] = paired[...].astype(BF16)


def run_cycle(channels, arrived, prior, gains, prepared, table):
    orders = prepared[4].shape[1]
    hidden = prepared[1].shape[0]
    return pl.pallas_call(
        lambda *refs: cycle_kernel(channels, *refs),
        out_shape=jax.ShapeDtypeStruct((2 * orders, LANES), BF16),
        in_specs=[IN_VMEM] * 8 + [IN_HBM] * 4,
        out_specs=IN_VMEM,
        scratch_shapes=[
            *(pltpu.VMEM(part.shape, BF16) for part in table),
            pltpu.SemaphoreType.DMA((4,)),
            pltpu.VMEM((BLOCKS * ROWS, WIDTH), F32),
            pltpu.VMEM((BLOCKS, hidden, WIDTH), F32),
            pltpu.VMEM((BANDS // 2, FIELDS, LANES), F32),
            pltpu.VMEM((BLOCKS * ROWS, BANDS * SLOTS), BF16),
            pltpu.VMEM((2 * WIDTH, BANDS * SLOTS), BF16),
            pltpu.VMEM((2 * orders, LANES), F32),
        ],
        compiler_params=pltpu.CompilerParams(vmem_limit_bytes=36 * MIB),
        cost_estimate=pl.CostEstimate(
            flops=8_000_000_000, bytes_accessed=4_000_000, transcendentals=1_200_000
        ),
        name="cycle",
    )(arrived, prior, gains, *prepared, *in_hbm(*table))


def analysis_kernel(parity, arrived, control, sigma, table_high, table_low, out, rows):
    channels = sigma.shape[0]
    orders = arrived.shape[0] // 2
    rows[...] = arrived[...].astype(F32)
    lanes = lane_ids((orders, LANES))
    for r in range(2):
        both = rows[pl.ds(r, orders, stride=2), :]
        low = pltpu.roll(both, LANES - channels, 1)
        grad = jnp.where(lanes < channels, both, 0.0)
        grad = grad + jnp.where(lanes < LANES - channels, low, 0.0)
        grad_t = split(grad.T[0:ROWS])
        projected = dot3(grad_t, (table_high[0], table_low[0]))
        out[:, r, 0, :] = control[:, r, 0, :] + sigma[:, 0, :] * projected[0:channels]


def analysis(parity, arrived, control, sigma, table):
    wave_count = table[0].shape[2]
    lat_count = table[0].shape[1]
    whole = lambda shape: pl.BlockSpec(shape, lambda i, p: (0,) * len(shape))
    chosen = pl.BlockSpec((1, lat_count, wave_count), lambda i, p: (p[0], 0, 0))
    return pl.pallas_call(
        analysis_kernel,
        out_shape=jax.ShapeDtypeStruct(control.shape, F32),
        grid_spec=pltpu.PrefetchScalarGridSpec(
            num_scalar_prefetch=1,
            grid=(1,),
            in_specs=[
                whole(arrived.shape),
                whole(control.shape),
                whole(sigma.shape),
                chosen,
                chosen,
            ],
            out_specs=whole(control.shape),
            scratch_shapes=[pltpu.VMEM(arrived.shape, F32)],
        ),
        cost_estimate=pl.CostEstimate(flops=400_000_000, bytes_accessed=2_000_000, transcendentals=0),
        compiler_params=pltpu.CompilerParams(vmem_limit_bytes=12 * MIB),
        name="analysis",
    )(parity, arrived, control, sigma, *table)


def shards(
    control,
    spec_sigma,
    prior_mean_field,
    magnitude_factor,
    w_in,
    w_out,
    obs_band,
    obs_cell,
    obs_value,
    obs_weight,
    obs_offset,
):
    channels, _, _, wave_count = control.shape
    lat_count = BANDS * TPS
    lon_count = prior_mean_field.shape[2]
    legendre = legendre_np(wave_count, lat_count)
    zonal = zonal_np(lat_count, lon_count)
    turns = turn_np(lat_count, lon_count)
    parity = (lax.axis_index("tp") % 2).astype(jnp.int32).reshape(1)
    send = synthesis(control, spec_sigma, w_in, w_out.T, legendre)
    got = lax.all_to_all(send, "tp", split_axis=0, concat_axis=0, tiled=True)
    obs = pack_obs(
        *(
            field.reshape(-1, LANES)
            for field in (obs_band, obs_cell, obs_value, obs_weight, obs_offset)
        )
    )
    send = regroup(got, obs).reshape(BANDS, 16, LANES)
    arrived = lax.all_to_all(send, "band", split_axis=0, concat_axis=0, tiled=True)
    other = lax.ppermute(got, "band", [(i, i ^ 1) for i in range(BANDS)])
    prepared = prepare(got, other, (turns,))
    prior = jnp.pad(prior_mean_field[:, 0, :], ((0, ROWS - channels), (0, 0)))
    prior = jnp.concatenate([prior, prior[:, : WIDTH - STRIDE]], axis=1)
    prior = jnp.stack([prior[:, a * STRIDE : a * STRIDE + WIDTH] for a in range(BLOCKS)])
    gains = jnp.broadcast_to(
        jnp.pad(magnitude_factor, (0, ROWS - channels))[:, None], (ROWS, WIDTH)
    )
    modes = run_cycle(channels, arrived, prior, gains, prepared, zonal)
    modes = lax.all_to_all(
        modes.reshape(lat_count, 2, LANES),
        ("band", "tp"),
        split_axis=0,
        concat_axis=0,
        tiled=True,
    )
    modes = modes.reshape(2 * lat_count, LANES)
    return analysis(parity, modes, control, spec_sigma, legendre)


def solution(mesh):
    placed = (
        P(None, None, ("band", "tp"), None),
        P(None, ("band", "tp"), None),
        P(None, ("band", "tp"), None),
        P(),
        P(None, "tp"),
        P("tp", None),
        P("band", "tp", None, None),
        P("band", "tp", None),
        P("band", "tp", None),
        P("band", "tp", None),
        P("band", "tp", None),
    )
    return jax.shard_map(
        shards,
        mesh=mesh,
        in_specs=placed,
        out_specs=P(None, None, ("band", "tp"), None),
        check_vma=False,
    )
```

```python
import math

import jax
import jax.numpy as jnp
import ml_dtypes
import numpy as np
from jax import lax
from jax.experimental import pallas as pl
from jax.experimental.pallas import tpu as pltpu
from jax.sharding import PartitionSpec as P

EPSILON = 1e-06
BF16 = jnp.bfloat16
F32 = jnp.float32

BLOCKS = 6
PAIRS = BLOCKS // 2
STRIDE = 240
WIDTH = 256
ROWS = 72
LANES = 128
BANDS = 64
TPS = 8
SLOTS = 64
FIELDS = 8
ROW_SHIFT = 256
OBS_CHUNK = 512
MIB = 1024 * 1024


def split_np(table):
    high = table.astype(np.float32).astype(ml_dtypes.bfloat16)
    low = (table - high.astype(np.float64)).astype(np.float32).astype(ml_dtypes.bfloat16)
    return high, low


def legendre_np(wave_count, lat_count):
    cycles = np.arange(lat_count)
    tables = []
    for parity in range(2):
        frequency = np.arange(wave_count) + parity
        phases = (2 * cycles[:, None] + 1) * frequency[None, :] % (4 * lat_count)
        angles = phases * (math.pi / (2 * lat_count))
        basis = np.sin(angles) if parity else np.cos(angles)
        tables.append(basis * math.sqrt(2.0 / lat_count))
    return split_np(np.stack(tables))


def even_odd_np(orders):
    return np.concatenate([np.arange(0, orders, 2), np.arange(1, orders, 2)])


def zonal_np(orders, lon_count):
    phases = even_odd_np(orders)[:, None] * np.arange(WIDTH)[None, :] % lon_count
    angles = phases * (2.0 * math.pi / lon_count)
    halves = angles.reshape(2, 1, orders // 2, WIDTH)
    parts = np.concatenate([np.cos(halves), np.sin(halves)], axis=1)
    high, low = split_np(parts.reshape(2 * orders, WIDTH))
    return high, low, np.ascontiguousarray(high.T), np.ascontiguousarray(low.T)


def turn_np(orders, lon_count):
    phases = np.arange(PAIRS)[:, None] * STRIDE * even_odd_np(orders)[None, :] % lon_count
    angles = phases * (2.0 * math.pi / lon_count)
    pad = np.zeros((4 - PAIRS, orders))
    return np.concatenate([np.cos(angles), pad, np.sin(angles), pad]).astype(np.float32)


def split(values):
    high = values.astype(BF16)
    low = (values - high.astype(F32)).astype(BF16)
    return high, low


NN = (((1,), (0,)), ((), ()))
NT = (((1,), (1,)), ((), ()))


def dot(left, right, dims=NN):
    return lax.dot_general(left, right, dims, preferred_element_type=F32)


def dot3(left, right, dims=NN):
    return (
        dot(left[0], right[0], dims) + dot(left[0], right[1], dims) + dot(left[1], right[0], dims)
    )


def lane_ids(shape):
    return lax.broadcasted_iota(jnp.int32, shape, len(shape) - 1)


SEND_ROWS = 112
REST_LANE = 96
MORE_LANE = 112
QUARTER = 40


def synthesis_kernel(
    control_hbm,
    sigma_hbm,
    high_hbm,
    low_hbm,
    w_in_hbm,
    w_out_hbm,
    out,
    control,
    sigma,
    table_high,
    table_low,
    w_in,
    w_out,
    coef,
    modes,
    arrivals,
):
    parity = lax.rem(lax.axis_index("tp"), 2)
    copies = [
        pltpu.make_async_copy(source, target, arrivals.at[i])
        for i, (source, target) in enumerate(
            (
                (control_hbm, control),
                (sigma_hbm, sigma),
                (high_hbm.at[parity], table_high),
                (low_hbm.at[parity], table_low),
                (w_in_hbm, w_in),
                (w_out_hbm, w_out),
            )
        )
    ]
    for copy in copies:
        copy.start()
    channels = sigma.shape[0]
    coef[...] = jnp.zeros_like(coef)
    copies[0].wait()
    copies[1].wait()
    deviation = sigma[:, 0, :]
    first = deviation * control[:, 0, 0, :]
    second = deviation * control[:, 1, 0, :]
    coef[0:channels, :] = first
    coef[ROWS:LANES, :] = second[: LANES - ROWS]
    tail = channels - (LANES - ROWS)
    coef[LANES + REST_LANE : LANES + REST_LANE + tail, :] = second[LANES - ROWS :]
    parts = split(coef[...])
    for copy in copies[2:]:
        copy.wait()
    whole = dot3((table_high[...], table_low[...]), parts, NT)
    modes[0] = whole[:, 0:LANES]
    modes[1] = whole[:, LANES:]
    code = lax.rem(lax.axis_index("band"), 4)
    rows = jnp.where(lax.rem(code, 2) == 0, w_in[...].astype(F32), w_out[...].astype(F32))
    rows = jnp.pad(rows, ((0, 2 * QUARTER - channels), (0, LANES - rows.shape[1])))
    rows = jnp.where(code < 2, rows[0:QUARTER], rows[QUARTER:])
    rows = jnp.concatenate([rows, jnp.zeros((48 - QUARTER, LANES), F32)], axis=0)
    filler = jnp.zeros((32, LANES), F32)
    for dest in range(TPS):
        out[dest, 0:BANDS, :] = modes[0, pl.ds(dest, BANDS, stride=TPS), :].astype(BF16)
        rest = modes[1, pl.ds(dest, BANDS, stride=TPS), :]
        more = pltpu.roll(rest[48:BANDS], MORE_LANE - REST_LANE, 1)
        rest = rest[0:48] + jnp.concatenate([more, filler], axis=0)
        out[dest, BANDS:SEND_ROWS, :] = (rest + rows).astype(BF16)


def in_hbm(*arrays):
    return tuple(pltpu.with_memory_space_constraint(jnp.asarray(a), pltpu.HBM) for a in arrays)


IN_VMEM = pl.BlockSpec(memory_space=pltpu.VMEM)
IN_HBM = pl.BlockSpec(memory_space=pltpu.HBM)


def synthesis(control, sigma, w_in, w_out_t, table):
    lat_count, wave_count = table[0].shape[1:]
    return pl.pallas_call(
        synthesis_kernel,
        out_shape=jax.ShapeDtypeStruct((TPS, SEND_ROWS, LANES), BF16),
        in_specs=[IN_HBM] * 6,
        out_specs=IN_VMEM,
        scratch_shapes=[
            pltpu.VMEM(control.shape, F32),
            pltpu.VMEM(sigma.shape, F32),
            pltpu.VMEM((lat_count, wave_count), BF16),
            pltpu.VMEM((lat_count, wave_count), BF16),
            pltpu.VMEM(w_in.shape, BF16),
            pltpu.VMEM(w_in.shape, BF16),
            pltpu.VMEM((2 * LANES, wave_count), F32),
            pltpu.VMEM((2, lat_count, LANES), F32),
            pltpu.SemaphoreType.DMA((6,)),
        ],
        cost_estimate=pl.CostEstimate(flops=400_000_000, bytes_accessed=2_000_000, transcendentals=0),
        compiler_params=pltpu.CompilerParams(vmem_limit_bytes=12 * MIB),
        name="synthesis",
    )(*in_hbm(control, sigma, *table, w_in, w_out_t))


def pack_kernel(band, cell, value, weight, offset, out):
    blocks = band.shape[0]
    cells = cell[...].astype(F32)
    channel = jnp.floor((cells + 0.5) * (1.0 / 1440.0))
    start = cells - 1440.0 * channel - 1.0
    start = jnp.where(start < 0.0, start + 1440.0, start)
    part = jnp.floor((start + 0.5) * (1.0 / STRIDE))
    fields = []
    for source in (value, weight, offset):
        high = source[...].astype(BF16).astype(F32)
        fields += [high, source[...] - high]
    fields += [part * ROWS + channel - ROW_SHIFT, start - part * STRIDE]
    band_ids = lax.broadcasted_iota(jnp.int32, (BANDS, LANES), 0)
    hits = [band_ids == band[i : i + 1, :] for i in range(blocks)]
    ones = [jnp.where(hit, 1.0, 0.0) for hit in hits]
    square = (LANES, 2 * LANES)
    row, column = lax.broadcasted_iota(jnp.int32, square, 0), lane_ids(square)
    before = jnp.where((row < column) | (column >= LANES), 1.0, 0.0).astype(BF16)
    counts = dot(jnp.concatenate(ones, axis=0).astype(BF16), before)
    slot_ids = lax.broadcasted_iota(jnp.int32, (LANES, LANES), 0).astype(F32)
    taken = jnp.zeros((BANDS, LANES), F32)
    total = jnp.zeros((BANDS, FIELDS * LANES), F32)
    for i in range(blocks):
        within = counts[i * BANDS : (i + 1) * BANDS, :]
        rank = jnp.sum(ones[i] * (within[:, :LANES] + taken), axis=0, keepdims=True)
        taken = taken + within[:, LANES:]
        here = slot_ids == rank + (LANES - SLOTS)
        spread = [jnp.where(here, field[i : i + 1, :], 0.0).astype(BF16) for field in fields]
        total = total + dot(ones[i].astype(BF16), jnp.concatenate(spread, axis=0), NT)
    out[...] = total


def pack_obs(band, cell, value, weight, offset):
    return pl.pallas_call(
        pack_kernel,
        out_shape=jax.ShapeDtypeStruct((BANDS, FIELDS * LANES), F32),
        cost_estimate=pl.CostEstimate(flops=200_000_000, bytes_accessed=300_000, transcendentals=0),
        compiler_params=pltpu.CompilerParams(vmem_limit_bytes=8 * MIB),
        name="pack_obs",
    )(band, cell, value, weight, offset)


def regroup_kernel(arrived, obs, out, rows):
    lanes = lane_ids((BANDS, LANES))
    for t in range(TPS):
        rows[pl.ds(t, BANDS, stride=16), :] = arrived[t, 0:BANDS, :].astype(F32)
        rest = arrived[t, BANDS:SEND_ROWS, :].astype(F32)
        rest = jnp.concatenate(
            [
                pltpu.roll(rest, LANES - REST_LANE, 1),
                pltpu.roll(rest[0 : 2 * BANDS - SEND_ROWS], LANES - MORE_LANE, 1),
            ],
            axis=0,
        )
        rest = jnp.where(lanes < 16, rest, obs[:, t * LANES : (t + 1) * LANES])
        rows[pl.ds(8 + t, BANDS, stride=16), :] = rest
    out[...] = rows[...].astype(BF16)


def regroup(arrived, obs):
    return pl.pallas_call(
        regroup_kernel,
        out_shape=jax.ShapeDtypeStruct((BANDS * 16, LANES), BF16),
        scratch_shapes=[pltpu.VMEM((BANDS * 16, LANES), F32)],
        cost_estimate=pl.CostEstimate(flops=300_000, bytes_accessed=800_000, transcendentals=0),
        compiler_params=pltpu.CompilerParams(vmem_limit_bytes=8 * MIB),
        name="regroup",
    )(arrived, obs)


def prepare_kernel(*refs):
    arrived, (source,), (in_rows, in_columns, out_rows, out_columns, target), (arrival,) = (
        refs[:4],
        refs[4:5],
        refs[5:10],
        refs[10:],
    )
    copy = pltpu.make_async_copy(source, target, arrival)
    copy.start()
    code = lax.rem(lax.axis_index("band"), 4)
    filler = jnp.zeros((LANES - 2 * QUARTER, LANES), F32)
    for columns, rows, weight in ((in_columns, in_rows, 0), (out_columns, out_rows, 1)):
        pieces = []
        for t in range(TPS):
            quarters = []
            for wanted in (weight, weight + 2):
                choices = [arrived[wanted ^ own][t, BANDS:SEND_ROWS, :] for own in range(4)]
                choices = [choice.astype(F32)[0:QUARTER] for choice in choices]
                quarters.append(
                    jnp.where(
                        code < 2,
                        jnp.where(code == 0, choices[0], choices[1]),
                        jnp.where(code == 2, choices[2], choices[3]),
                    )
                )
            piece = jnp.concatenate([*quarters, filler], axis=0)
            pieces.append(piece.T[0:REST_LANE])
        upright = jnp.concatenate(pieces, axis=0)
        columns[...] = upright.astype(BF16)
        rows[...] = upright.T[0:80].astype(BF16)
    copy.wait()


def prepare(arrived, turns):
    hidden = TPS * 96
    return pl.pallas_call(
        prepare_kernel,
        out_shape=(
            jax.ShapeDtypeStruct((80, hidden), BF16),
            jax.ShapeDtypeStruct((hidden, LANES), BF16),
            jax.ShapeDtypeStruct((80, hidden), BF16),
            jax.ShapeDtypeStruct((hidden, LANES), BF16),
            jax.ShapeDtypeStruct(turns.shape, turns.dtype),
        ),
        in_specs=[IN_VMEM] * 4 + [IN_HBM],
        out_specs=[IN_VMEM] * 5,
        scratch_shapes=[pltpu.SemaphoreType.DMA],
        cost_estimate=pl.CostEstimate(flops=1_000_000, bytes_accessed=5_000_000, transcendentals=0),
        compiler_params=pltpu.CompilerParams(vmem_limit_bytes=8 * MIB),
        name="prepare",
    )(*arrived, *in_hbm(turns))


GELU_SCALE = math.sqrt(2.0 / math.pi)
GELU_CUBE = 0.044715


def lagrange_rows(offset):
    return (
        -offset * (offset - 1.0) * (offset - 2.0) / 6.0,
        (offset + 1.0) * (offset - 1.0) * (offset - 2.0) / 2.0,
        -(offset + 1.0) * offset * (offset - 2.0) / 2.0,
        (offset + 1.0) * offset * (offset - 1.0) / 6.0,
    )


def cycle_kernel(
    channels,
    arrived,
    prior,
    gains,
    in_rows,
    in_columns,
    out_rows,
    out_columns,
    turns,
    table_high_hbm,
    table_low_hbm,
    wide_high_hbm,
    wide_low_hbm,
    out,
    table_high,
    table_low,
    wide_high,
    wide_low,
    arrivals,
    state,
    slopes,
    obs,
    chosen_all,
    spread_all,
    paired,
):
    orders = turns.shape[1]
    copies = [
        pltpu.make_async_copy(table_high_hbm, table_high, arrivals.at[0]),
        pltpu.make_async_copy(table_low_hbm, table_low, arrivals.at[1]),
        pltpu.make_async_copy(wide_high_hbm, wide_high, arrivals.at[2]),
        pltpu.make_async_copy(wide_low_hbm, wide_low, arrivals.at[3]),
    ]
    for copy in copies:
        copy.start()
    slices = arrived[...].astype(F32)
    rest = slices[:, 8:16, :]
    half = orders // 2
    paired[0:orders, :] = slices[:, 0:8, :].reshape(orders, LANES)
    paired[orders:, :] = rest.reshape(orders, LANES)
    cos_sin = [paired[pl.ds(p, half, stride=2), :] for p in range(2)]
    cos_sin = jnp.concatenate(cos_sin, axis=0).T
    tail = [paired[pl.ds(orders + p, half, stride=2), :] for p in range(2)]
    tail = jnp.concatenate(tail, axis=0).T
    cos_part = cos_sin[0:ROWS]
    sin_part = jnp.concatenate([cos_sin[ROWS:LANES], tail[0:16]], axis=0)
    pairs = rest.reshape(BANDS // 2, 2, FIELDS, LANES)
    near = pltpu.roll(pairs[:, 0].reshape(BANDS // 2 * FIELDS, LANES), LANES - SLOTS, 1)
    near = near.reshape(BANDS // 2, FIELDS, LANES)
    obs[...] = jnp.where(lane_ids(near.shape) < SLOTS, near, pairs[:, 1])

    turned = []
    for a in range(PAIRS):
        turn_cos, turn_sin = turns[a : a + 1, :], turns[4 + a : 5 + a, :]
        turned_cos = cos_part * turn_cos + sin_part * turn_sin
        turned_sin = sin_part * turn_cos - cos_part * turn_sin
        turned.append(
            jnp.concatenate(
                [turned_cos[:, :half], turned_sin[:, :half], turned_cos[:, half:], turned_sin[:, half:]],
                axis=1,
            )
        )
    turned = split(jnp.concatenate(turned, axis=0))
    for copy in copies[:2]:
        copy.wait()
    sums = []
    for p in range(2):
        span = slice(p * orders, (p + 1) * orders)
        part = (turned[0][:, span], turned[1][:, span])
        sums.append(dot3(part, (table_high[span, :], table_low[span, :])))
    field = jnp.concatenate([sums[0] + sums[1], sums[0] - sums[1]], axis=0)
    state[...] = prior[...].reshape(BLOCKS * ROWS, WIDTH) + field

    forecast = []
    for a in range(BLOCKS):
        field = state[a * ROWS : (a + 1) * ROWS, :]
        mean_sq = jnp.sum(field * field, axis=0, keepdims=True) * (1.0 / channels)
        unit = (field * gains[...] * lax.rsqrt(mean_sq + EPSILON)).astype(BF16)
        pre = dot(in_columns[:, 0:ROWS], unit)
        square = pre * pre
        inner = pre * (GELU_SCALE + (GELU_SCALE * GELU_CUBE) * square)
        gate = 0.5 + 0.5 * jnp.tanh(inner)
        hidden = pre * gate
        slopes[a] = gate + hidden * (1.0 - gate) * (
            2.0 * GELU_SCALE + (6.0 * GELU_SCALE * GELU_CUBE) * square
        )
        forecast.append(field + dot(out_rows[...], hidden.astype(BF16))[0:ROWS])
    forecast = split(jnp.concatenate(forecast, axis=0).T)
    forecast = jnp.concatenate(forecast, axis=0)

    per_chunk = OBS_CHUNK // LANES
    chunks = obs.shape[0] // per_chunk
    low_ids = lax.broadcasted_iota(jnp.int32, (16, OBS_CHUNK), 0).astype(F32)
    near_ids = lax.broadcasted_iota(jnp.int32, (32, OBS_CHUNK), 0).astype(F32)
    none = jnp.zeros((16, OBS_CHUNK), BF16)

    def fields_of(chunk):
        fields = [obs[chunk * per_chunk + i] for i in range(per_chunk)]
        return jnp.concatenate(fields, axis=1)

    def choose(chunk):
        row = fields_of(chunk)[6:7] + float(ROW_SHIFT)
        row_group = jnp.floor(row * (1.0 / 16.0))
        first = jnp.where(low_ids == row - 16.0 * row_group, 1.0, 0.0).astype(BF16)
        row_group = jnp.broadcast_to(row_group, (16, OBS_CHUNK)).astype(BF16)
        chosen = jnp.concatenate(
            [
                jnp.where(row_group == jnp.array(float(g), BF16), first, none)
                for g in range(BLOCKS * ROWS // 16)
            ],
            axis=0,
        )
        chosen_all[:, chunk * OBS_CHUNK : (chunk + 1) * OBS_CHUNK] = chosen
        return chosen

    def observe(chunk, picked):
        fields = fields_of(chunk)
        columns = slice(chunk * OBS_CHUNK, (chunk + 1) * OBS_CHUNK)
        value = fields[0:1] + fields[1:2]
        weight = fields[2:3] + fields[3:4]
        offset = fields[4:5] + fields[5:6]
        group = jnp.floor(fields[7:8] * (1.0 / 16.0))
        place = near_ids - (fields[7:8] - 16.0 * group)
        group8 = jnp.broadcast_to(group, (8, OBS_CHUNK))
        window = [jnp.zeros((8, OBS_CHUNK), F32)] * 4
        for g in range(WIDTH // 16 - 1):
            mask = group8 == float(g)
            for i in range(4):
                rows = slice(16 * g + 8 * i, 16 * g + 8 * i + 8)
                window[i] = jnp.where(mask, picked[rows] + picked[WIDTH:][rows], window[i])
        window = jnp.concatenate(window, axis=0)
        w_left, w_here, w_right, w_far = lagrange_rows(offset)
        stencil = jnp.where(
            place == 0.0,
            w_left,
            jnp.where(
                place == 1.0,
                w_here,
                jnp.where(place == 2.0, w_right, jnp.where(place == 3.0, w_far, 0.0)),
            ),
        )
        reading = jnp.sum(stencil * window, axis=0, keepdims=True)
        parts = split(stencil * (weight * (reading - value)))
        group = jnp.broadcast_to(group, (16, OBS_CHUNK)).astype(BF16)
        masks = [group == jnp.array(float(g), BF16) for g in range(WIDTH // 16 - 1)]
        for i, part in enumerate(parts):
            pieces = []
            for g in range(WIDTH // 16):
                piece = none
                if g > 0:
                    piece = jnp.where(masks[g - 1], part[16:32], piece)
                if g < WIDTH // 16 - 1:
                    piece = jnp.where(masks[g], part[0:16], piece)
                pieces.append(piece)
            spread_all[i * WIDTH : (i + 1) * WIDTH, columns] = jnp.concatenate(pieces, axis=0)

    chosen = choose(0)
    picked = None
    for chunk in range(chunks):
        latest = dot(forecast, chosen)
        if chunk + 1 < chunks:
            chosen = choose(chunk + 1)
        if chunk > 0:
            observe(chunk - 1, picked)
        picked = latest
    observe(chunks - 1, picked)
    forcing = dot(spread_all[...], chosen_all[...], NT)
    forcing = (forcing[0:WIDTH] + forcing[WIDTH:]).T

    lanes = lane_ids((BLOCKS * ROWS, WIDTH))
    halo = pltpu.roll(forcing, WIDTH - STRIDE, 1)
    halo = jnp.concatenate([halo[(BLOCKS - 1) * ROWS :], halo[: (BLOCKS - 1) * ROWS]], axis=0)
    forcing = jnp.where(lanes < STRIDE, forcing, 0.0) + jnp.where(lanes < 3, halo, 0.0)
    costate = []
    for a in range(BLOCKS):
        force = forcing[a * ROWS : (a + 1) * ROWS]
        grad_hidden = dot(out_columns[:, 0:ROWS], force.astype(BF16))
        grad_pre = (grad_hidden * slopes[a]).astype(BF16)
        grad_unit = dot(in_rows[...], grad_pre)[0:ROWS]
        field = state[a * ROWS : (a + 1) * ROWS, :]
        mean_sq = jnp.sum(field * field, axis=0, keepdims=True) * (1.0 / channels)
        inverse = lax.rsqrt(mean_sq + EPSILON)
        scaled = grad_unit * gains[...]
        along = jnp.sum(scaled * field, axis=0, keepdims=True) * (1.0 / channels)
        costate.append(force + scaled * inverse - field * (along * inverse * inverse * inverse))
    near = jnp.concatenate(costate[:PAIRS], axis=0)
    far = jnp.concatenate(costate[PAIRS:], axis=0)
    for copy in copies[2:]:
        copy.wait()
    pad = jnp.zeros((LANES - ROWS, half), F32)
    lanes = lane_ids((half, LANES))
    for p, both in enumerate((near + far, near - far)):
        span = slice(p * orders, (p + 1) * orders)
        blocks = dot3(split(both), (wide_high[:, span], wide_low[:, span]))
        grads = [jnp.zeros((ROWS, half), F32)] * 2
        for a in range(PAIRS):
            turn_cos = turns[a : a + 1, p * half : (p + 1) * half]
            turn_sin = turns[4 + a : 5 + a, p * half : (p + 1) * half]
            block = blocks[a * ROWS : (a + 1) * ROWS]
            block_cos, block_sin = block[:, :half], block[:, half:]
            grads[0] = grads[0] + turn_cos * block_cos - turn_sin * block_sin
            grads[1] = grads[1] + turn_sin * block_cos + turn_cos * block_sin
        for r in range(2):
            upright = jnp.concatenate([grads[r], pad], axis=0).T
            high = upright.astype(BF16).astype(F32)
            low = pltpu.roll(upright - high, channels, 1)
            place = pl.ds(2 * p + r, half, stride=4)
            paired[place, :] = jnp.where(lanes < channels, high, low)
    out[...] = paired[...].astype(BF16)


def run_cycle(channels, arrived, prior, gains, prepared, table):
    orders = prepared[4].shape[1]
    hidden = prepared[1].shape[0]
    return pl.pallas_call(
        lambda *refs: cycle_kernel(channels, *refs),
        out_shape=jax.ShapeDtypeStruct((2 * orders, LANES), BF16),
        in_specs=[IN_VMEM] * 8 + [IN_HBM] * 4,
        out_specs=IN_VMEM,
        scratch_shapes=[
            *(pltpu.VMEM(part.shape, BF16) for part in table),
            pltpu.SemaphoreType.DMA((4,)),
            pltpu.VMEM((BLOCKS * ROWS, WIDTH), F32),
            pltpu.VMEM((BLOCKS, hidden, WIDTH), F32),
            pltpu.VMEM((BANDS // 2, FIELDS, LANES), F32),
            pltpu.VMEM((BLOCKS * ROWS, BANDS * SLOTS), BF16),
            pltpu.VMEM((2 * WIDTH, BANDS * SLOTS), BF16),
            pltpu.VMEM((2 * orders, LANES), F32),
        ],
        compiler_params=pltpu.CompilerParams(vmem_limit_bytes=36 * MIB),
        cost_estimate=pl.CostEstimate(
            flops=8_000_000_000, bytes_accessed=4_000_000, transcendentals=1_200_000
        ),
        name="cycle",
    )(arrived, prior, gains, *prepared, *in_hbm(*table))


def analysis_kernel(parity, arrived, control, sigma, table_high, table_low, out, rows):
    channels = sigma.shape[0]
    orders = arrived.shape[0] // 2
    rows[...] = arrived[...].astype(F32)
    lanes = lane_ids((orders, LANES))
    for r in range(2):
        both = rows[pl.ds(r, orders, stride=2), :]
        low = pltpu.roll(both, LANES - channels, 1)
        grad = jnp.where(lanes < channels, both, 0.0)
        grad = grad + jnp.where(lanes < LANES - channels, low, 0.0)
        grad_t = split(grad.T[0:ROWS])
        projected = dot3(grad_t, (table_high[0], table_low[0]))
        out[:, r, 0, :] = control[:, r, 0, :] + sigma[:, 0, :] * projected[0:channels]


def analysis(parity, arrived, control, sigma, table):
    wave_count = table[0].shape[2]
    lat_count = table[0].shape[1]
    whole = lambda shape: pl.BlockSpec(shape, lambda i, p: (0,) * len(shape))
    chosen = pl.BlockSpec((1, lat_count, wave_count), lambda i, p: (p[0], 0, 0))
    return pl.pallas_call(
        analysis_kernel,
        out_shape=jax.ShapeDtypeStruct(control.shape, F32),
        grid_spec=pltpu.PrefetchScalarGridSpec(
            num_scalar_prefetch=1,
            grid=(1,),
            in_specs=[
                whole(arrived.shape),
                whole(control.shape),
                whole(sigma.shape),
                chosen,
                chosen,
            ],
            out_specs=whole(control.shape),
            scratch_shapes=[pltpu.VMEM(arrived.shape, F32)],
        ),
        cost_estimate=pl.CostEstimate(flops=400_000_000, bytes_accessed=2_000_000, transcendentals=0),
        compiler_params=pltpu.CompilerParams(vmem_limit_bytes=12 * MIB),
        name="analysis",
    )(parity, arrived, control, sigma, *table)


def shards(
    control,
    spec_sigma,
    prior_mean_field,
    magnitude_factor,
    w_in,
    w_out,
    obs_band,
    obs_cell,
    obs_value,
    obs_weight,
    obs_offset,
):
    channels, _, _, wave_count = control.shape
    lat_count = BANDS * TPS
    lon_count = prior_mean_field.shape[2]
    legendre = legendre_np(wave_count, lat_count)
    zonal = zonal_np(lat_count, lon_count)
    turns = turn_np(lat_count, lon_count)
    parity = (lax.axis_index("tp") % 2).astype(jnp.int32).reshape(1)
    send = synthesis(control, spec_sigma, w_in, w_out.T, legendre)
    got = lax.all_to_all(send, "tp", split_axis=0, concat_axis=0, tiled=True)
    obs = pack_obs(
        *(
            field.reshape(-1, LANES)
            for field in (obs_band, obs_cell, obs_value, obs_weight, obs_offset)
        )
    )
    send = regroup(got, obs).reshape(BANDS, 16, LANES)
    arrived = lax.all_to_all(send, "band", split_axis=0, concat_axis=0, tiled=True)
    others = [
        lax.ppermute(got, "band", [(i, i ^ flip) for i in range(BANDS)]) for flip in (1, 2, 3)
    ]
    prepared = prepare([got, *others], turns)
    prior = jnp.pad(prior_mean_field[:, 0, :], ((0, ROWS - channels), (0, 0)))
    prior = jnp.concatenate([prior, prior[:, : WIDTH - STRIDE]], axis=1)
    prior = jnp.stack([prior[:, a * STRIDE : a * STRIDE + WIDTH] for a in range(BLOCKS)])
    gains = jnp.broadcast_to(
        jnp.pad(magnitude_factor, (0, ROWS - channels))[:, None], (ROWS, WIDTH)
    )
    modes = run_cycle(channels, arrived, prior, gains, prepared, zonal)
    modes = lax.all_to_all(
        modes.reshape(lat_count, 2, LANES),
        ("band", "tp"),
        split_axis=0,
        concat_axis=0,
        tiled=True,
    )
    modes = modes.reshape(2 * lat_count, LANES)
    return analysis(parity, modes, control, spec_sigma, legendre)


def solution(mesh):
    placed = (
        P(None, None, ("band", "tp"), None),
        P(None, ("band", "tp"), None),
        P(None, ("band", "tp"), None),
        P(),
        P(None, "tp"),
        P("tp", None),
        P("band", "tp", None, None),
        P("band", "tp", None),
        P("band", "tp", None),
        P("band", "tp", None),
        P("band", "tp", None),
    )
    return jax.shard_map(
        shards,
        mesh=mesh,
        in_specs=placed,
        out_specs=P(None, None, ("band", "tp"), None),
        check_vma=False,
    )
```

```python
import math

import jax
import jax.numpy as jnp
import ml_dtypes
import numpy as np
from jax import lax
from jax.experimental import pallas as pl
from jax.experimental.pallas import tpu as pltpu
from jax.sharding import PartitionSpec as P

EPSILON = 1e-06
BF16 = jnp.bfloat16
F32 = jnp.float32

BLOCKS = 6
PAIRS = BLOCKS // 2
STRIDE = 240
WIDTH = 256
ROWS = 72
LANES = 128
BANDS = 64
TPS = 8
SLOTS = 64
FIELDS = 8
ROW_SHIFT = 256
OBS_CHUNK = 512
MIB = 1024 * 1024


def split_np(table):
    high = table.astype(np.float32).astype(ml_dtypes.bfloat16)
    low = (table - high.astype(np.float64)).astype(np.float32).astype(ml_dtypes.bfloat16)
    return high, low


def legendre_np(wave_count, lat_count):
    cycles = np.arange(lat_count)
    tables = []
    for parity in range(2):
        frequency = np.arange(wave_count) + parity
        phases = (2 * cycles[:, None] + 1) * frequency[None, :] % (4 * lat_count)
        angles = phases * (math.pi / (2 * lat_count))
        basis = np.sin(angles) if parity else np.cos(angles)
        tables.append(basis * math.sqrt(2.0 / lat_count))
    return split_np(np.stack(tables))


def even_odd_np(orders):
    return np.concatenate([np.arange(0, orders, 2), np.arange(1, orders, 2)])


def zonal_np(orders, lon_count):
    phases = even_odd_np(orders)[:, None] * np.arange(WIDTH)[None, :] % lon_count
    angles = phases * (2.0 * math.pi / lon_count)
    halves = angles.reshape(2, 1, orders // 2, WIDTH)
    parts = np.concatenate([np.cos(halves), np.sin(halves)], axis=1)
    high, low = split_np(parts.reshape(2 * orders, WIDTH))
    return high, low, np.ascontiguousarray(high.T), np.ascontiguousarray(low.T)


def turn_np(orders, lon_count):
    phases = np.arange(PAIRS)[:, None] * STRIDE * even_odd_np(orders)[None, :] % lon_count
    angles = phases * (2.0 * math.pi / lon_count)
    pad = np.zeros((4 - PAIRS, orders))
    return np.concatenate([np.cos(angles), pad, np.sin(angles), pad]).astype(np.float32)


def split(values):
    high = values.astype(BF16)
    low = (values - high.astype(F32)).astype(BF16)
    return high, low


NN = (((1,), (0,)), ((), ()))
NT = (((1,), (1,)), ((), ()))


def dot(left, right, dims=NN):
    return lax.dot_general(left, right, dims, preferred_element_type=F32)


def dot3(left, right, dims=NN):
    return (
        dot(left[0], right[0], dims) + dot(left[0], right[1], dims) + dot(left[1], right[0], dims)
    )


def lane_ids(shape):
    return lax.broadcasted_iota(jnp.int32, shape, len(shape) - 1)


SEND_ROWS = 128
REST_LANE = 96
PIECE_LANE = 112


def synthesis_kernel(
    control_hbm,
    sigma_hbm,
    high_hbm,
    low_hbm,
    w_in_hbm,
    w_out_hbm,
    out,
    control,
    sigma,
    table_high,
    table_low,
    w_in,
    w_out,
    coef,
    modes,
    arrivals,
):
    parity = lax.rem(lax.axis_index("tp"), 2)
    copies = [
        pltpu.make_async_copy(source, target, arrivals.at[i])
        for i, (source, target) in enumerate(
            (
                (control_hbm, control),
                (sigma_hbm, sigma),
                (high_hbm.at[parity], table_high),
                (low_hbm.at[parity], table_low),
                (w_in_hbm, w_in),
                (w_out_hbm, w_out),
            )
        )
    ]
    for copy in copies:
        copy.start()
    channels = sigma.shape[0]
    coef[...] = jnp.zeros_like(coef)
    copies[0].wait()
    copies[1].wait()
    deviation = sigma[:, 0, :]
    first = deviation * control[:, 0, 0, :]
    second = deviation * control[:, 1, 0, :]
    coef[0:channels, :] = first
    coef[ROWS:LANES, :] = second[: LANES - ROWS]
    tail = channels - (LANES - ROWS)
    coef[LANES + REST_LANE : LANES + REST_LANE + tail, :] = second[LANES - ROWS :]
    parts = split(coef[...])
    for copy in copies[2:]:
        copy.wait()
    whole = dot3((table_high[...], table_low[...]), parts, NT)
    modes[0] = whole[:, 0:LANES]
    modes[1] = whole[:, LANES:]
    even = lax.rem(lax.axis_index("band"), 2) == 0
    rows = jnp.where(even, w_in[...].astype(F32), w_out[...].astype(F32))
    rows = jnp.pad(rows, ((0, ROWS - channels), (0, LANES - rows.shape[1])))
    lanes = lane_ids((8, LANES))
    pieces = [
        jnp.where(
            lanes >= PIECE_LANE,
            pltpu.roll(rows[BANDS:ROWS], PIECE_LANE - start, 1),
            rows[start // 2 : start // 2 + 8],
        )
        for start in range(0, REST_LANE, 16)
    ]
    rows = jnp.concatenate([*pieces, rows[REST_LANE // 2 : BANDS]], axis=0)
    for dest in range(TPS):
        out[dest, 0:BANDS, :] = modes[0, pl.ds(dest, BANDS, stride=TPS), :].astype(BF16)
        rest = modes[1, pl.ds(dest, BANDS, stride=TPS), :]
        out[dest, BANDS:SEND_ROWS, :] = (rest + rows).astype(BF16)


def in_hbm(*arrays):
    return tuple(pltpu.with_memory_space_constraint(jnp.asarray(a), pltpu.HBM) for a in arrays)


IN_VMEM = pl.BlockSpec(memory_space=pltpu.VMEM)
IN_HBM = pl.BlockSpec(memory_space=pltpu.HBM)


def synthesis(control, sigma, w_in, w_out_t, table):
    lat_count, wave_count = table[0].shape[1:]
    return pl.pallas_call(
        synthesis_kernel,
        out_shape=jax.ShapeDtypeStruct((TPS, SEND_ROWS, LANES), BF16),
        in_specs=[IN_HBM] * 6,
        out_specs=IN_VMEM,
        scratch_shapes=[
            pltpu.VMEM(control.shape, F32),
            pltpu.VMEM(sigma.shape, F32),
            pltpu.VMEM((lat_count, wave_count), BF16),
            pltpu.VMEM((lat_count, wave_count), BF16),
            pltpu.VMEM(w_in.shape, BF16),
            pltpu.VMEM(w_in.shape, BF16),
            pltpu.VMEM((2 * LANES, wave_count), F32),
            pltpu.VMEM((2, lat_count, LANES), F32),
            pltpu.SemaphoreType.DMA((6,)),
        ],
        cost_estimate=pl.CostEstimate(flops=400_000_000, bytes_accessed=2_000_000, transcendentals=0),
        compiler_params=pltpu.CompilerParams(vmem_limit_bytes=12 * MIB),
        name="synthesis",
    )(*in_hbm(control, sigma, *table, w_in, w_out_t))


def pack_kernel(band, cell, value, weight, offset, out):
    blocks = band.shape[0]
    cells = cell[...].astype(F32)
    channel = jnp.floor((cells + 0.5) * (1.0 / 1440.0))
    start = cells - 1440.0 * channel - 1.0
    start = jnp.where(start < 0.0, start + 1440.0, start)
    part = jnp.floor((start + 0.5) * (1.0 / STRIDE))
    fields = []
    for source in (value, weight, offset):
        high = source[...].astype(BF16).astype(F32)
        fields += [high, source[...] - high]
    fields += [part * ROWS + channel - ROW_SHIFT, start - part * STRIDE]
    band_ids = lax.broadcasted_iota(jnp.int32, (BANDS, LANES), 0)
    hits = [band_ids == band[i : i + 1, :] for i in range(blocks)]
    ones = [jnp.where(hit, 1.0, 0.0) for hit in hits]
    square = (LANES, 2 * LANES)
    row, column = lax.broadcasted_iota(jnp.int32, square, 0), lane_ids(square)
    before = jnp.where((row < column) | (column >= LANES), 1.0, 0.0).astype(BF16)
    counts = dot(jnp.concatenate(ones, axis=0).astype(BF16), before)
    slot_ids = lax.broadcasted_iota(jnp.int32, (LANES, LANES), 0).astype(F32)
    taken = jnp.zeros((BANDS, LANES), F32)
    total = jnp.zeros((BANDS, FIELDS * LANES), F32)
    for i in range(blocks):
        within = counts[i * BANDS : (i + 1) * BANDS, :]
        rank = jnp.sum(ones[i] * (within[:, :LANES] + taken), axis=0, keepdims=True)
        taken = taken + within[:, LANES:]
        here = slot_ids == rank + (LANES - SLOTS)
        spread = [jnp.where(here, field[i : i + 1, :], 0.0).astype(BF16) for field in fields]
        total = total + dot(ones[i].astype(BF16), jnp.concatenate(spread, axis=0), NT)
    out[...] = total


def pack_obs(band, cell, value, weight, offset):
    return pl.pallas_call(
        pack_kernel,
        out_shape=jax.ShapeDtypeStruct((BANDS, FIELDS * LANES), F32),
        cost_estimate=pl.CostEstimate(flops=200_000_000, bytes_accessed=300_000, transcendentals=0),
        compiler_params=pltpu.CompilerParams(vmem_limit_bytes=8 * MIB),
        name="pack_obs",
    )(band, cell, value, weight, offset)


def regroup_kernel(arrived, obs, out, rows):
    lanes = lane_ids((BANDS, LANES))
    for t in range(TPS):
        rows[pl.ds(t, BANDS, stride=16), :] = arrived[t, 0:BANDS, :].astype(F32)
        rest = pltpu.roll(arrived[t, BANDS : 2 * BANDS, :].astype(F32), LANES - REST_LANE, 1)
        rest = jnp.where(lanes < 16, rest, obs[:, t * LANES : (t + 1) * LANES])
        rows[pl.ds(8 + t, BANDS, stride=16), :] = rest
    out[...] = rows[...].astype(BF16)


def regroup(arrived, obs):
    return pl.pallas_call(
        regroup_kernel,
        out_shape=jax.ShapeDtypeStruct((BANDS * 16, LANES), BF16),
        scratch_shapes=[pltpu.VMEM((BANDS * 16, LANES), F32)],
        cost_estimate=pl.CostEstimate(flops=300_000, bytes_accessed=800_000, transcendentals=0),
        compiler_params=pltpu.CompilerParams(vmem_limit_bytes=8 * MIB),
        name="regroup",
    )(arrived, obs)


def prepare_kernel(own, other, *refs):
    sources, (in_rows, in_columns, out_rows, out_columns, *targets), (arrivals,) = (
        refs[:3],
        refs[3:10],
        refs[10:],
    )
    copies = [
        pltpu.make_async_copy(source, target, arrivals.at[i])
        for i, (source, target) in enumerate(zip(sources, targets))
    ]
    for copy in copies:
        copy.start()
    even = lax.rem(lax.axis_index("band"), 2) == 0
    lanes = lane_ids((8, LANES))
    filler = jnp.zeros((LANES - ROWS, LANES), F32)
    for columns, rows, first in ((in_columns, in_rows, True), (out_columns, out_rows, False)):
        pieces = []
        for t in range(TPS):
            mine = own[t, BANDS:SEND_ROWS, :].astype(F32)
            theirs = other[t, BANDS:SEND_ROWS, :].astype(F32)
            piece = jnp.where(even == first, mine, theirs)
            last = jnp.zeros((8, LANES), F32)
            for start in range(0, REST_LANE, 16):
                part = piece[start // 2 : start // 2 + 8]
                part = pltpu.roll(part, LANES - PIECE_LANE + start, 1)
                last = jnp.where((lanes >= start) & (lanes < start + 16), part, last)
            piece = jnp.concatenate([piece, last, filler], axis=0)
            pieces.append(piece.T[0:REST_LANE])
        upright = jnp.concatenate(pieces, axis=0)
        columns[...] = upright.astype(BF16)
        rows[...] = upright.T[0:80].astype(BF16)
    for copy in copies:
        copy.wait()


def prepare(own, other, tables):
    hidden = TPS * 96
    return pl.pallas_call(
        prepare_kernel,
        out_shape=(
            jax.ShapeDtypeStruct((80, hidden), BF16),
            jax.ShapeDtypeStruct((hidden, LANES), BF16),
            jax.ShapeDtypeStruct((80, hidden), BF16),
            jax.ShapeDtypeStruct((hidden, LANES), BF16),
            *(jax.ShapeDtypeStruct(table.shape, table.dtype) for table in tables),
        ),
        in_specs=[IN_VMEM] * 2 + [IN_HBM] * 3,
        out_specs=[IN_VMEM] * 7,
        scratch_shapes=[pltpu.SemaphoreType.DMA((3,))],
        cost_estimate=pl.CostEstimate(flops=1_000_000, bytes_accessed=5_000_000, transcendentals=0),
        compiler_params=pltpu.CompilerParams(vmem_limit_bytes=8 * MIB),
        name="prepare",
    )(own, other, *in_hbm(*tables))


GELU_SCALE = math.sqrt(2.0 / math.pi)
GELU_CUBE = 0.044715


def lagrange_rows(offset):
    return (
        -offset * (offset - 1.0) * (offset - 2.0) / 6.0,
        (offset + 1.0) * (offset - 1.0) * (offset - 2.0) / 2.0,
        -(offset + 1.0) * offset * (offset - 2.0) / 2.0,
        (offset + 1.0) * offset * (offset - 1.0) / 6.0,
    )


def cycle_kernel(
    channels,
    arrived,
    gains,
    in_rows,
    in_columns,
    out_rows,
    out_columns,
    turns,
    table_high,
    table_low,
    prior_hbm,
    wide_high_hbm,
    wide_low_hbm,
    out,
    prior,
    wide_high,
    wide_low,
    arrivals,
    state,
    slopes,
    obs,
    chosen_all,
    spread_all,
    paired,
):
    orders = turns.shape[1]
    copies = [
        pltpu.make_async_copy(prior_hbm, prior, arrivals.at[0]),
        pltpu.make_async_copy(wide_high_hbm, wide_high, arrivals.at[1]),
        pltpu.make_async_copy(wide_low_hbm, wide_low, arrivals.at[2]),
    ]
    for copy in copies:
        copy.start()
    slices = arrived[...].astype(F32)
    rest = slices[:, 8:16, :]
    half = orders // 2
    paired[0:orders, :] = slices[:, 0:8, :].reshape(orders, LANES)
    paired[orders:, :] = rest.reshape(orders, LANES)
    cos_sin = [paired[pl.ds(p, half, stride=2), :] for p in range(2)]
    cos_sin = jnp.concatenate(cos_sin, axis=0).T
    tail = [paired[pl.ds(orders + p, half, stride=2), :] for p in range(2)]
    tail = jnp.concatenate(tail, axis=0).T
    cos_part = cos_sin[0:ROWS]
    sin_part = jnp.concatenate([cos_sin[ROWS:LANES], tail[0:16]], axis=0)
    pairs = rest.reshape(BANDS // 2, 2, FIELDS, LANES)
    near = pltpu.roll(pairs[:, 0].reshape(BANDS // 2 * FIELDS, LANES), LANES - SLOTS, 1)
    near = near.reshape(BANDS // 2, FIELDS, LANES)
    obs[...] = jnp.where(lane_ids(near.shape) < SLOTS, near, pairs[:, 1])

    turned = []
    for a in range(PAIRS):
        turn_cos, turn_sin = turns[a : a + 1, :], turns[4 + a : 5 + a, :]
        turned_cos = cos_part * turn_cos + sin_part * turn_sin
        turned_sin = sin_part * turn_cos - cos_part * turn_sin
        turned.append(
            jnp.concatenate(
                [turned_cos[:, :half], turned_sin[:, :half], turned_cos[:, half:], turned_sin[:, half:]],
                axis=1,
            )
        )
    turned = split(jnp.concatenate(turned, axis=0))
    sums = []
    for p in range(2):
        span = slice(p * orders, (p + 1) * orders)
        part = (turned[0][:, span], turned[1][:, span])
        sums.append(dot3(part, (table_high[span, :], table_low[span, :])))
    field = jnp.concatenate([sums[0] + sums[1], sums[0] - sums[1]], axis=0)
    copies[0].wait()
    state[...] = prior[...].reshape(BLOCKS * ROWS, WIDTH) + field

    forecast = []
    for a in range(BLOCKS):
        field = state[a * ROWS : (a + 1) * ROWS, :]
        mean_sq = jnp.sum(field * field, axis=0, keepdims=True) * (1.0 / channels)
        unit = (field * gains[...] * lax.rsqrt(mean_sq + EPSILON)).astype(BF16)
        pre = dot(in_columns[:, 0:ROWS], unit)
        square = pre * pre
        inner = pre * (GELU_SCALE + (GELU_SCALE * GELU_CUBE) * square)
        gate = 0.5 + 0.5 * jnp.tanh(inner)
        hidden = pre * gate
        slopes[a] = gate + hidden * (1.0 - gate) * (
            2.0 * GELU_SCALE + (6.0 * GELU_SCALE * GELU_CUBE) * square
        )
        forecast.append(field + dot(out_rows[...], hidden.astype(BF16))[0:ROWS])
    forecast = split(jnp.concatenate(forecast, axis=0).T)
    forecast = jnp.concatenate(forecast, axis=0)

    per_chunk = OBS_CHUNK // LANES
    chunks = obs.shape[0] // per_chunk
    low_ids = lax.broadcasted_iota(jnp.int32, (16, OBS_CHUNK), 0).astype(F32)
    near_ids = lax.broadcasted_iota(jnp.int32, (32, OBS_CHUNK), 0).astype(F32)
    none = jnp.zeros((16, OBS_CHUNK), BF16)

    def fields_of(chunk):
        fields = [obs[chunk * per_chunk + i] for i in range(per_chunk)]
        return jnp.concatenate(fields, axis=1)

    def choose(chunk):
        row = fields_of(chunk)[6:7] + float(ROW_SHIFT)
        row_group = jnp.floor(row * (1.0 / 16.0))
        first = jnp.where(low_ids == row - 16.0 * row_group, 1.0, 0.0).astype(BF16)
        row_group = jnp.broadcast_to(row_group, (16, OBS_CHUNK)).astype(BF16)
        chosen = jnp.concatenate(
            [
                jnp.where(row_group == jnp.array(float(g), BF16), first, none)
                for g in range(BLOCKS * ROWS // 16)
            ],
            axis=0,
        )
        chosen_all[:, chunk * OBS_CHUNK : (chunk + 1) * OBS_CHUNK] = chosen
        return chosen

    def observe(chunk, picked):
        fields = fields_of(chunk)
        columns = slice(chunk * OBS_CHUNK, (chunk + 1) * OBS_CHUNK)
        value = fields[0:1] + fields[1:2]
        weight = fields[2:3] + fields[3:4]
        offset = fields[4:5] + fields[5:6]
        group = jnp.floor(fields[7:8] * (1.0 / 16.0))
        place = near_ids - (fields[7:8] - 16.0 * group)
        group8 = jnp.broadcast_to(group, (8, OBS_CHUNK))
        window = [jnp.zeros((8, OBS_CHUNK), F32)] * 4
        for g in range(WIDTH // 16 - 1):
            mask = group8 == float(g)
            for i in range(4):
                rows = slice(16 * g + 8 * i, 16 * g + 8 * i + 8)
                window[i] = jnp.where(mask, picked[rows] + picked[WIDTH:][rows], window[i])
        window = jnp.concatenate(window, axis=0)
        w_left, w_here, w_right, w_far = lagrange_rows(offset)
        stencil = jnp.where(
            place == 0.0,
            w_left,
            jnp.where(
                place == 1.0,
                w_here,
                jnp.where(place == 2.0, w_right, jnp.where(place == 3.0, w_far, 0.0)),
            ),
        )
        reading = jnp.sum(stencil * window, axis=0, keepdims=True)
        parts = split(stencil * (weight * (reading - value)))
        group = jnp.broadcast_to(group, (16, OBS_CHUNK)).astype(BF16)
        masks = [group == jnp.array(float(g), BF16) for g in range(WIDTH // 16 - 1)]
        for i, part in enumerate(parts):
            pieces = []
            for g in range(WIDTH // 16):
                piece = none
                if g > 0:
                    piece = jnp.where(masks[g - 1], part[16:32], piece)
                if g < WIDTH // 16 - 1:
                    piece = jnp.where(masks[g], part[0:16], piece)
                pieces.append(piece)
            spread_all[i * WIDTH : (i + 1) * WIDTH, columns] = jnp.concatenate(pieces, axis=0)

    chosen = choose(0)
    picked = None
    for chunk in range(chunks):
        latest = dot(forecast, chosen)
        if chunk + 1 < chunks:
            chosen = choose(chunk + 1)
        if chunk > 0:
            observe(chunk - 1, picked)
        picked = latest
    observe(chunks - 1, picked)
    forcing = dot(spread_all[...], chosen_all[...], NT)
    forcing = (forcing[0:WIDTH] + forcing[WIDTH:]).T

    lanes = lane_ids((BLOCKS * ROWS, WIDTH))
    halo = pltpu.roll(forcing, WIDTH - STRIDE, 1)
    halo = jnp.concatenate([halo[(BLOCKS - 1) * ROWS :], halo[: (BLOCKS - 1) * ROWS]], axis=0)
    forcing = jnp.where(lanes < STRIDE, forcing, 0.0) + jnp.where(lanes < 3, halo, 0.0)
    costate = []
    for a in range(BLOCKS):
        force = forcing[a * ROWS : (a + 1) * ROWS]
        grad_hidden = dot(out_columns[:, 0:ROWS], force.astype(BF16))
        grad_pre = (grad_hidden * slopes[a]).astype(BF16)
        grad_unit = dot(in_rows[...], grad_pre)[0:ROWS]
        field = state[a * ROWS : (a + 1) * ROWS, :]
        mean_sq = jnp.sum(field * field, axis=0, keepdims=True) * (1.0 / channels)
        inverse = lax.rsqrt(mean_sq + EPSILON)
        scaled = grad_unit * gains[...]
        along = jnp.sum(scaled * field, axis=0, keepdims=True) * (1.0 / channels)
        costate.append(force + scaled * inverse - field * (along * inverse * inverse * inverse))
    near = jnp.concatenate(costate[:PAIRS], axis=0)
    far = jnp.concatenate(costate[PAIRS:], axis=0)
    for copy in copies[1:]:
        copy.wait()
    pad = jnp.zeros((LANES - ROWS, half), F32)
    lanes = lane_ids((half, LANES))
    for p, both in enumerate((near + far, near - far)):
        span = slice(p * orders, (p + 1) * orders)
        blocks = dot3(split(both), (wide_high[:, span], wide_low[:, span]))
        grads = [jnp.zeros((ROWS, half), F32)] * 2
        for a in range(PAIRS):
            turn_cos = turns[a : a + 1, p * half : (p + 1) * half]
            turn_sin = turns[4 + a : 5 + a, p * half : (p + 1) * half]
            block = blocks[a * ROWS : (a + 1) * ROWS]
            block_cos, block_sin = block[:, :half], block[:, half:]
            grads[0] = grads[0] + turn_cos * block_cos - turn_sin * block_sin
            grads[1] = grads[1] + turn_sin * block_cos + turn_cos * block_sin
        for r in range(2):
            upright = jnp.concatenate([grads[r], pad], axis=0).T
            high = upright.astype(BF16).astype(F32)
            low = pltpu.roll(upright - high, channels, 1)
            place = pl.ds(2 * p + r, half, stride=4)
            paired[place, :] = jnp.where(lanes < channels, high, low)
    out[...] = paired[...].astype(BF16)


def run_cycle(channels, arrived, prior, gains, prepared, wide):
    orders = prepared[4].shape[1]
    hidden = prepared[1].shape[0]
    return pl.pallas_call(
        lambda *refs: cycle_kernel(channels, *refs),
        out_shape=jax.ShapeDtypeStruct((2 * orders, LANES), BF16),
        in_specs=[IN_VMEM] * 9 + [IN_HBM] * 3,
        out_specs=IN_VMEM,
        scratch_shapes=[
            pltpu.VMEM(prior.shape, F32),
            *(pltpu.VMEM(part.shape, BF16) for part in wide),
            pltpu.SemaphoreType.DMA((3,)),
            pltpu.VMEM((BLOCKS * ROWS, WIDTH), F32),
            pltpu.VMEM((BLOCKS, hidden, WIDTH), F32),
            pltpu.VMEM((BANDS // 2, FIELDS, LANES), F32),
            pltpu.VMEM((BLOCKS * ROWS, BANDS * SLOTS), BF16),
            pltpu.VMEM((2 * WIDTH, BANDS * SLOTS), BF16),
            pltpu.VMEM((2 * orders, LANES), F32),
        ],
        compiler_params=pltpu.CompilerParams(vmem_limit_bytes=36 * MIB),
        cost_estimate=pl.CostEstimate(
            flops=8_000_000_000, bytes_accessed=4_000_000, transcendentals=1_200_000
        ),
        name="cycle",
    )(arrived, gains, *prepared, *in_hbm(prior, *wide))


def analysis_kernel(arrived, control, sigma, table_high, table_low, out, rows):
    parity = lax.rem(lax.axis_index("tp"), 2)
    channels = sigma.shape[0]
    orders = arrived.shape[0] // 2
    rows[...] = arrived[...].astype(F32)
    lanes = lane_ids((orders, LANES))
    for r in range(2):
        both = rows[pl.ds(r, orders, stride=2), :]
        low = pltpu.roll(both, LANES - channels, 1)
        grad = jnp.where(lanes < channels, both, 0.0)
        grad = grad + jnp.where(lanes < LANES - channels, low, 0.0)
        grad_t = split(grad.T[0:ROWS])
        projected = dot3(grad_t, (table_high[parity], table_low[parity]))
        out[:, r, 0, :] = control[:, r, 0, :] + sigma[:, 0, :] * projected[0:channels]


def analysis(arrived, control, sigma, table):
    return pl.pallas_call(
        analysis_kernel,
        out_shape=jax.ShapeDtypeStruct(control.shape, F32),
        scratch_shapes=[pltpu.VMEM(arrived.shape, F32)],
        cost_estimate=pl.CostEstimate(flops=400_000_000, bytes_accessed=2_000_000, transcendentals=0),
        compiler_params=pltpu.CompilerParams(vmem_limit_bytes=12 * MIB),
        name="analysis",
    )(arrived, control, sigma, *table)


def shards(
    control,
    spec_sigma,
    prior_mean_field,
    magnitude_factor,
    w_in,
    w_out,
    obs_band,
    obs_cell,
    obs_value,
    obs_weight,
    obs_offset,
):
    channels, _, _, wave_count = control.shape
    lat_count = BANDS * TPS
    lon_count = prior_mean_field.shape[2]
    legendre = legendre_np(wave_count, lat_count)
    zonal = zonal_np(lat_count, lon_count)
    turns = turn_np(lat_count, lon_count)
    send = synthesis(control, spec_sigma, w_in, w_out.T, legendre)
    got = lax.all_to_all(send, "tp", split_axis=0, concat_axis=0, tiled=True)
    obs = pack_obs(
        *(
            field.reshape(-1, LANES)
            for field in (obs_band, obs_cell, obs_value, obs_weight, obs_offset)
        )
    )
    send = regroup(got, obs).reshape(BANDS, 16, LANES)
    arrived = lax.all_to_all(send, "band", split_axis=0, concat_axis=0, tiled=True)
    other = lax.ppermute(got, "band", [(i, i ^ 1) for i in range(BANDS)])
    prepared = prepare(got, other, (turns, *zonal[:2]))
    prior = jnp.pad(prior_mean_field[:, 0, :], ((0, ROWS - channels), (0, 0)))
    prior = jnp.concatenate([prior, prior[:, : WIDTH - STRIDE]], axis=1)
    prior = jnp.stack([prior[:, a * STRIDE : a * STRIDE + WIDTH] for a in range(BLOCKS)])
    gains = jnp.broadcast_to(
        jnp.pad(magnitude_factor, (0, ROWS - channels))[:, None], (ROWS, WIDTH)
    )
    modes = run_cycle(channels, arrived, prior, gains, prepared, zonal[2:])
    modes = lax.all_to_all(
        modes.reshape(lat_count, 2, LANES),
        ("band", "tp"),
        split_axis=0,
        concat_axis=0,
        tiled=True,
    )
    modes = modes.reshape(2 * lat_count, LANES)
    return analysis(modes, control, spec_sigma, legendre)


def solution(mesh):
    placed = (
        P(None, None, ("band", "tp"), None),
        P(None, ("band", "tp"), None),
        P(None, ("band", "tp"), None),
        P(),
        P(None, "tp"),
        P("tp", None),
        P("band", "tp", None, None),
        P("band", "tp", None),
        P("band", "tp", None),
        P("band", "tp", None),
        P("band", "tp", None),
    )
    return jax.shard_map(
        shards,
        mesh=mesh,
        in_specs=placed,
        out_specs=P(None, None, ("band", "tp"), None),
        check_vma=False,
    )
```

```python
import math

import jax
import jax.numpy as jnp
import ml_dtypes
import numpy as np
from jax import lax
from jax.experimental import pallas as pl
from jax.experimental.pallas import tpu as pltpu
from jax.sharding import PartitionSpec as P

EPSILON = 1e-06
BF16 = jnp.bfloat16
F32 = jnp.float32

BLOCKS = 6
PAIRS = BLOCKS // 2
STRIDE = 240
WIDTH = 256
ROWS = 72
LANES = 128
BANDS = 64
TPS = 8
SLOTS = 64
FIELDS = 8
ROW_SHIFT = 256
OBS_CHUNK = 512
GROUP = 2
MIB = 1024 * 1024


def split_np(table):
    high = table.astype(np.float32).astype(ml_dtypes.bfloat16)
    low = (table - high.astype(np.float64)).astype(np.float32).astype(ml_dtypes.bfloat16)
    return high, low


def legendre_np(wave_count, lat_count):
    cycles = np.arange(lat_count)
    tables = []
    for parity in range(2):
        frequency = np.arange(wave_count) + parity
        phases = (2 * cycles[:, None] + 1) * frequency[None, :] % (4 * lat_count)
        angles = phases * (math.pi / (2 * lat_count))
        basis = np.sin(angles) if parity else np.cos(angles)
        tables.append(basis * math.sqrt(2.0 / lat_count))
    return split_np(np.stack(tables))


def even_odd_np(orders):
    return np.concatenate([np.arange(0, orders, 2), np.arange(1, orders, 2)])


def zonal_np(orders, lon_count):
    phases = even_odd_np(orders)[:, None] * np.arange(WIDTH)[None, :] % lon_count
    angles = phases * (2.0 * math.pi / lon_count)
    halves = angles.reshape(2, 1, orders // 2, WIDTH)
    parts = np.concatenate([np.cos(halves), np.sin(halves)], axis=1)
    high, low = split_np(parts.reshape(2 * orders, WIDTH))
    return high, low, np.ascontiguousarray(high.T), np.ascontiguousarray(low.T)


def turn_np(orders, lon_count):
    phases = np.arange(PAIRS)[:, None] * STRIDE * even_odd_np(orders)[None, :] % lon_count
    angles = phases * (2.0 * math.pi / lon_count)
    pad = np.zeros((4 - PAIRS, orders))
    return np.concatenate([np.cos(angles), pad, np.sin(angles), pad]).astype(np.float32)


def split(values):
    high = values.astype(BF16)
    low = (values - high.astype(F32)).astype(BF16)
    return high, low


NN = (((1,), (0,)), ((), ()))
NT = (((1,), (1,)), ((), ()))


def dot(left, right, dims=NN):
    return lax.dot_general(left, right, dims, preferred_element_type=F32)


def dot3(left, right, dims=NN):
    return (
        dot(left[0], right[0], dims) + dot(left[0], right[1], dims) + dot(left[1], right[0], dims)
    )


def lane_ids(shape):
    return lax.broadcasted_iota(jnp.int32, shape, len(shape) - 1)


SEND_ROWS = 128
REST_LANE = 96
PIECE_LANE = 112


def synthesis_kernel(
    control_hbm,
    sigma_hbm,
    high_hbm,
    low_hbm,
    w_in_hbm,
    w_out_hbm,
    out,
    control,
    sigma,
    table_high,
    table_low,
    w_in,
    w_out,
    coef,
    modes,
    arrivals,
):
    parity = lax.rem(lax.axis_index("tp"), 2)
    copies = [
        pltpu.make_async_copy(source, target, arrivals.at[i])
        for i, (source, target) in enumerate(
            (
                (control_hbm, control),
                (sigma_hbm, sigma),
                (high_hbm.at[parity], table_high),
                (low_hbm.at[parity], table_low),
                (w_in_hbm, w_in),
                (w_out_hbm, w_out),
            )
        )
    ]
    for copy in copies:
        copy.start()
    channels = sigma.shape[0]
    coef[...] = jnp.zeros_like(coef)
    copies[0].wait()
    copies[1].wait()
    deviation = sigma[:, 0, :]
    first = deviation * control[:, 0, 0, :]
    second = deviation * control[:, 1, 0, :]
    coef[0:channels, :] = first
    coef[ROWS:LANES, :] = second[: LANES - ROWS]
    tail = channels - (LANES - ROWS)
    coef[LANES + REST_LANE : LANES + REST_LANE + tail, :] = second[LANES - ROWS :]
    parts = split(coef[...])
    for copy in copies[2:]:
        copy.wait()
    whole = dot3((table_high[...], table_low[...]), parts, NT)
    modes[0] = whole[:, 0:LANES]
    modes[1] = whole[:, LANES:]
    even = lax.rem(lax.axis_index("band"), 2) == 0
    rows = jnp.where(even, w_in[...].astype(F32), w_out[...].astype(F32))
    rows = jnp.pad(rows, ((0, ROWS - channels), (0, LANES - rows.shape[1])))
    lanes = lane_ids((8, LANES))
    pieces = [
        jnp.where(
            lanes >= PIECE_LANE,
            pltpu.roll(rows[BANDS:ROWS], PIECE_LANE - start, 1),
            rows[start // 2 : start // 2 + 8],
        )
        for start in range(0, REST_LANE, 16)
    ]
    rows = jnp.concatenate([*pieces, rows[REST_LANE // 2 : BANDS]], axis=0)
    for dest in range(TPS):
        out[dest, 0:BANDS, :] = modes[0, pl.ds(dest, BANDS, stride=TPS), :].astype(BF16)
        rest = modes[1, pl.ds(dest, BANDS, stride=TPS), :]
        out[dest, BANDS:SEND_ROWS, :] = (rest + rows).astype(BF16)


def in_hbm(*arrays):
    return tuple(pltpu.with_memory_space_constraint(jnp.asarray(a), pltpu.HBM) for a in arrays)


IN_VMEM = pl.BlockSpec(memory_space=pltpu.VMEM)
IN_HBM = pl.BlockSpec(memory_space=pltpu.HBM)


def synthesis(control, sigma, w_in, w_out_t, table):
    lat_count, wave_count = table[0].shape[1:]
    return pl.pallas_call(
        synthesis_kernel,
        out_shape=jax.ShapeDtypeStruct((TPS, SEND_ROWS, LANES), BF16),
        in_specs=[IN_HBM] * 6,
        out_specs=IN_VMEM,
        scratch_shapes=[
            pltpu.VMEM(control.shape, F32),
            pltpu.VMEM(sigma.shape, F32),
            pltpu.VMEM((lat_count, wave_count), BF16),
            pltpu.VMEM((lat_count, wave_count), BF16),
            pltpu.VMEM(w_in.shape, BF16),
            pltpu.VMEM(w_in.shape, BF16),
            pltpu.VMEM((2 * LANES, wave_count), F32),
            pltpu.VMEM((2, lat_count, LANES), F32),
            pltpu.SemaphoreType.DMA((6,)),
        ],
        cost_estimate=pl.CostEstimate(flops=400_000_000, bytes_accessed=2_000_000, transcendentals=0),
        compiler_params=pltpu.CompilerParams(vmem_limit_bytes=12 * MIB),
        name="synthesis",
    )(*in_hbm(control, sigma, *table, w_in, w_out_t))


def pack_kernel(band, cell, value, weight, offset, out):
    blocks = band.shape[0]
    cells = cell[...].astype(F32)
    channel = jnp.floor((cells + 0.5) * (1.0 / 1440.0))
    start = cells - 1440.0 * channel - 1.0
    start = jnp.where(start < 0.0, start + 1440.0, start)
    part = jnp.floor((start + 0.5) * (1.0 / STRIDE))
    fields = []
    for source in (value, weight, offset):
        high = source[...].astype(BF16).astype(F32)
        fields += [high, source[...] - high]
    fields += [part * ROWS + channel - ROW_SHIFT, start - part * STRIDE]
    band_ids = lax.broadcasted_iota(jnp.int32, (BANDS, LANES), 0)
    hits = [band_ids == band[i : i + 1, :] for i in range(blocks)]
    ones = [jnp.where(hit, 1.0, 0.0) for hit in hits]
    square = (LANES, 2 * LANES)
    row, column = lax.broadcasted_iota(jnp.int32, square, 0), lane_ids(square)
    before = jnp.where((row < column) | (column >= LANES), 1.0, 0.0).astype(BF16)
    counts = dot(jnp.concatenate(ones, axis=0).astype(BF16), before)
    slot_ids = lax.broadcasted_iota(jnp.int32, (LANES, LANES), 0).astype(F32)
    taken = jnp.zeros((BANDS, LANES), F32)
    total = jnp.zeros((BANDS, FIELDS * LANES), F32)
    for i in range(blocks):
        within = counts[i * BANDS : (i + 1) * BANDS, :]
        rank = jnp.sum(ones[i] * (within[:, :LANES] + taken), axis=0, keepdims=True)
        taken = taken + within[:, LANES:]
        here = slot_ids == rank + (LANES - SLOTS)
        spread = [jnp.where(here, field[i : i + 1, :], 0.0).astype(BF16) for field in fields]
        total = total + dot(ones[i].astype(BF16), jnp.concatenate(spread, axis=0), NT)
    out[...] = total


def pack_obs(band, cell, value, weight, offset):
    return pl.pallas_call(
        pack_kernel,
        out_shape=jax.ShapeDtypeStruct((BANDS, FIELDS * LANES), F32),
        cost_estimate=pl.CostEstimate(flops=200_000_000, bytes_accessed=300_000, transcendentals=0),
        compiler_params=pltpu.CompilerParams(vmem_limit_bytes=8 * MIB),
        name="pack_obs",
    )(band, cell, value, weight, offset)


def regroup_kernel(arrived, obs, out, rows):
    lanes = lane_ids((BANDS, LANES))
    for t in range(TPS):
        rows[pl.ds(t, BANDS, stride=16), :] = arrived[t, 0:BANDS, :].astype(F32)
        rest = pltpu.roll(arrived[t, BANDS : 2 * BANDS, :].astype(F32), LANES - REST_LANE, 1)
        rest = jnp.where(lanes < 16, rest, obs[:, t * LANES : (t + 1) * LANES])
        rows[pl.ds(8 + t, BANDS, stride=16), :] = rest
    out[...] = rows[...].astype(BF16)


def regroup(arrived, obs):
    return pl.pallas_call(
        regroup_kernel,
        out_shape=jax.ShapeDtypeStruct((BANDS * 16, LANES), BF16),
        scratch_shapes=[pltpu.VMEM((BANDS * 16, LANES), F32)],
        cost_estimate=pl.CostEstimate(flops=300_000, bytes_accessed=800_000, transcendentals=0),
        compiler_params=pltpu.CompilerParams(vmem_limit_bytes=8 * MIB),
        name="regroup",
    )(arrived, obs)


def prepare_kernel(own, other, *refs):
    sources, (in_rows, in_columns, out_rows, out_columns, *targets), (arrivals,) = (
        refs[:3],
        refs[3:10],
        refs[10:],
    )
    copies = [
        pltpu.make_async_copy(source, target, arrivals.at[i])
        for i, (source, target) in enumerate(zip(sources, targets))
    ]
    for copy in copies:
        copy.start()
    even = lax.rem(lax.axis_index("band"), 2) == 0
    lanes = lane_ids((8, LANES))
    filler = jnp.zeros((LANES - ROWS, LANES), F32)
    for columns, rows, first in ((in_columns, in_rows, True), (out_columns, out_rows, False)):
        pieces = []
        for t in range(TPS):
            mine = own[t, BANDS:SEND_ROWS, :].astype(F32)
            theirs = other[t, BANDS:SEND_ROWS, :].astype(F32)
            piece = jnp.where(even == first, mine, theirs)
            last = jnp.zeros((8, LANES), F32)
            for start in range(0, REST_LANE, 16):
                part = piece[start // 2 : start // 2 + 8]
                part = pltpu.roll(part, LANES - PIECE_LANE + start, 1)
                last = jnp.where((lanes >= start) & (lanes < start + 16), part, last)
            piece = jnp.concatenate([piece, last, filler], axis=0)
            pieces.append(piece.T[0:REST_LANE])
        upright = jnp.concatenate(pieces, axis=0)
        columns[...] = upright.astype(BF16)
        rows[...] = upright.T[0:80].astype(BF16)
    for copy in copies:
        copy.wait()


def prepare(own, other, tables):
    hidden = TPS * 96
    return pl.pallas_call(
        prepare_kernel,
        out_shape=(
            jax.ShapeDtypeStruct((80, hidden), BF16),
            jax.ShapeDtypeStruct((hidden, LANES), BF16),
            jax.ShapeDtypeStruct((80, hidden), BF16),
            jax.ShapeDtypeStruct((hidden, LANES), BF16),
            *(jax.ShapeDtypeStruct(table.shape, table.dtype) for table in tables),
        ),
        in_specs=[IN_VMEM] * 2 + [IN_HBM] * 3,
        out_specs=[IN_VMEM] * 7,
        scratch_shapes=[pltpu.SemaphoreType.DMA((3,))],
        cost_estimate=pl.CostEstimate(flops=1_000_000, bytes_accessed=5_000_000, transcendentals=0),
        compiler_params=pltpu.CompilerParams(vmem_limit_bytes=8 * MIB),
        name="prepare",
    )(own, other, *in_hbm(*tables))


GELU_SCALE = math.sqrt(2.0 / math.pi)
GELU_CUBE = 0.044715


def lagrange_rows(offset):
    return (
        -offset * (offset - 1.0) * (offset - 2.0) / 6.0,
        (offset + 1.0) * (offset - 1.0) * (offset - 2.0) / 2.0,
        -(offset + 1.0) * offset * (offset - 2.0) / 2.0,
        (offset + 1.0) * offset * (offset - 1.0) / 6.0,
    )


def cycle_kernel(
    channels,
    arrived,
    gains,
    in_rows,
    in_columns,
    out_rows,
    out_columns,
    turns,
    table_high,
    table_low,
    prior_hbm,
    wide_high_hbm,
    wide_low_hbm,
    out,
    prior,
    wide_high,
    wide_low,
    arrivals,
    state,
    slopes,
    obs,
    chosen_all,
    spread_all,
    paired,
):
    orders = turns.shape[1]
    copies = [
        pltpu.make_async_copy(prior_hbm, prior, arrivals.at[0]),
        pltpu.make_async_copy(wide_high_hbm, wide_high, arrivals.at[1]),
        pltpu.make_async_copy(wide_low_hbm, wide_low, arrivals.at[2]),
    ]
    for copy in copies:
        copy.start()
    slices = arrived[...].astype(F32)
    rest = slices[:, 8:16, :]
    half = orders // 2
    paired[0:orders, :] = slices[:, 0:8, :].reshape(orders, LANES)
    paired[orders:, :] = rest.reshape(orders, LANES)
    cos_sin = [paired[pl.ds(p, half, stride=2), :] for p in range(2)]
    cos_sin = jnp.concatenate(cos_sin, axis=0).T
    tail = [paired[pl.ds(orders + p, half, stride=2), :] for p in range(2)]
    tail = jnp.concatenate(tail, axis=0).T
    cos_part = cos_sin[0:ROWS]
    sin_part = jnp.concatenate([cos_sin[ROWS:LANES], tail[0:16]], axis=0)
    pairs = rest.reshape(BANDS // 2, 2, FIELDS, LANES)
    near = pltpu.roll(pairs[:, 0].reshape(BANDS // 2 * FIELDS, LANES), LANES - SLOTS, 1)
    near = near.reshape(BANDS // 2, FIELDS, LANES)
    obs[...] = jnp.where(lane_ids(near.shape) < SLOTS, near, pairs[:, 1])

    turned = []
    for a in range(PAIRS):
        turn_cos, turn_sin = turns[a : a + 1, :], turns[4 + a : 5 + a, :]
        turned_cos = cos_part * turn_cos + sin_part * turn_sin
        turned_sin = sin_part * turn_cos - cos_part * turn_sin
        turned.append(
            jnp.concatenate(
                [turned_cos[:, :half], turned_sin[:, :half], turned_cos[:, half:], turned_sin[:, half:]],
                axis=1,
            )
        )
    turned = split(jnp.concatenate(turned, axis=0))
    sums = []
    for p in range(2):
        span = slice(p * orders, (p + 1) * orders)
        part = (turned[0][:, span], turned[1][:, span])
        sums.append(dot3(part, (table_high[span, :], table_low[span, :])))
    field = jnp.concatenate([sums[0] + sums[1], sums[0] - sums[1]], axis=0)
    copies[0].wait()
    state[...] = prior[...].reshape(BLOCKS * ROWS, WIDTH) + field

    forecast = []
    gain = jnp.concatenate([gains[...]] * GROUP, axis=1)
    groups = [range(a, a + GROUP) for a in range(0, BLOCKS, GROUP)]
    for g, group in enumerate(groups):
        field = [state[a * ROWS : (a + 1) * ROWS, :] for a in group]
        field = jnp.concatenate(field, axis=1)
        mean_sq = jnp.sum(field * field, axis=0, keepdims=True) * (1.0 / channels)
        unit = (field * gain * lax.rsqrt(mean_sq + EPSILON)).astype(BF16)
        pre = dot(in_columns[:, 0:ROWS], unit)
        square = pre * pre
        inner = pre * (GELU_SCALE + (GELU_SCALE * GELU_CUBE) * square)
        gate = 0.5 + 0.5 * jnp.tanh(inner)
        hidden = pre * gate
        slopes[g] = gate + hidden * (1.0 - gate) * (
            2.0 * GELU_SCALE + (6.0 * GELU_SCALE * GELU_CUBE) * square
        )
        ahead = field + dot(out_rows[...], hidden.astype(BF16))[0:ROWS]
        forecast += [ahead[:, i * WIDTH : (i + 1) * WIDTH] for i in range(GROUP)]
    forecast = split(jnp.concatenate(forecast, axis=0).T)
    forecast = jnp.concatenate(forecast, axis=0)

    per_chunk = OBS_CHUNK // LANES
    chunks = obs.shape[0] // per_chunk
    low_ids = lax.broadcasted_iota(jnp.int32, (16, OBS_CHUNK), 0).astype(F32)
    near_ids = lax.broadcasted_iota(jnp.int32, (32, OBS_CHUNK), 0).astype(F32)
    none = jnp.zeros((16, OBS_CHUNK), BF16)

    def fields_of(chunk):
        fields = [obs[chunk * per_chunk + i] for i in range(per_chunk)]
        return jnp.concatenate(fields, axis=1)

    def choose(chunk):
        row = fields_of(chunk)[6:7] + float(ROW_SHIFT)
        row_group = jnp.floor(row * (1.0 / 16.0))
        first = jnp.where(low_ids == row - 16.0 * row_group, 1.0, 0.0).astype(BF16)
        row_group = jnp.broadcast_to(row_group, (16, OBS_CHUNK)).astype(BF16)
        chosen = jnp.concatenate(
            [
                jnp.where(row_group == jnp.array(float(g), BF16), first, none)
                for g in range(BLOCKS * ROWS // 16)
            ],
            axis=0,
        )
        chosen_all[:, chunk * OBS_CHUNK : (chunk + 1) * OBS_CHUNK] = chosen
        return chosen

    def observe(chunk, picked):
        fields = fields_of(chunk)
        columns = slice(chunk * OBS_CHUNK, (chunk + 1) * OBS_CHUNK)
        value = fields[0:1] + fields[1:2]
        weight = fields[2:3] + fields[3:4]
        offset = fields[4:5] + fields[5:6]
        group = jnp.floor(fields[7:8] * (1.0 / 16.0))
        place = near_ids - (fields[7:8] - 16.0 * group)
        group8 = jnp.broadcast_to(group, (8, OBS_CHUNK))
        window = [jnp.zeros((8, OBS_CHUNK), F32)] * 4
        for g in range(WIDTH // 16 - 1):
            mask = group8 == float(g)
            for i in range(4):
                rows = slice(16 * g + 8 * i, 16 * g + 8 * i + 8)
                window[i] = jnp.where(mask, picked[rows] + picked[WIDTH:][rows], window[i])
        window = jnp.concatenate(window, axis=0)
        w_left, w_here, w_right, w_far = lagrange_rows(offset)
        stencil = jnp.where(
            place == 0.0,
            w_left,
            jnp.where(
                place == 1.0,
                w_here,
                jnp.where(place == 2.0, w_right, jnp.where(place == 3.0, w_far, 0.0)),
            ),
        )
        reading = jnp.sum(stencil * window, axis=0, keepdims=True)
        parts = split(stencil * (weight * (reading - value)))
        group = jnp.broadcast_to(group, (16, OBS_CHUNK)).astype(BF16)
        masks = [group == jnp.array(float(g), BF16) for g in range(WIDTH // 16 - 1)]
        for i, part in enumerate(parts):
            pieces = []
            for g in range(WIDTH // 16):
                piece = none
                if g > 0:
                    piece = jnp.where(masks[g - 1], part[16:32], piece)
                if g < WIDTH // 16 - 1:
                    piece = jnp.where(masks[g], part[0:16], piece)
                pieces.append(piece)
            spread_all[i * WIDTH : (i + 1) * WIDTH, columns] = jnp.concatenate(pieces, axis=0)

    chosen = choose(0)
    picked = None
    for chunk in range(chunks):
        latest = dot(forecast, chosen)
        if chunk + 1 < chunks:
            chosen = choose(chunk + 1)
        if chunk > 0:
            observe(chunk - 1, picked)
        picked = latest
    observe(chunks - 1, picked)
    forcing = dot(spread_all[...], chosen_all[...], NT)
    forcing = (forcing[0:WIDTH] + forcing[WIDTH:]).T

    lanes = lane_ids((BLOCKS * ROWS, WIDTH))
    halo = pltpu.roll(forcing, WIDTH - STRIDE, 1)
    halo = jnp.concatenate([halo[(BLOCKS - 1) * ROWS :], halo[: (BLOCKS - 1) * ROWS]], axis=0)
    forcing = jnp.where(lanes < STRIDE, forcing, 0.0) + jnp.where(lanes < 3, halo, 0.0)
    costate = []
    for g, group in enumerate(groups):
        force = [forcing[a * ROWS : (a + 1) * ROWS] for a in group]
        force = jnp.concatenate(force, axis=1)
        grad_hidden = dot(out_columns[:, 0:ROWS], force.astype(BF16))
        grad_pre = (grad_hidden * slopes[g]).astype(BF16)
        grad_unit = dot(in_rows[...], grad_pre)[0:ROWS]
        field = [state[a * ROWS : (a + 1) * ROWS, :] for a in group]
        field = jnp.concatenate(field, axis=1)
        mean_sq = jnp.sum(field * field, axis=0, keepdims=True) * (1.0 / channels)
        inverse = lax.rsqrt(mean_sq + EPSILON)
        scaled = grad_unit * gain
        along = jnp.sum(scaled * field, axis=0, keepdims=True) * (1.0 / channels)
        total = force + scaled * inverse - field * (along * inverse * inverse * inverse)
        costate += [total[:, i * WIDTH : (i + 1) * WIDTH] for i in range(GROUP)]
    near = jnp.concatenate(costate[:PAIRS], axis=0)
    far = jnp.concatenate(costate[PAIRS:], axis=0)
    for copy in copies[1:]:
        copy.wait()
    pad = jnp.zeros((LANES - ROWS, half), F32)
    lanes = lane_ids((half, LANES))
    for p, both in enumerate((near + far, near - far)):
        span = slice(p * orders, (p + 1) * orders)
        blocks = dot3(split(both), (wide_high[:, span], wide_low[:, span]))
        grads = [jnp.zeros((ROWS, half), F32)] * 2
        for a in range(PAIRS):
            turn_cos = turns[a : a + 1, p * half : (p + 1) * half]
            turn_sin = turns[4 + a : 5 + a, p * half : (p + 1) * half]
            block = blocks[a * ROWS : (a + 1) * ROWS]
            block_cos, block_sin = block[:, :half], block[:, half:]
            grads[0] = grads[0] + turn_cos * block_cos - turn_sin * block_sin
            grads[1] = grads[1] + turn_sin * block_cos + turn_cos * block_sin
        for r in range(2):
            upright = jnp.concatenate([grads[r], pad], axis=0).T
            high = upright.astype(BF16).astype(F32)
            low = pltpu.roll(upright - high, channels, 1)
            place = pl.ds(2 * p + r, half, stride=4)
            paired[place, :] = jnp.where(lanes < channels, high, low)
    out[...] = paired[...].astype(BF16)


def run_cycle(channels, arrived, prior, gains, prepared, wide):
    orders = prepared[4].shape[1]
    hidden = prepared[1].shape[0]
    return pl.pallas_call(
        lambda *refs: cycle_kernel(channels, *refs),
        out_shape=jax.ShapeDtypeStruct((2 * orders, LANES), BF16),
        in_specs=[IN_VMEM] * 9 + [IN_HBM] * 3,
        out_specs=IN_VMEM,
        scratch_shapes=[
            pltpu.VMEM(prior.shape, F32),
            *(pltpu.VMEM(part.shape, BF16) for part in wide),
            pltpu.SemaphoreType.DMA((3,)),
            pltpu.VMEM((BLOCKS * ROWS, WIDTH), F32),
            pltpu.VMEM((BLOCKS // GROUP, hidden, GROUP * WIDTH), F32),
            pltpu.VMEM((BANDS // 2, FIELDS, LANES), F32),
            pltpu.VMEM((BLOCKS * ROWS, BANDS * SLOTS), BF16),
            pltpu.VMEM((2 * WIDTH, BANDS * SLOTS), BF16),
            pltpu.VMEM((2 * orders, LANES), F32),
        ],
        compiler_params=pltpu.CompilerParams(vmem_limit_bytes=36 * MIB),
        cost_estimate=pl.CostEstimate(
            flops=8_000_000_000, bytes_accessed=4_000_000, transcendentals=1_200_000
        ),
        name="cycle",
    )(arrived, gains, *prepared, *in_hbm(prior, *wide))


def analysis_kernel(arrived, control, sigma, table_high, table_low, out, rows):
    parity = lax.rem(lax.axis_index("tp"), 2)
    channels = sigma.shape[0]
    orders = arrived.shape[0] // 2
    rows[...] = arrived[...].astype(F32)
    lanes = lane_ids((orders, LANES))
    for r in range(2):
        both = rows[pl.ds(r, orders, stride=2), :]
        low = pltpu.roll(both, LANES - channels, 1)
        grad = jnp.where(lanes < channels, both, 0.0)
        grad = grad + jnp.where(lanes < LANES - channels, low, 0.0)
        grad_t = split(grad.T[0:ROWS])
        projected = dot3(grad_t, (table_high[parity], table_low[parity]))
        out[:, r, 0, :] = control[:, r, 0, :] + sigma[:, 0, :] * projected[0:channels]


def analysis(arrived, control, sigma, table):
    return pl.pallas_call(
        analysis_kernel,
        out_shape=jax.ShapeDtypeStruct(control.shape, F32),
        scratch_shapes=[pltpu.VMEM(arrived.shape, F32)],
        cost_estimate=pl.CostEstimate(flops=400_000_000, bytes_accessed=2_000_000, transcendentals=0),
        compiler_params=pltpu.CompilerParams(vmem_limit_bytes=12 * MIB),
        name="analysis",
    )(arrived, control, sigma, *table)


def shards(
    control,
    spec_sigma,
    prior_mean_field,
    magnitude_factor,
    w_in,
    w_out,
    obs_band,
    obs_cell,
    obs_value,
    obs_weight,
    obs_offset,
):
    channels, _, _, wave_count = control.shape
    lat_count = BANDS * TPS
    lon_count = prior_mean_field.shape[2]
    legendre = legendre_np(wave_count, lat_count)
    zonal = zonal_np(lat_count, lon_count)
    turns = turn_np(lat_count, lon_count)
    send = synthesis(control, spec_sigma, w_in, w_out.T, legendre)
    got = lax.all_to_all(send, "tp", split_axis=0, concat_axis=0, tiled=True)
    obs = pack_obs(
        *(
            field.reshape(-1, LANES)
            for field in (obs_band, obs_cell, obs_value, obs_weight, obs_offset)
        )
    )
    send = regroup(got, obs).reshape(BANDS, 16, LANES)
    arrived = lax.all_to_all(send, "band", split_axis=0, concat_axis=0, tiled=True)
    other = lax.ppermute(got, "band", [(i, i ^ 1) for i in range(BANDS)])
    prepared = prepare(got, other, (turns, *zonal[:2]))
    prior = jnp.pad(prior_mean_field[:, 0, :], ((0, ROWS - channels), (0, 0)))
    prior = jnp.concatenate([prior, prior[:, : WIDTH - STRIDE]], axis=1)
    prior = jnp.stack([prior[:, a * STRIDE : a * STRIDE + WIDTH] for a in range(BLOCKS)])
    gains = jnp.broadcast_to(
        jnp.pad(magnitude_factor, (0, ROWS - channels))[:, None], (ROWS, WIDTH)
    )
    modes = run_cycle(channels, arrived, prior, gains, prepared, zonal[2:])
    modes = lax.all_to_all(
        modes.reshape(lat_count, 2, LANES),
        ("band", "tp"),
        split_axis=0,
        concat_axis=0,
        tiled=True,
    )
    modes = modes.reshape(2 * lat_count, LANES)
    return analysis(modes, control, spec_sigma, legendre)


def solution(mesh):
    placed = (
        P(None, None, ("band", "tp"), None),
        P(None, ("band", "tp"), None),
        P(None, ("band", "tp"), None),
        P(),
        P(None, "tp"),
        P("tp", None),
        P("band", "tp", None, None),
        P("band", "tp", None),
        P("band", "tp", None),
        P("band", "tp", None),
        P("band", "tp", None),
    )
    return jax.shard_map(
        shards,
        mesh=mesh,
        in_specs=placed,
        out_specs=P(None, None, ("band", "tp"), None),
        check_vma=False,
    )
```

```python
import math

import jax
import jax.numpy as jnp
import ml_dtypes
import numpy as np
from jax import lax
from jax.experimental import pallas as pl
from jax.experimental.pallas import tpu as pltpu
from jax.sharding import PartitionSpec as P

EPSILON = 1e-06
BF16 = jnp.bfloat16
F32 = jnp.float32

BLOCKS = 6
PAIRS = BLOCKS // 2
STRIDE = 240
WIDTH = 256
ROWS = 72
LANES = 128
BANDS = 64
TPS = 8
SLOTS = 64
FIELDS = 8
ROW_SHIFT = 256
OBS_CHUNK = 512
GROUP = 2
MIB = 1024 * 1024


def split_np(table):
    high = table.astype(np.float32).astype(ml_dtypes.bfloat16)
    low = (table - high.astype(np.float64)).astype(np.float32).astype(ml_dtypes.bfloat16)
    return high, low


def legendre_np(wave_count, lat_count):
    cycles = np.arange(lat_count)
    tables = []
    for parity in range(2):
        frequency = np.arange(wave_count) + parity
        phases = (2 * cycles[:, None] + 1) * frequency[None, :] % (4 * lat_count)
        angles = phases * (math.pi / (2 * lat_count))
        basis = np.sin(angles) if parity else np.cos(angles)
        tables.append(basis * math.sqrt(2.0 / lat_count))
    return split_np(np.stack(tables))


def even_odd_np(orders):
    return np.concatenate([np.arange(0, orders, 2), np.arange(1, orders, 2)])


def zonal_np(orders, lon_count):
    phases = even_odd_np(orders)[:, None] * np.arange(WIDTH)[None, :] % lon_count
    angles = phases * (2.0 * math.pi / lon_count)
    halves = angles.reshape(2, 1, orders // 2, WIDTH)
    parts = np.concatenate([np.cos(halves), np.sin(halves)], axis=1)
    high, low = split_np(parts.reshape(2 * orders, WIDTH))
    return high, low, np.ascontiguousarray(high.T), np.ascontiguousarray(low.T)


def turn_np(orders, lon_count):
    phases = np.arange(PAIRS)[:, None] * STRIDE * even_odd_np(orders)[None, :] % lon_count
    angles = phases * (2.0 * math.pi / lon_count)
    pad = np.zeros((4 - PAIRS, orders))
    return np.concatenate([np.cos(angles), pad, np.sin(angles), pad]).astype(np.float32)


def split(values):
    high = values.astype(BF16)
    low = (values - high.astype(F32)).astype(BF16)
    return high, low


NN = (((1,), (0,)), ((), ()))
NT = (((1,), (1,)), ((), ()))


def dot(left, right, dims=NN):
    return lax.dot_general(left, right, dims, preferred_element_type=F32)


def dot3(left, right, dims=NN):
    return (
        dot(left[0], right[0], dims) + dot(left[0], right[1], dims) + dot(left[1], right[0], dims)
    )


def lane_ids(shape):
    return lax.broadcasted_iota(jnp.int32, shape, len(shape) - 1)


SEND_ROWS = 128
REST_LANE = 96
PIECE_LANE = 112


def synthesis_kernel(
    control_hbm,
    sigma_hbm,
    high_hbm,
    low_hbm,
    w_in_hbm,
    w_out_hbm,
    out,
    control,
    sigma,
    table_high,
    table_low,
    w_in,
    w_out,
    coef,
    modes,
    arrivals,
):
    parity = lax.rem(lax.axis_index("tp"), 2)
    copies = [
        pltpu.make_async_copy(source, target, arrivals.at[i])
        for i, (source, target) in enumerate(
            (
                (control_hbm, control),
                (sigma_hbm, sigma),
                (high_hbm.at[parity], table_high),
                (low_hbm.at[parity], table_low),
                (w_in_hbm, w_in),
                (w_out_hbm, w_out),
            )
        )
    ]
    for copy in copies:
        copy.start()
    channels = sigma.shape[0]
    coef[...] = jnp.zeros_like(coef)
    copies[0].wait()
    copies[1].wait()
    deviation = sigma[:, 0, :]
    first = deviation * control[:, 0, 0, :]
    second = deviation * control[:, 1, 0, :]
    coef[0:channels, :] = first
    coef[ROWS:LANES, :] = second[: LANES - ROWS]
    tail = channels - (LANES - ROWS)
    coef[LANES + REST_LANE : LANES + REST_LANE + tail, :] = second[LANES - ROWS :]
    parts = split(coef[...])
    for copy in copies[2:]:
        copy.wait()
    whole = dot(table_high[...], jnp.concatenate(parts, axis=0), NT)
    whole = whole[:, : 2 * LANES] + whole[:, 2 * LANES :] + dot(table_low[...], parts[0], NT)
    modes[0] = whole[:, 0:LANES]
    modes[1] = whole[:, LANES:]
    even = lax.rem(lax.axis_index("band"), 2) == 0
    rows = jnp.where(even, w_in[...].astype(F32), w_out[...].astype(F32))
    rows = jnp.pad(rows, ((0, ROWS - channels), (0, LANES - rows.shape[1])))
    lanes = lane_ids((8, LANES))
    pieces = [
        jnp.where(
            lanes >= PIECE_LANE,
            pltpu.roll(rows[BANDS:ROWS], PIECE_LANE - start, 1),
            rows[start // 2 : start // 2 + 8],
        )
        for start in range(0, REST_LANE, 16)
    ]
    rows = jnp.concatenate([*pieces, rows[REST_LANE // 2 : BANDS]], axis=0)
    for dest in range(TPS):
        out[dest, 0:BANDS, :] = modes[0, pl.ds(dest, BANDS, stride=TPS), :].astype(BF16)
        rest = modes[1, pl.ds(dest, BANDS, stride=TPS), :]
        out[dest, BANDS:SEND_ROWS, :] = (rest + rows).astype(BF16)


def in_hbm(*arrays):
    return tuple(pltpu.with_memory_space_constraint(jnp.asarray(a), pltpu.HBM) for a in arrays)


IN_VMEM = pl.BlockSpec(memory_space=pltpu.VMEM)
IN_HBM = pl.BlockSpec(memory_space=pltpu.HBM)


def synthesis(control, sigma, w_in, w_out_t, table):
    lat_count, wave_count = table[0].shape[1:]
    return pl.pallas_call(
        synthesis_kernel,
        out_shape=jax.ShapeDtypeStruct((TPS, SEND_ROWS, LANES), BF16),
        in_specs=[IN_HBM] * 6,
        out_specs=IN_VMEM,
        scratch_shapes=[
            pltpu.VMEM(control.shape, F32),
            pltpu.VMEM(sigma.shape, F32),
            pltpu.VMEM((lat_count, wave_count), BF16),
            pltpu.VMEM((lat_count, wave_count), BF16),
            pltpu.VMEM(w_in.shape, BF16),
            pltpu.VMEM(w_in.shape, BF16),
            pltpu.VMEM((2 * LANES, wave_count), F32),
            pltpu.VMEM((2, lat_count, LANES), F32),
            pltpu.SemaphoreType.DMA((6,)),
        ],
        cost_estimate=pl.CostEstimate(flops=400_000_000, bytes_accessed=2_000_000, transcendentals=0),
        compiler_params=pltpu.CompilerParams(vmem_limit_bytes=12 * MIB),
        name="synthesis",
    )(*in_hbm(control, sigma, *table, w_in, w_out_t))


def pack_kernel(band, cell, value, weight, offset, out):
    blocks = band.shape[0]
    cells = cell[...].astype(F32)
    channel = jnp.floor((cells + 0.5) * (1.0 / 1440.0))
    start = cells - 1440.0 * channel - 1.0
    start = jnp.where(start < 0.0, start + 1440.0, start)
    part = jnp.floor((start + 0.5) * (1.0 / STRIDE))
    fields = []
    for source in (value, weight, offset):
        high = source[...].astype(BF16).astype(F32)
        fields += [high, source[...] - high]
    fields += [part * ROWS + channel - ROW_SHIFT, start - part * STRIDE]
    band_ids = lax.broadcasted_iota(jnp.int32, (BANDS, LANES), 0)
    hits = [band_ids == band[i : i + 1, :] for i in range(blocks)]
    ones = [jnp.where(hit, 1.0, 0.0) for hit in hits]
    square = (LANES, 2 * LANES)
    row, column = lax.broadcasted_iota(jnp.int32, square, 0), lane_ids(square)
    before = jnp.where((row < column) | (column >= LANES), 1.0, 0.0).astype(BF16)
    counts = dot(jnp.concatenate(ones, axis=0).astype(BF16), before)
    slot_ids = lax.broadcasted_iota(jnp.int32, (LANES, LANES), 0).astype(F32)
    taken = jnp.zeros((BANDS, LANES), F32)
    total = jnp.zeros((BANDS, FIELDS * LANES), F32)
    for i in range(blocks):
        within = counts[i * BANDS : (i + 1) * BANDS, :]
        rank = jnp.sum(ones[i] * (within[:, :LANES] + taken), axis=0, keepdims=True)
        taken = taken + within[:, LANES:]
        here = slot_ids == rank + (LANES - SLOTS)
        spread = [jnp.where(here, field[i : i + 1, :], 0.0).astype(BF16) for field in fields]
        total = total + dot(ones[i].astype(BF16), jnp.concatenate(spread, axis=0), NT)
    out[...] = total


def pack_obs(band, cell, value, weight, offset):
    return pl.pallas_call(
        pack_kernel,
        out_shape=jax.ShapeDtypeStruct((BANDS, FIELDS * LANES), F32),
        cost_estimate=pl.CostEstimate(flops=200_000_000, bytes_accessed=300_000, transcendentals=0),
        compiler_params=pltpu.CompilerParams(vmem_limit_bytes=8 * MIB),
        name="pack_obs",
    )(band, cell, value, weight, offset)


def regroup_kernel(arrived, obs, out, rows):
    lanes = lane_ids((BANDS, LANES))
    for t in range(TPS):
        rows[pl.ds(t, BANDS, stride=16), :] = arrived[t, 0:BANDS, :].astype(F32)
        rest = pltpu.roll(arrived[t, BANDS : 2 * BANDS, :].astype(F32), LANES - REST_LANE, 1)
        rest = jnp.where(lanes < 16, rest, obs[:, t * LANES : (t + 1) * LANES])
        rows[pl.ds(8 + t, BANDS, stride=16), :] = rest
    out[...] = rows[...].astype(BF16)


def regroup(arrived, obs):
    return pl.pallas_call(
        regroup_kernel,
        out_shape=jax.ShapeDtypeStruct((BANDS * 16, LANES), BF16),
        scratch_shapes=[pltpu.VMEM((BANDS * 16, LANES), F32)],
        cost_estimate=pl.CostEstimate(flops=300_000, bytes_accessed=800_000, transcendentals=0),
        compiler_params=pltpu.CompilerParams(vmem_limit_bytes=8 * MIB),
        name="regroup",
    )(arrived, obs)


def prepare_kernel(own, other, *refs):
    sources, (in_rows, in_columns, out_rows, out_columns, *targets), (arrivals,) = (
        refs[:3],
        refs[3:10],
        refs[10:],
    )
    copies = [
        pltpu.make_async_copy(source, target, arrivals.at[i])
        for i, (source, target) in enumerate(zip(sources, targets))
    ]
    for copy in copies:
        copy.start()
    even = lax.rem(lax.axis_index("band"), 2) == 0
    lanes = lane_ids((8, LANES))
    filler = jnp.zeros((LANES - ROWS, LANES), F32)
    for columns, rows, first in ((in_columns, in_rows, True), (out_columns, out_rows, False)):
        pieces = []
        for t in range(TPS):
            mine = own[t, BANDS:SEND_ROWS, :].astype(F32)
            theirs = other[t, BANDS:SEND_ROWS, :].astype(F32)
            piece = jnp.where(even == first, mine, theirs)
            last = jnp.zeros((8, LANES), F32)
            for start in range(0, REST_LANE, 16):
                part = piece[start // 2 : start // 2 + 8]
                part = pltpu.roll(part, LANES - PIECE_LANE + start, 1)
                last = jnp.where((lanes >= start) & (lanes < start + 16), part, last)
            piece = jnp.concatenate([piece, last, filler], axis=0)
            pieces.append(piece.T[0:REST_LANE])
        upright = jnp.concatenate(pieces, axis=0)
        columns[...] = upright.astype(BF16)
        rows[...] = upright.T[0:80].astype(BF16)
    for copy in copies:
        copy.wait()


def prepare(own, other, tables):
    hidden = TPS * 96
    return pl.pallas_call(
        prepare_kernel,
        out_shape=(
            jax.ShapeDtypeStruct((80, hidden), BF16),
            jax.ShapeDtypeStruct((hidden, LANES), BF16),
            jax.ShapeDtypeStruct((80, hidden), BF16),
            jax.ShapeDtypeStruct((hidden, LANES), BF16),
            *(jax.ShapeDtypeStruct(table.shape, table.dtype) for table in tables),
        ),
        in_specs=[IN_VMEM] * 2 + [IN_HBM] * 3,
        out_specs=[IN_VMEM] * 7,
        scratch_shapes=[pltpu.SemaphoreType.DMA((3,))],
        cost_estimate=pl.CostEstimate(flops=1_000_000, bytes_accessed=5_000_000, transcendentals=0),
        compiler_params=pltpu.CompilerParams(vmem_limit_bytes=8 * MIB),
        name="prepare",
    )(own, other, *in_hbm(*tables))


GELU_SCALE = math.sqrt(2.0 / math.pi)
GELU_CUBE = 0.044715


def lagrange_rows(offset):
    return (
        -offset * (offset - 1.0) * (offset - 2.0) / 6.0,
        (offset + 1.0) * (offset - 1.0) * (offset - 2.0) / 2.0,
        -(offset + 1.0) * offset * (offset - 2.0) / 2.0,
        (offset + 1.0) * offset * (offset - 1.0) / 6.0,
    )


def cycle_kernel(
    channels,
    arrived,
    gains,
    in_rows,
    in_columns,
    out_rows,
    out_columns,
    turns,
    table_high,
    table_low,
    prior_hbm,
    wide_high_hbm,
    wide_low_hbm,
    out,
    prior,
    wide_high,
    wide_low,
    arrivals,
    state,
    slopes,
    obs,
    chosen_all,
    spread_all,
    paired,
):
    orders = turns.shape[1]
    copies = [
        pltpu.make_async_copy(prior_hbm, prior, arrivals.at[0]),
        pltpu.make_async_copy(wide_high_hbm, wide_high, arrivals.at[1]),
        pltpu.make_async_copy(wide_low_hbm, wide_low, arrivals.at[2]),
    ]
    for copy in copies:
        copy.start()
    slices = arrived[...].astype(F32)
    rest = slices[:, 8:16, :]
    half = orders // 2
    paired[0:orders, :] = slices[:, 0:8, :].reshape(orders, LANES)
    paired[orders:, :] = rest.reshape(orders, LANES)
    cos_sin = [paired[pl.ds(p, half, stride=2), :] for p in range(2)]
    cos_sin = jnp.concatenate(cos_sin, axis=0).T
    tail = [paired[pl.ds(orders + p, half, stride=2), :] for p in range(2)]
    tail = jnp.concatenate(tail, axis=0).T
    cos_part = cos_sin[0:ROWS]
    sin_part = jnp.concatenate([cos_sin[ROWS:LANES], tail[0:16]], axis=0)
    pairs = rest.reshape(BANDS // 2, 2, FIELDS, LANES)
    near = pltpu.roll(pairs[:, 0].reshape(BANDS // 2 * FIELDS, LANES), LANES - SLOTS, 1)
    near = near.reshape(BANDS // 2, FIELDS, LANES)
    obs[...] = jnp.where(lane_ids(near.shape) < SLOTS, near, pairs[:, 1])

    turned = []
    for a in range(PAIRS):
        turn_cos, turn_sin = turns[a : a + 1, :], turns[4 + a : 5 + a, :]
        turned_cos = cos_part * turn_cos + sin_part * turn_sin
        turned_sin = sin_part * turn_cos - cos_part * turn_sin
        turned.append(
            jnp.concatenate(
                [turned_cos[:, :half], turned_sin[:, :half], turned_cos[:, half:], turned_sin[:, half:]],
                axis=1,
            )
        )
    turned = split(jnp.concatenate(turned, axis=0))
    sums = []
    for p in range(2):
        span = slice(p * orders, (p + 1) * orders)
        part = (turned[0][:, span], turned[1][:, span])
        sums.append(dot3(part, (table_high[span, :], table_low[span, :])))
    field = jnp.concatenate([sums[0] + sums[1], sums[0] - sums[1]], axis=0)
    copies[0].wait()
    state[...] = prior[...].reshape(BLOCKS * ROWS, WIDTH) + field

    forecast = []
    gain = jnp.concatenate([gains[...]] * GROUP, axis=1)
    groups = [range(a, a + GROUP) for a in range(0, BLOCKS, GROUP)]
    for g, group in enumerate(groups):
        field = [state[a * ROWS : (a + 1) * ROWS, :] for a in group]
        field = jnp.concatenate(field, axis=1)
        mean_sq = jnp.sum(field * field, axis=0, keepdims=True) * (1.0 / channels)
        unit = (field * gain * lax.rsqrt(mean_sq + EPSILON)).astype(BF16)
        pre = dot(in_columns[:, 0:ROWS], unit)
        square = pre * pre
        inner = pre * (GELU_SCALE + (GELU_SCALE * GELU_CUBE) * square)
        gate = 0.5 + 0.5 * jnp.tanh(inner)
        hidden = pre * gate
        slopes[g] = gate + hidden * (1.0 - gate) * (
            2.0 * GELU_SCALE + (6.0 * GELU_SCALE * GELU_CUBE) * square
        )
        ahead = field + dot(out_rows[...], hidden.astype(BF16))[0:ROWS]
        forecast += [ahead[:, i * WIDTH : (i + 1) * WIDTH] for i in range(GROUP)]
    forecast = split(jnp.concatenate(forecast, axis=0).T)
    forecast = jnp.concatenate(forecast, axis=0)

    per_chunk = OBS_CHUNK // LANES
    chunks = obs.shape[0] // per_chunk
    low_ids = lax.broadcasted_iota(jnp.int32, (16, OBS_CHUNK), 0).astype(F32)
    near_ids = lax.broadcasted_iota(jnp.int32, (32, OBS_CHUNK), 0).astype(F32)
    none = jnp.zeros((16, OBS_CHUNK), BF16)

    def fields_of(chunk):
        fields = [obs[chunk * per_chunk + i] for i in range(per_chunk)]
        return jnp.concatenate(fields, axis=1)

    def choose(chunk):
        row = fields_of(chunk)[6:7] + float(ROW_SHIFT)
        row_group = jnp.floor(row * (1.0 / 16.0))
        first = jnp.where(low_ids == row - 16.0 * row_group, 1.0, 0.0).astype(BF16)
        row_group = jnp.broadcast_to(row_group, (16, OBS_CHUNK)).astype(BF16)
        chosen = jnp.concatenate(
            [
                jnp.where(row_group == jnp.array(float(g), BF16), first, none)
                for g in range(BLOCKS * ROWS // 16)
            ],
            axis=0,
        )
        chosen_all[:, chunk * OBS_CHUNK : (chunk + 1) * OBS_CHUNK] = chosen
        return chosen

    def observe(chunk, picked):
        fields = fields_of(chunk)
        columns = slice(chunk * OBS_CHUNK, (chunk + 1) * OBS_CHUNK)
        value = fields[0:1] + fields[1:2]
        weight = fields[2:3] + fields[3:4]
        offset = fields[4:5] + fields[5:6]
        group = jnp.floor(fields[7:8] * (1.0 / 16.0))
        place = near_ids - (fields[7:8] - 16.0 * group)
        group8 = jnp.broadcast_to(group, (8, OBS_CHUNK))
        window = [jnp.zeros((8, OBS_CHUNK), F32)] * 4
        for g in range(WIDTH // 16 - 1):
            mask = group8 == float(g)
            for i in range(4):
                rows = slice(16 * g + 8 * i, 16 * g + 8 * i + 8)
                window[i] = jnp.where(mask, picked[rows] + picked[WIDTH:][rows], window[i])
        window = jnp.concatenate(window, axis=0)
        w_left, w_here, w_right, w_far = lagrange_rows(offset)
        stencil = jnp.where(
            place == 0.0,
            w_left,
            jnp.where(
                place == 1.0,
                w_here,
                jnp.where(place == 2.0, w_right, jnp.where(place == 3.0, w_far, 0.0)),
            ),
        )
        reading = jnp.sum(stencil * window, axis=0, keepdims=True)
        parts = split(stencil * (weight * (reading - value)))
        group = jnp.broadcast_to(group, (16, OBS_CHUNK)).astype(BF16)
        masks = [group == jnp.array(float(g), BF16) for g in range(WIDTH // 16 - 1)]
        for i, part in enumerate(parts):
            pieces = []
            for g in range(WIDTH // 16):
                piece = none
                if g > 0:
                    piece = jnp.where(masks[g - 1], part[16:32], piece)
                if g < WIDTH // 16 - 1:
                    piece = jnp.where(masks[g], part[0:16], piece)
                pieces.append(piece)
            spread_all[i * WIDTH : (i + 1) * WIDTH, columns] = jnp.concatenate(pieces, axis=0)

    chosen = choose(0)
    picked = None
    for chunk in range(chunks):
        latest = dot(forecast, chosen)
        if chunk + 1 < chunks:
            chosen = choose(chunk + 1)
        if chunk > 0:
            observe(chunk - 1, picked)
        picked = latest
    observe(chunks - 1, picked)
    forcing = dot(spread_all[...], chosen_all[...], NT)
    forcing = (forcing[0:WIDTH] + forcing[WIDTH:]).T

    lanes = lane_ids((BLOCKS * ROWS, WIDTH))
    halo = pltpu.roll(forcing, WIDTH - STRIDE, 1)
    halo = jnp.concatenate([halo[(BLOCKS - 1) * ROWS :], halo[: (BLOCKS - 1) * ROWS]], axis=0)
    forcing = jnp.where(lanes < STRIDE, forcing, 0.0) + jnp.where(lanes < 3, halo, 0.0)
    costate = []
    for g, group in enumerate(groups):
        force = [forcing[a * ROWS : (a + 1) * ROWS] for a in group]
        force = jnp.concatenate(force, axis=1)
        grad_hidden = dot(out_columns[:, 0:ROWS], force.astype(BF16))
        grad_pre = (grad_hidden * slopes[g]).astype(BF16)
        grad_unit = dot(in_rows[...], grad_pre)[0:ROWS]
        field = [state[a * ROWS : (a + 1) * ROWS, :] for a in group]
        field = jnp.concatenate(field, axis=1)
        mean_sq = jnp.sum(field * field, axis=0, keepdims=True) * (1.0 / channels)
        inverse = lax.rsqrt(mean_sq + EPSILON)
        scaled = grad_unit * gain
        along = jnp.sum(scaled * field, axis=0, keepdims=True) * (1.0 / channels)
        total = force + scaled * inverse - field * (along * inverse * inverse * inverse)
        costate += [total[:, i * WIDTH : (i + 1) * WIDTH] for i in range(GROUP)]
    near = jnp.concatenate(costate[:PAIRS], axis=0)
    far = jnp.concatenate(costate[PAIRS:], axis=0)
    for copy in copies[1:]:
        copy.wait()
    pad = jnp.zeros((LANES - ROWS, half), F32)
    lanes = lane_ids((half, LANES))
    for p, both in enumerate((near + far, near - far)):
        span = slice(p * orders, (p + 1) * orders)
        blocks = dot3(split(both), (wide_high[:, span], wide_low[:, span]))
        grads = [jnp.zeros((ROWS, half), F32)] * 2
        for a in range(PAIRS):
            turn_cos = turns[a : a + 1, p * half : (p + 1) * half]
            turn_sin = turns[4 + a : 5 + a, p * half : (p + 1) * half]
            block = blocks[a * ROWS : (a + 1) * ROWS]
            block_cos, block_sin = block[:, :half], block[:, half:]
            grads[0] = grads[0] + turn_cos * block_cos - turn_sin * block_sin
            grads[1] = grads[1] + turn_sin * block_cos + turn_cos * block_sin
        for r in range(2):
            upright = jnp.concatenate([grads[r], pad], axis=0).T
            high = upright.astype(BF16).astype(F32)
            low = pltpu.roll(upright - high, channels, 1)
            place = pl.ds(2 * p + r, half, stride=4)
            paired[place, :] = jnp.where(lanes < channels, high, low)
    out[...] = paired[...].astype(BF16)


def run_cycle(channels, arrived, prior, gains, prepared, wide):
    orders = prepared[4].shape[1]
    hidden = prepared[1].shape[0]
    return pl.pallas_call(
        lambda *refs: cycle_kernel(channels, *refs),
        out_shape=jax.ShapeDtypeStruct((2 * orders, LANES), BF16),
        in_specs=[IN_VMEM] * 9 + [IN_HBM] * 3,
        out_specs=IN_VMEM,
        scratch_shapes=[
            pltpu.VMEM(prior.shape, F32),
            *(pltpu.VMEM(part.shape, BF16) for part in wide),
            pltpu.SemaphoreType.DMA((3,)),
            pltpu.VMEM((BLOCKS * ROWS, WIDTH), F32),
            pltpu.VMEM((BLOCKS // GROUP, hidden, GROUP * WIDTH), F32),
            pltpu.VMEM((BANDS // 2, FIELDS, LANES), F32),
            pltpu.VMEM((BLOCKS * ROWS, BANDS * SLOTS), BF16),
            pltpu.VMEM((2 * WIDTH, BANDS * SLOTS), BF16),
            pltpu.VMEM((2 * orders, LANES), F32),
        ],
        compiler_params=pltpu.CompilerParams(vmem_limit_bytes=36 * MIB),
        cost_estimate=pl.CostEstimate(
            flops=8_000_000_000, bytes_accessed=4_000_000, transcendentals=1_200_000
        ),
        name="cycle",
    )(arrived, gains, *prepared, *in_hbm(prior, *wide))


def analysis_kernel(arrived, control, sigma, table_high, table_low, out, rows):
    parity = lax.rem(lax.axis_index("tp"), 2)
    channels = sigma.shape[0]
    orders = arrived.shape[0] // 2
    rows[...] = arrived[...].astype(F32)
    lanes = lane_ids((orders, LANES))
    grads = []
    for r in range(2):
        both = rows[pl.ds(r, orders, stride=2), :]
        low = pltpu.roll(both, LANES - channels, 1)
        grad = jnp.where(lanes < channels, both, 0.0)
        grad = grad + jnp.where(lanes < LANES - channels, low, 0.0)
        grads.append(grad.T[0:ROWS])
    grads = split(jnp.concatenate(grads, axis=0))
    projected = dot3(grads, (table_high[parity], table_low[parity]))
    for r in range(2):
        step = projected[r * ROWS : r * ROWS + channels]
        out[:, r, 0, :] = control[:, r, 0, :] + sigma[:, 0, :] * step


def analysis(arrived, control, sigma, table):
    return pl.pallas_call(
        analysis_kernel,
        out_shape=jax.ShapeDtypeStruct(control.shape, F32),
        scratch_shapes=[pltpu.VMEM(arrived.shape, F32)],
        cost_estimate=pl.CostEstimate(flops=400_000_000, bytes_accessed=2_000_000, transcendentals=0),
        compiler_params=pltpu.CompilerParams(vmem_limit_bytes=12 * MIB),
        name="analysis",
    )(arrived, control, sigma, *table)


def shards(
    control,
    spec_sigma,
    prior_mean_field,
    magnitude_factor,
    w_in,
    w_out,
    obs_band,
    obs_cell,
    obs_value,
    obs_weight,
    obs_offset,
):
    channels, _, _, wave_count = control.shape
    lat_count = BANDS * TPS
    lon_count = prior_mean_field.shape[2]
    legendre = legendre_np(wave_count, lat_count)
    zonal = zonal_np(lat_count, lon_count)
    turns = turn_np(lat_count, lon_count)
    send = synthesis(control, spec_sigma, w_in, w_out.T, legendre)
    got = lax.all_to_all(send, "tp", split_axis=0, concat_axis=0, tiled=True)
    obs = pack_obs(
        *(
            field.reshape(-1, LANES)
            for field in (obs_band, obs_cell, obs_value, obs_weight, obs_offset)
        )
    )
    send = regroup(got, obs).reshape(BANDS, 16, LANES)
    arrived = lax.all_to_all(send, "band", split_axis=0, concat_axis=0, tiled=True)
    other = lax.ppermute(got, "band", [(i, i ^ 1) for i in range(BANDS)])
    prepared = prepare(got, other, (turns, *zonal[:2]))
    prior = jnp.pad(prior_mean_field[:, 0, :], ((0, ROWS - channels), (0, 0)))
    prior = jnp.concatenate([prior, prior[:, : WIDTH - STRIDE]], axis=1)
    prior = jnp.stack([prior[:, a * STRIDE : a * STRIDE + WIDTH] for a in range(BLOCKS)])
    gains = jnp.broadcast_to(
        jnp.pad(magnitude_factor, (0, ROWS - channels))[:, None], (ROWS, WIDTH)
    )
    modes = run_cycle(channels, arrived, prior, gains, prepared, zonal[2:])
    modes = lax.all_to_all(
        modes.reshape(lat_count, 2, LANES),
        ("band", "tp"),
        split_axis=0,
        concat_axis=0,
        tiled=True,
    )
    modes = modes.reshape(2 * lat_count, LANES)
    return analysis(modes, control, spec_sigma, legendre)


def solution(mesh):
    placed = (
        P(None, None, ("band", "tp"), None),
        P(None, ("band", "tp"), None),
        P(None, ("band", "tp"), None),
        P(),
        P(None, "tp"),
        P("tp", None),
        P("band", "tp", None, None),
        P("band", "tp", None),
        P("band", "tp", None),
        P("band", "tp", None),
        P("band", "tp", None),
    )
    return jax.shard_map(
        shards,
        mesh=mesh,
        in_specs=placed,
        out_specs=P(None, None, ("band", "tp"), None),
        check_vma=False,
    )
```
